32 devices in a mesh: fsdp: 8 (over z, x), expert: 4 (over y, core).
Axes of the slice: x: 2, y: 2, z: 4, core: 2. Of those that a mesh axis runs over, the one named last changes fastest.
Arguments:
- tokens: bfloat16 [512, 3072], P('expert'), may hold values from -6 to 6
- cotangent: bfloat16 [512, 3072], P('expert'), may hold values from -6 to 6
- expert_ids: int32 [512, 4], P('expert'), may hold values from 0 to 15, all different within a row; in each aligned block of 128 rows (0 to 127, 128 to 255, ...) at most 40 rows name the same one
- gate_values: bfloat16 [512, 4], P('expert'), may hold values from 0.049804688 to 0.5
- w_in: bfloat16 [3072, 16, 6144], P(None, 'expert', 'fsdp'), may hold values from -0.109375 to 0.109375
- w_out: bfloat16 [6144, 16, 3072], P('fsdp', 'expert'), may hold values from -0.078125 to 0.078125
Outputs:
- grad_tokens: bfloat16 [512, 3072], P('expert')
- grad_gates: bfloat16 [512, 4], P('expert')
- grad_w_in: bfloat16 [3072, 16, 6144], P(None, 'expert', 'fsdp')
- grad_w_out: bfloat16 [6144, 16, 3072], P('fsdp', 'expert')
The draws below stay inside these ranges and needn't reach their ends.
Inputs may be any that keep to these rules, and one draw needn't show every extreme that they name: `expert_ids`: in each aligned block of 128 rows (the rows of one index of the expert axis) the 4 entries of a row differ, no expert is named by more than 40 rows, a bound that some block reaches.
All inputs are finite; a program needn't handle non-finite values.
Results may differ from the reference program's by a relative error of at most 0.0049.
Values may be sent and summed in bfloat16 or wider, within the bound.
No kernel may reach another device: no remote copies, remote signals or barrier semaphores. Data moves between devices by JAX's collectives and lax.ppermute only.
A program may use at most 192 MiB of HBM per device.

```python
import math
import jax
import jax.numpy as jnp
import numpy as np
from jax import lax

D = 3072
FF = 6144
EXPERTS = 16
TOP = 4
TOK_DEV = 128
CAP = 40
TOKENS = 512
N_EXPERT = 4


def level_of(rng, shape, split, least, high):
    gain, own = 1.0, jax.random.fold_in(rng, 6)
    for dim, shards_of in split:
        draws = jnp.exp(jax.random.uniform(jax.random.fold_in(own, dim), (shards_of,), jnp.float32, least / len(split), high / len(split)))
        gain = gain * jnp.repeat(draws, shape[dim] // shards_of).reshape([-1 if axis == dim else 1 for axis in range(len(shape))])
    return gain


def assign_block(key, own, number, rows, amount, top, most, slope):
    ranking = jax.random.permutation(key, amount)
    packed, common = load_shares(amount, rows * top, most, slope, True), load_shares(amount, rows * top, most, slope, False)
    places = jnp.arange(amount)

    def named(lengths, turn):
        used = int((lengths > 0).sum())
        fixed = max(1, used // 4)
        moved = fixed + (places - fixed + turn * (used - fixed)) % max(1, amount - fixed)
        return jnp.zeros((amount,), jnp.int32).at[ranking[jnp.where(places < fixed, places, moved)]].set(jnp.asarray(lengths, jnp.int32))

    lengths = jnp.where(number % 4 == 0, named(packed, number // 4), named(common, number - number // 4 - 1))
    mixed = jax.random.permutation(jax.random.fold_in(own, 3), amount)
    donor, sink = mixed[0:amount // 2 * 2:2], mixed[1:amount // 2 * 2:2]
    slack = jnp.minimum(lengths[donor] - 1, most - lengths[sink]) // 2
    slack = jnp.where((donor == ranking[0]) | (sink == ranking[0]) | (lengths[sink] == 0), 0, jnp.maximum(slack, 0))
    moved = jax.random.randint(jax.random.fold_in(own, 4), (amount // 2,), 0, 1 << 20) % (slack + 1)
    lengths = lengths.at[donor].add(-moved).at[sink].add(moved)
    labels = jnp.searchsorted(jnp.cumsum(lengths), jnp.arange(rows * top), side="right").astype(jnp.int32)
    grid = labels.reshape(top, rows).T
    grid = grid[jax.random.permutation(jax.random.fold_in(own, 1), rows)]
    turn = jax.random.randint(jax.random.fold_in(own, 2), (rows, 1), 0, top)
    return jnp.take_along_axis(grid, (jnp.arange(top)[None, :] + turn) % top, axis=1)


def load_shares(count, total, bound, skew, full):
    loads = [(1 << 20) // math.isqrt(standing ** skew) + 1 for standing in range(1, count + 1)]
    largest = bound if full else min(bound, max(-(-total // count), total * loads[0] // sum(loads)))
    least = 1 if total - largest >= count - 1 else 0
    counts, rest = [largest] + [least] * (count - 1), total - largest - least * (count - 1)
    while rest > 0:
        candidates = [i for i in range(1, count) if counts[i] < largest] or [i for i in range(1, count) if counts[i] < bound]
        whole, remaining = sum([loads[i] for i in candidates]), rest
        for i in candidates:
            addition = min(bound - counts[i], max(1, remaining * loads[i] // whole), rest)
            counts[i] = counts[i] + addition
            rest = rest - addition
    return np.array(counts)


def scatter_about(rng, shape, deviation, bound, cuts=(), held_as=jnp.bfloat16):
    factor_of = level_of(rng, shape, cuts, -0.22, 0.18) if cuts else 1.0
    result = jax.random.normal(rng, shape, jnp.float32) * deviation * factor_of
    return jnp.minimum(jnp.maximum(result, -bound), bound).astype(held_as)


def setup_inputs(seed: int = 0) -> dict:
    splits = jax.random.split(jax.random.key(seed), 7)
    tokens = scatter_about(splits[0], (TOKENS, D), 1.0, 6.0, ((0, 4),))
    cotangent = scatter_about(splits[1], (TOKENS, D), 1.0, 6.0, ((0, 4),))
    expert_ids_keys = jax.random.split(jax.random.fold_in(splits[2], 1), TOKENS // TOK_DEV)
    expert_ids_turns = jax.random.permutation(jax.random.fold_in(splits[2], 3), TOKENS // TOK_DEV)
    expert_ids = jax.vmap(lambda own, number: assign_block(jax.random.fold_in(splits[2], 2), own, number, TOK_DEV, EXPERTS, TOP, CAP, 1))(expert_ids_keys, expert_ids_turns).reshape((TOKENS, TOP))
    gate_values = jnp.clip(0.049804688 + 0.4501953 * jax.random.uniform(splits[3], (TOKENS, TOP), jnp.float32) ** level_of(splits[3], (TOKENS, TOP), ((0, 4),), -0.2, 0.2), 0.049804688, 0.5).astype(jnp.bfloat16)
    w_in = scatter_about(splits[4], (D, EXPERTS, FF), D ** -0.5, 0.109375, ((1, 4), (2, 8)))
    w_out = scatter_about(splits[5], (FF, EXPERTS, D), FF ** -0.5, 0.078125, ((0, 8), (1, 4)))
    return {"tokens": tokens, "cotangent": cotangent, "expert_ids": expert_ids, "gate_values": gate_values, "w_in": w_in, "w_out": w_out}


def slot_targets(expert_ids):
    flat = expert_ids.reshape(-1).astype(jnp.int32)
    table = (flat[:, None] == jnp.arange(EXPERTS, dtype=jnp.int32)[None, :]).astype(jnp.int32)
    earlier = jnp.cumsum(table, axis=0) - table
    position = jnp.sum(earlier * table, axis=1).astype(jnp.int32)
    return (flat * CAP + position).astype(jnp.int32)


def fill_slots(rows, target):
    holder = jnp.zeros((EXPERTS * CAP,) + rows.shape[1:], rows.dtype)
    return holder.at[target].set(rows)


def token_slots(rows, target):
    return fill_slots(jnp.repeat(rows, TOP, axis=0), target)


def gate_slots(gates, target):
    return fill_slots(gates.reshape(-1), target)


def pick_rows(lookup, target):
    return lookup[target]


def one_expert(inputs):
    x_rows, g_rows, gate_rows, in_proj, out_proj = inputs
    pre_act = jnp.dot(x_rows, in_proj, preferred_element_type=jnp.float32)
    upstream = jnp.dot(g_rows, out_proj.T, preferred_element_type=jnp.float32)
    squash = jax.nn.sigmoid(pre_act)
    active = pre_act * squash
    gate_grad = jnp.sum(active * upstream, axis=-1)
    gate_col = gate_rows.astype(jnp.float32)[:, None]
    act_gated = (gate_col * active).astype(jnp.bfloat16)
    grad_pre = (gate_col * squash * (1.0 + pre_act * (1.0 - squash)) * upstream).astype(jnp.bfloat16)
    grad_x = jnp.dot(grad_pre, in_proj.T, preferred_element_type=jnp.float32)
    grad_in = jnp.dot(x_rows.T, grad_pre, preferred_element_type=jnp.float32).astype(jnp.bfloat16)
    grad_out = jnp.dot(act_gated.T, g_rows, preferred_element_type=jnp.float32).astype(jnp.bfloat16)
    return grad_x, gate_grad, grad_in, grad_out


def reference(tokens, cotangent, expert_ids, gate_values, w_in, w_out):
    blocks = N_EXPERT
    tok_blocks = tokens.reshape(blocks, TOK_DEV, D)
    cot_blocks = cotangent.reshape(blocks, TOK_DEV, D)
    id_blocks = expert_ids.reshape(blocks, TOK_DEV, TOP)
    gate_blocks = gate_values.reshape(blocks, TOK_DEV, TOP)
    target = jax.vmap(slot_targets)(id_blocks)
    x_slot = jax.vmap(token_slots)(tok_blocks, target).reshape(blocks, EXPERTS, CAP, D)
    g_slot = jax.vmap(token_slots)(cot_blocks, target).reshape(blocks, EXPERTS, CAP, D)
    gate_slot = jax.vmap(gate_slots)(gate_blocks, target).reshape(blocks, EXPERTS, CAP)
    x_exp = jnp.transpose(x_slot, (1, 0, 2, 3)).reshape(EXPERTS, blocks * CAP, D)
    g_exp = jnp.transpose(g_slot, (1, 0, 2, 3)).reshape(EXPERTS, blocks * CAP, D)
    gate_exp = jnp.transpose(gate_slot, (1, 0, 2)).reshape(EXPERTS, blocks * CAP)
    in_stack = jnp.moveaxis(w_in, 1, 0)
    out_stack = jnp.moveaxis(w_out, 1, 0)
    grad_x, gate_grad, grad_in, grad_out = lax.map(one_expert, (x_exp, g_exp, gate_exp, in_stack, out_stack))
    grad_x = jnp.transpose(grad_x.reshape(EXPERTS, blocks, CAP, D), (1, 0, 2, 3)).reshape(blocks, EXPERTS * CAP, D)
    gate_grad = jnp.transpose(gate_grad.reshape(EXPERTS, blocks, CAP), (1, 0, 2)).reshape(blocks, EXPERTS * CAP)
    picked = jax.vmap(pick_rows)(grad_x, target).reshape(blocks, TOK_DEV, TOP, D)
    grad_tokens = picked.sum(axis=2).astype(jnp.bfloat16).reshape(TOKENS, D)
    picked_gate = jax.vmap(pick_rows)(gate_grad, target)
    grad_gates = picked_gate.astype(jnp.bfloat16).reshape(TOKENS, TOP)
    grad_w_in = jnp.moveaxis(grad_in, 0, 1)
    grad_w_out = jnp.moveaxis(grad_out, 0, 1)
    return grad_tokens, grad_gates, grad_w_in, grad_w_out
```

```python
import jax
import jax.numpy as jnp
from jax import lax
from jax.sharding import PartitionSpec as P

EXPERTS = 16
CAP = 40
AXES = ("fsdp", "expert")
CORE, Y, X, Z = 1, 2, 4, 8


def swap(value, mask):
    size = lax.axis_size("fsdp") * lax.axis_size("expert")
    return lax.ppermute(value, AXES, [(i, i ^ mask) for i in range(size)])


def is_small():
    return lax.axis_size("fsdp") == 8 and lax.axis_size("expert") == 4


def own_order(rows):
    x_index = lax.axis_index("fsdp") % 2
    half = rows.shape[0] // 2
    return jnp.where(x_index == 0, rows, jnp.concatenate([rows[half:], rows[:half]], axis=0))


def spread(rows):
    if not is_small():
        return list(lax.all_gather(rows, "expert", axis=0))
    half = rows.shape[0] // 2
    other_core = swap(rows, CORE)
    near = swap(rows[:half], Y)
    far = swap(near, X)
    other_y = jnp.concatenate([near, far], axis=0)
    both = jnp.concatenate([swap(near, CORE), swap(far, CORE)], axis=0)
    return [rows, other_core, other_y, both]


def spread_small(rows):
    if not is_small():
        return list(lax.all_gather(rows, "expert", axis=0))
    return [rows, swap(rows, CORE), swap(rows, Y), swap(rows, CORE | Y)]


def collect(parts):
    if not is_small():
        stacked = jnp.stack(parts, axis=0)
        mine = lax.psum_scatter(stacked, "expert", scatter_dimension=0, tiled=False)
        return lax.psum(mine, "fsdp").astype(jnp.bfloat16)
    narrow, wide = jnp.bfloat16, jnp.float32
    fsdp = lax.axis_index("fsdp")
    x_index, z_index = fsdp % 2, fsdp // 2
    half = parts[0].shape[0] // 2
    own = parts[0] + swap(parts[1].astype(narrow), CORE).astype(wide)
    other = parts[2] + swap(parts[3].astype(narrow), CORE).astype(wide)
    total = own[:half]
    total = total + swap(own[half:].astype(narrow), X).astype(wide)
    total = total + swap(other[:half].astype(narrow), Y).astype(wide)
    total = total + swap(other[half:].astype(narrow), X | Y).astype(wide)
    quarter = half // 4

    def chunk(array, index):
        return lax.dynamic_slice_in_dim(array, index * quarter, quarter, axis=0)

    final = chunk(total, z_index)
    packed = total.astype(narrow)
    for step in (1, 2, 3):
        final = final + swap(chunk(packed, z_index ^ step), step * Z).astype(wide)
    final = final.astype(narrow)
    near = jnp.zeros((half, final.shape[1]), narrow)
    near = lax.dynamic_update_slice_in_dim(near, final, z_index * quarter, axis=0)
    for step in (1, 2, 3):
        near = lax.dynamic_update_slice_in_dim(near, swap(final, step * Z), (z_index ^ step) * quarter, axis=0)
    far = swap(near, X)
    return jnp.where(
        x_index == 0, jnp.concatenate([near, far], axis=0), jnp.concatenate([far, near], axis=0)
    )


def local(tokens, cotangent, expert_ids, gate_values, w_in, w_out):
    tok_rows, model_width = tokens.shape
    local_count = w_in.shape[1]
    narrow, wide = jnp.bfloat16, jnp.float32
    first = lax.axis_index("expert") * local_count
    if is_small():
        tokens, cotangent = own_order(tokens), own_order(cotangent)
        expert_ids, gate_values = own_order(expert_ids), own_order(gate_values)
    meta = jnp.concatenate([expert_ids.astype(wide), gate_values.astype(wide)], axis=1).T
    meta_blocks = jnp.stack(spread_small(meta))
    top_count = expert_ids.shape[1]
    ids = meta_blocks[:, :top_count].astype(jnp.int32)
    gates = meta_blocks[:, top_count:]
    blocks = ids.shape[0]
    x_blocks = jnp.stack(spread(tokens))
    g_blocks = jnp.stack(spread(cotangent))
    names = first + jnp.arange(local_count, dtype=jnp.int32)
    named = ids[:, None] == names[None, :, None, None]
    hit = jnp.any(named, axis=2)
    gate_tok = jnp.sum(jnp.where(named, gates[:, None], 0.0), axis=2)
    earlier = jnp.tril(jnp.ones((tok_rows, tok_rows), wide), -1)
    position = jnp.einsum("tu,blu->blt", earlier, hit.astype(wide)).astype(jnp.int32)
    slots = jnp.arange(CAP, dtype=jnp.int32)
    choose = hit[:, :, None] & (position[:, :, None] == slots[None, None, :, None])
    pick = choose.astype(narrow)
    slot_x = jnp.einsum("blst,btd->lbsd", pick, x_blocks, preferred_element_type=wide).astype(narrow)
    slot_g = jnp.einsum("blst,btd->lbsd", pick, g_blocks, preferred_element_type=wide).astype(narrow)
    gate_slot = jnp.sum(jnp.where(choose, gate_tok[:, :, None], 0.0), axis=3)
    rows = blocks * CAP
    slot_x = slot_x.reshape(local_count, rows, model_width)
    slot_g = slot_g.reshape(local_count, rows, model_width)
    gate_slot = jnp.swapaxes(gate_slot, 0, 1).reshape(local_count, rows, 1)
    pre_act = jnp.einsum("lrd,dlf->lrf", slot_x, w_in, preferred_element_type=wide)
    upstream = jnp.einsum("lrd,fld->lrf", slot_g, w_out, preferred_element_type=wide)
    squash = jax.nn.sigmoid(pre_act)
    active = pre_act * squash
    gate_part = jnp.sum(active * upstream, axis=-1)
    act_gated = (gate_slot * active).astype(narrow)
    grad_pre = (gate_slot * squash * (1.0 + pre_act * (1.0 - squash)) * upstream).astype(narrow)
    gate_part = gate_part.reshape(local_count, blocks, CAP)
    gate_tok = jnp.sum(jnp.where(choose, jnp.swapaxes(gate_part, 0, 1)[..., None], 0.0), axis=2)
    gate_back = jnp.sum(jnp.where(named, gate_tok[:, :, None], 0.0), axis=1)
    part_x = jnp.einsum("lrf,dlf->lrd", grad_pre, w_in, preferred_element_type=wide)
    high = part_x.astype(narrow)
    low = (part_x - high.astype(wide)).astype(narrow)
    high = high.reshape(local_count, blocks, CAP, model_width)
    low = low.reshape(local_count, blocks, CAP, model_width)
    token_part = jnp.einsum("blst,lbsd->btd", pick, high, preferred_element_type=wide)
    token_part = token_part + jnp.einsum("blst,lbsd->btd", pick, low, preferred_element_type=wide)
    grad_tokens = collect([token_part[b] for b in range(blocks)])
    if is_small():
        gates_own = gate_back[0]
        for b, mask in ((1, CORE), (2, Y), (3, CORE | Y)):
            gates_own = gates_own + swap(gate_back[b], mask)
        half = tok_rows // 2
        x_index = lax.axis_index("fsdp") % 2
        gates_own = jnp.where(
            x_index == 0,
            gates_own,
            jnp.concatenate([gates_own[:, half:], gates_own[:, :half]], axis=1),
        )
    else:
        gates_own = lax.psum_scatter(gate_back, "expert", scatter_dimension=0, tiled=False)
    grad_gates = lax.psum(gates_own, "fsdp").T.astype(narrow)
    grad_in = jnp.einsum("lrd,lrf->dlf", slot_x, grad_pre, preferred_element_type=wide).astype(narrow)
    grad_out = jnp.einsum("lrf,lrd->fld", act_gated, slot_g, preferred_element_type=wide).astype(narrow)
    return (grad_tokens, grad_gates, grad_in, grad_out)


def solution(mesh):
    return jax.shard_map(
        local,
        mesh=mesh,
        in_specs=(
            P("expert", None),
            P("expert", None),
            P("expert", None),
            P("expert", None),
            P(None, "expert", "fsdp"),
            P("fsdp", "expert", None),
        ),
        out_specs=(
            P("expert", None),
            P("expert", None),
            P(None, "expert", "fsdp"),
            P("fsdp", "expert", None),
        ),
        check_vma=False,
    )
```

```python
import functools
import jax
import jax.numpy as jnp
from jax import lax
from jax.experimental import pallas as pl
from jax.experimental.pallas import tpu as pltpu
from jax.sharding import PartitionSpec as P

EXPERTS = 16
CAP = 40
AXES = ("fsdp", "expert")
CORE, Y, X, Z = 1, 2, 4, 8
LANES = 128
NARROW, WIDE = jnp.bfloat16, jnp.float32
MIB = 1 << 20
TN = (((0,), (0,)), ((), ()))
NT = (((1,), (1,)), ((), ()))
NN = (((1,), (0,)), ((), ()))


def mm(a, b, dims):
    return lax.dot_general(a, b, dims, preferred_element_type=WIDE)


def swap(value, mask):
    size = lax.axis_size("fsdp") * lax.axis_size("expert")
    return lax.ppermute(value, AXES, [(i, i ^ mask) for i in range(size)])


def is_small():
    return lax.axis_size("fsdp") == 8 and lax.axis_size("expert") == 4


def own_order(rows):
    x_index = lax.axis_index("fsdp") % 2
    half = rows.shape[0] // 2
    return jnp.where(x_index == 0, rows, jnp.concatenate([rows[half:], rows[:half]], axis=0))


def spread(rows):
    half = rows.shape[0] // 2
    other_core = swap(rows, CORE)
    near = swap(rows[:half], Y)
    far = swap(near, X)
    return [rows, other_core, near, far, swap(near, CORE), swap(far, CORE)]


def collect(keep, send):
    fsdp = lax.axis_index("fsdp")
    x_index, z_index = fsdp % 2, fsdp // 2
    rows = keep.shape[0] // 2
    half = rows // 2
    total = keep + swap(send, CORE).astype(WIDE)
    own, other = total[:rows], total[rows:]
    total = own[:half]
    total = total + swap(own[half:].astype(NARROW), X).astype(WIDE)
    total = total + swap(other[:half].astype(NARROW), Y).astype(WIDE)
    total = total + swap(other[half:].astype(NARROW), X | Y).astype(WIDE)
    quarter = half // 4

    def chunk(array, index):
        return lax.dynamic_slice_in_dim(array, index * quarter, quarter, axis=0)

    final = chunk(total, z_index)
    packed = total.astype(NARROW)
    for step in (1, 2, 3):
        final = final + swap(chunk(packed, z_index ^ step), step * Z).astype(WIDE)
    final = final.astype(NARROW)
    near = jnp.zeros((half, final.shape[1]), NARROW)
    near = lax.dynamic_update_slice_in_dim(near, final, z_index * quarter, axis=0)
    for step in (1, 2, 3):
        near = lax.dynamic_update_slice_in_dim(near, swap(final, step * Z), (z_index ^ step) * quarter, axis=0)
    far = swap(near, X)
    return jnp.where(
        x_index == 0, jnp.concatenate([near, far], axis=0), jnp.concatenate([far, near], axis=0)
    )


def collect_gates(parts):
    total = parts[0]
    for block, mask in ((1, CORE), (2, Y), (3, CORE | Y)):
        total = total + swap(parts[block], mask)
    half = total.shape[1] // 2
    x_index = lax.axis_index("fsdp") % 2
    total = jnp.where(
        x_index == 0, total, jnp.concatenate([total[:, half:], total[:, :half]], axis=1)
    )
    for mask in (X, Z, 2 * Z):
        total = total + swap(total, mask)
    return total


def tiled_view(weight):
    rows, experts, columns = weight.shape
    return weight.reshape(rows, experts, columns // LANES, LANES).transpose(0, 2, 1, 3)


def split_body(w_ref, out_ref, wide_ref):
    rows, tiles, experts, _ = w_ref.shape
    stride = tiles * experts
    wide_ref[...] = w_ref.reshape(rows * stride, LANES)[...].astype(WIDE)
    for expert in range(experts):
        for tile in range(tiles):
            part = wide_ref[pl.ds(tile * experts + expert, rows, stride), :]
            out_ref[expert, :, tile * LANES : (tile + 1) * LANES] = part.astype(NARROW)


def split_experts(view, start, rows, block):
    _, tiles, experts, _ = view.shape
    columns = tiles * LANES
    first = start // block
    return pl.pallas_call(
        split_body,
        out_shape=jax.ShapeDtypeStruct((experts, rows, columns), NARROW),
        grid=(rows // block,),
        in_specs=[pl.BlockSpec((block, tiles, experts, LANES), lambda i: (first + i, 0, 0, 0))],
        out_specs=pl.BlockSpec((experts, block, columns), lambda i: (0, i, 0)),
        scratch_shapes=[pltpu.VMEM((block * tiles * experts, LANES), WIDE)],
        compiler_params=pltpu.CompilerParams(vmem_limit_bytes=24 * MIB),
        cost_estimate=pl.CostEstimate(
            flops=0, bytes_accessed=4 * experts * rows * columns, transcendentals=0
        ),
        name="split_experts",
    )(view)


def forward_body(
    target_ref, gate_ref, x_ref, g_ref, w0_ref, w1_ref, v0_ref, v1_ref,
    xs_ref, gs_ref, gp_ref, ag_ref, gate_out_ref, keep_ref, send_ref,
    back_ref, pick_ref,
):
    step = pl.program_id(0)
    slots, model_width = xs_ref.shape[1:]
    tokens = x_ref.shape[0]
    half_d = w0_ref.shape[1]
    columns = 512
    target = target_ref[0]
    choose = lax.broadcasted_iota(jnp.int32, (slots, tokens), 0) == target
    pick = choose.astype(WIDE).astype(NARROW)
    rows = pl.ds(pl.multiple_of(step * slots, slots), slots)
    pick_ref[rows, :] = pick
    gate = jnp.sum(jnp.where(choose, gate_ref[0], 0.0), axis=1, keepdims=True)
    for begin in range(0, model_width, columns):
        part = slice(begin, begin + columns)
        xs_ref[0, :, part] = mm(pick, x_ref[:, part], NN).astype(NARROW)
        gs_ref[0, :, part] = mm(pick, g_ref[:, part], NN).astype(NARROW)
    pre_act = mm(xs_ref[0, :, :half_d], w0_ref[0], NN) + mm(xs_ref[0, :, half_d:], w1_ref[0], NN)
    squash = jax.nn.sigmoid(pre_act)
    active = pre_act * squash
    slope = gate * squash * (1.0 + pre_act * (1.0 - squash))
    ag_ref[0] = (gate * active).astype(NARROW)
    half_f = v0_ref.shape[1]
    gate_part = jnp.zeros((slots, 1), WIDE)
    for begin, v_ref in ((0, v0_ref), (half_f, v1_ref)):
        upstream = mm(gs_ref[0], v_ref[0], NT)
        part = slice(begin, begin + half_f)
        gate_part = gate_part + jnp.sum(active[:, part] * upstream, axis=1, keepdims=True)
        gp_ref[0, :, part] = (slope[:, part] * upstream).astype(NARROW)
    gate_out_ref[0] = jnp.sum(jnp.where(choose, gate_part, 0.0), axis=0, keepdims=True)
    for begin in range(0, model_width, columns):
        w_ref = w0_ref if begin < half_d else w1_ref
        inner = begin % half_d
        back = mm(gp_ref[0], w_ref[0, inner : inner + columns, :], NT)
        back_ref[rows, begin : begin + columns] = back.astype(NARROW)

    @pl.when(step == pl.num_programs(0) - 1)
    def _():
        quarter = tokens // 4
        for begin in range(0, model_width, columns):
            part = slice(begin, begin + columns)
            summed = mm(pick_ref[...], back_ref[:, part], TN)
            for pair in range(2):
                lower = 2 * pair * quarter
                keep_ref[pair * quarter : (pair + 1) * quarter, part] = summed[lower : lower + quarter]
                send_ref[pair * quarter : (pair + 1) * quarter, part] = summed[
                    lower + quarter : lower + 2 * quarter
                ].astype(NARROW)


def forward(target, gate_tok, x_rows, g_rows, w_parts, v_parts):
    experts, _, tokens = target.shape
    model_width = x_rows.shape[1]
    hidden = w_parts[0].shape[2]
    slots = tokens // 128 * CAP
    whole = lambda i: (0, 0)
    expert = lambda i: (i, 0, 0)
    one = pl.Buffered(1)
    flops = 2 * slots * experts * model_width * (3 * hidden + 3 * tokens)
    weight_specs = [
        pl.BlockSpec((1,) + part.shape[1:], expert) for part in (*w_parts, *v_parts)
    ]
    return pl.pallas_call(
        forward_body,
        out_shape=[
            jax.ShapeDtypeStruct((experts, slots, model_width), NARROW),
            jax.ShapeDtypeStruct((experts, slots, model_width), NARROW),
            jax.ShapeDtypeStruct((experts, slots, hidden), NARROW),
            jax.ShapeDtypeStruct((experts, slots, hidden), NARROW),
            jax.ShapeDtypeStruct((experts, 1, tokens), WIDE),
            jax.ShapeDtypeStruct((tokens // 2, model_width), WIDE),
            jax.ShapeDtypeStruct((tokens // 2, model_width), NARROW),
        ],
        grid=(experts,),
        in_specs=[
            pl.BlockSpec((1, 1, tokens), expert),
            pl.BlockSpec((1, 1, tokens), expert),
            pl.BlockSpec((tokens, model_width), whole, pipeline_mode=one),
            pl.BlockSpec((tokens, model_width), whole, pipeline_mode=one),
            *weight_specs,
        ],
        out_specs=[
            pl.BlockSpec((1, slots, model_width), expert),
            pl.BlockSpec((1, slots, model_width), expert),
            pl.BlockSpec((1, slots, hidden), expert),
            pl.BlockSpec((1, slots, hidden), expert),
            pl.BlockSpec((1, 1, tokens), expert),
            pl.BlockSpec((tokens // 2, model_width), whole, pipeline_mode=one),
            pl.BlockSpec((tokens // 2, model_width), whole, pipeline_mode=one),
        ],
        scratch_shapes=[
            pltpu.VMEM((experts * slots, model_width), NARROW),
            pltpu.VMEM((experts * slots, tokens), NARROW),
        ],
        compiler_params=pltpu.CompilerParams(vmem_limit_bytes=58 * MIB),
        cost_estimate=pl.CostEstimate(
            flops=flops, bytes_accessed=4 * experts * model_width * hidden, transcendentals=0
        ),
        name="forward",
    )(target, gate_tok, x_rows, g_rows, *w_parts, *v_parts)


def outer_body(a_ref, b_ref, _, out_ref, wide_ref):
    rows, tiles, experts, _ = out_ref.shape
    stride = wide_ref.shape[0] // rows
    group = stride // experts
    out = out_ref.reshape(rows, tiles * experts, LANES)
    for begin in range(0, tiles, group):
        for expert in range(experts):
            part = mm(a_ref[expert], b_ref[expert, :, begin * LANES : (begin + group) * LANES], TN)
            for tile in range(group):
                wide_ref[pl.ds(tile * experts + expert, rows, stride), :] = part[
                    :, tile * LANES : (tile + 1) * LANES
                ]
        out[:, begin * experts : (begin + group) * experts, :] = (
            wide_ref[...].astype(NARROW).reshape(rows, stride, LANES)
        )


def outer(a, b, holder, start, count, block, group):
    experts, slots, total = a.shape
    columns = b.shape[2]
    tiles = columns // LANES
    first = start // block
    shape = (total, tiles, experts, LANES)
    inputs = [a, b]
    specs = [
        pl.BlockSpec((experts, slots, block), lambda i: (0, 0, first + i)),
        pl.BlockSpec((experts, slots, columns), lambda i: (0, 0, 0), pipeline_mode=pl.Buffered(1)),
    ]
    body, aliases = outer_body, {2: 0}
    if holder is None:
        body, aliases = (lambda a_ref, b_ref, *rest: outer_body(a_ref, b_ref, None, *rest)), {}
    else:
        inputs.append(holder)
        specs.append(pl.BlockSpec(memory_space=pl.ANY))
    return pl.pallas_call(
        body,
        out_shape=jax.ShapeDtypeStruct(shape, NARROW),
        grid=(count // block,),
        in_specs=specs,
        out_specs=pl.BlockSpec((block, tiles, experts, LANES), lambda i: (first + i, 0, 0, 0)),
        scratch_shapes=[pltpu.VMEM((block * group * experts, LANES), WIDE)],
        input_output_aliases=aliases,
        compiler_params=pltpu.CompilerParams(vmem_limit_bytes=32 * MIB),
        cost_estimate=pl.CostEstimate(
            flops=2 * experts * slots * count * columns,
            bytes_accessed=4 * experts * count * columns,
            transcendentals=0,
        ),
        name="weight_gradient",
    )(*inputs)


def stored_view(tiled):
    rows, tiles, experts, _ = tiled.shape
    return tiled.transpose(0, 2, 1, 3).reshape(rows, experts, tiles * LANES)


def local(tokens, cotangent, expert_ids, gate_values, w_in, w_out):
    if not is_small():
        return local_general(tokens, cotangent, expert_ids, gate_values, w_in, w_out)
    tok_rows, model_width = tokens.shape
    top_count = expert_ids.shape[1]
    local_count = w_in.shape[1]
    hidden = w_in.shape[2]
    first = lax.axis_index("expert") * local_count
    meta = own_order(jnp.concatenate([expert_ids.astype(WIDE), gate_values.astype(WIDE)], axis=1)).T
    meta = jnp.stack([meta, swap(meta, CORE), swap(meta, Y), swap(meta, CORE | Y)])
    x_rows = jnp.concatenate(spread(own_order(tokens)), axis=0)
    g_rows = jnp.concatenate(spread(own_order(cotangent)), axis=0)
    w_view, v_view = tiled_view(w_in), tiled_view(w_out)
    w_parts = [split_experts(w_view, s, model_width // 2, 128) for s in (0, model_width // 2)]
    v_parts = [split_experts(v_view, s, hidden // 2, 32) for s in (0, hidden // 2)]

    ids, gates = meta[:, :top_count].astype(jnp.int32), meta[:, top_count:]
    blocks = ids.shape[0]
    names = first + jnp.arange(local_count, dtype=jnp.int32)
    named = ids[:, None] == names[None, :, None, None]
    hit = jnp.any(named, axis=2)
    gate_tok = jnp.sum(jnp.where(named, gates[:, None], 0.0), axis=2)
    earlier = jnp.tril(jnp.ones((tok_rows, tok_rows), WIDE), -1)
    position = jnp.einsum("tu,blu->blt", earlier, hit.astype(WIDE)).astype(jnp.int32)
    base = jnp.arange(blocks, dtype=jnp.int32)[:, None, None] * CAP
    target = jnp.where(hit, base + position, -1)

    def by_expert(value):
        return jnp.swapaxes(value, 0, 1).reshape(local_count, 1, blocks * tok_rows)

    xs, gs, gp, ag, gate_out, keep, send = forward(
        by_expert(target), by_expert(gate_tok), x_rows, g_rows, w_parts, v_parts
    )
    gate_out = jnp.swapaxes(gate_out.reshape(local_count, blocks, tok_rows), 0, 1)
    gate_back = jnp.sum(jnp.where(named, gate_out[:, :, None], 0.0), axis=1)
    grad_gates = collect_gates(gate_back).T.astype(NARROW)
    grad_tokens = collect(keep, send)
    grad_in = outer(xs, gp, None, 0, model_width // 2, 128, 6)
    grad_in = outer(xs, gp, grad_in, model_width // 2, model_width // 2, 128, 6)
    grad_out = outer(ag, gs, None, 0, hidden // 2, 128, 4)
    grad_out = outer(ag, gs, grad_out, hidden // 2, hidden // 2, 128, 4)
    return (grad_tokens, grad_gates, stored_view(grad_in), stored_view(grad_out))


def local_general(tokens, cotangent, expert_ids, gate_values, w_in, w_out):
    tok_rows, model_width = tokens.shape
    local_count = w_in.shape[1]
    first = lax.axis_index("expert") * local_count
    gather = functools.partial(lax.all_gather, axis_name="expert", axis=0)
    ids, gates = gather(expert_ids), gather(gate_values).astype(WIDE)
    x_blocks, g_blocks = gather(tokens), gather(cotangent)
    blocks = ids.shape[0]
    names = first + jnp.arange(local_count, dtype=jnp.int32)
    named = ids[:, None] == names[None, :, None, None]
    hit = jnp.any(named, axis=3)
    gate_tok = jnp.sum(jnp.where(named, gates[:, None], 0.0), axis=3)
    earlier = jnp.tril(jnp.ones((tok_rows, tok_rows), WIDE), -1)
    position = jnp.einsum("tu,blu->blt", earlier, hit.astype(WIDE)).astype(jnp.int32)
    slots = jnp.arange(CAP, dtype=jnp.int32)
    choose = hit[:, :, None] & (position[:, :, None] == slots[None, None, :, None])
    pick = choose.astype(NARROW)
    slot_x = jnp.einsum("blst,btd->lbsd", pick, x_blocks, preferred_element_type=WIDE).astype(NARROW)
    slot_g = jnp.einsum("blst,btd->lbsd", pick, g_blocks, preferred_element_type=WIDE).astype(NARROW)
    gate_slot = jnp.sum(jnp.where(choose, gate_tok[:, :, None], 0.0), axis=3)
    rows = blocks * CAP
    slot_x = slot_x.reshape(local_count, rows, model_width)
    slot_g = slot_g.reshape(local_count, rows, model_width)
    gate_slot = jnp.swapaxes(gate_slot, 0, 1).reshape(local_count, rows, 1)
    pre_act = jnp.einsum("lrd,dlf->lrf", slot_x, w_in, preferred_element_type=WIDE)
    upstream = jnp.einsum("lrd,fld->lrf", slot_g, w_out, preferred_element_type=WIDE)
    squash = jax.nn.sigmoid(pre_act)
    active = pre_act * squash
    gate_part = jnp.sum(active * upstream, axis=-1)
    act_gated = (gate_slot * active).astype(NARROW)
    grad_pre = (gate_slot * squash * (1.0 + pre_act * (1.0 - squash)) * upstream).astype(NARROW)
    gate_part = jnp.swapaxes(gate_part.reshape(local_count, blocks, CAP), 0, 1)
    gate_tok = jnp.sum(jnp.where(choose, gate_part[..., None], 0.0), axis=2)
    gate_back = jnp.sum(jnp.where(named, gate_tok[..., None], 0.0), axis=1)
    part_x = jnp.einsum("lrf,dlf->lrd", grad_pre, w_in, preferred_element_type=WIDE)
    part_x = part_x.astype(NARROW).reshape(local_count, blocks, CAP, model_width)
    token_part = jnp.einsum("blst,lbsd->btd", pick, part_x, preferred_element_type=WIDE)
    scatter = functools.partial(lax.psum_scatter, axis_name="expert", scatter_dimension=0)
    grad_tokens = lax.psum(scatter(token_part), "fsdp").astype(NARROW)
    grad_gates = lax.psum(scatter(gate_back), "fsdp").astype(NARROW)
    grad_in = jnp.einsum("lrd,lrf->dlf", slot_x, grad_pre, preferred_element_type=WIDE).astype(NARROW)
    grad_out = jnp.einsum("lrf,lrd->fld", act_gated, slot_g, preferred_element_type=WIDE).astype(NARROW)
    return (grad_tokens, grad_gates, grad_in, grad_out)


def solution(mesh):
    return jax.shard_map(
        local,
        mesh=mesh,
        in_specs=(
            P("expert", None),
            P("expert", None),
            P("expert", None),
            P("expert", None),
            P(None, "expert", "fsdp"),
            P("fsdp", "expert", None),
        ),
        out_specs=(
            P("expert", None),
            P("expert", None),
            P(None, "expert", "fsdp"),
            P("fsdp", "expert", None),
        ),
        check_vma=False,
    )
```

```python
import functools
import jax
import jax.numpy as jnp
from jax import lax
from jax.experimental import pallas as pl
from jax.experimental.pallas import tpu as pltpu
from jax.sharding import PartitionSpec as P

EXPERTS = 16
CAP = 40
AXES = ("fsdp", "expert")
CORE, Y, X, Z = 1, 2, 4, 8
LANES = 128
NARROW, WIDE = jnp.bfloat16, jnp.float32
MIB = 1 << 20
TN = (((0,), (0,)), ((), ()))
NT = (((1,), (1,)), ((), ()))
NN = (((1,), (0,)), ((), ()))


def mm(a, b, dims):
    return lax.dot_general(a, b, dims, preferred_element_type=WIDE)


def swap(value, mask):
    size = lax.axis_size("fsdp") * lax.axis_size("expert")
    return lax.ppermute(value, AXES, [(i, i ^ mask) for i in range(size)])


def is_small():
    return lax.axis_size("fsdp") == 8 and lax.axis_size("expert") == 4


def own_order(rows):
    x_index = lax.axis_index("fsdp") % 2
    half = rows.shape[-1] // 2
    return jnp.where(
        x_index == 0, rows, jnp.concatenate([rows[..., half:], rows[..., :half]], axis=-1)
    )


ANY = pl.BlockSpec(memory_space=pl.ANY)
FLAG = jax.ShapeDtypeStruct((8, LANES), WIDE)


def small_call(body, place, inputs, after, outs, name):
    given = len(inputs)

    def run(place_ref, *refs):
        body(place_ref, refs[:given], refs[given + len(after) :])

    def whole(array):
        return pl.BlockSpec(array.shape, lambda: (0,) * len(array.shape))

    return pl.pallas_call(
        run,
        out_shape=outs,
        in_specs=[pl.BlockSpec(memory_space=pltpu.SMEM)]
        + [whole(array) for array in inputs]
        + [ANY] * len(after),
        out_specs=[whole(out) for out in outs],
        compiler_params=pltpu.CompilerParams(vmem_limit_bytes=32 * MIB),
        cost_estimate=pl.CostEstimate(flops=0, bytes_accessed=1 << 20, transcendentals=0),
        name=name,
    )(place, *inputs, *after)


def hold(arrays, after):
    count = len(arrays)
    return pl.pallas_call(
        lambda *refs: None,
        out_shape=[jax.ShapeDtypeStruct(array.shape, array.dtype) for array in arrays],
        in_specs=[ANY] * (count + len(after)),
        out_specs=[ANY] * count,
        input_output_aliases={number: number for number in range(count)},
        cost_estimate=pl.CostEstimate(flops=0, bytes_accessed=1 << 18, transcendentals=0),
        name="hold",
    )(*arrays, *after)


def at(index, size):
    return pl.ds(pl.multiple_of(index * size, size), size)


def first_sum(place_ref, ins, outs):
    keep_ref, got_ref = ins
    mine_ref, x_ref, y_ref, xy_ref = outs
    half = mine_ref.shape[0]
    x_index = place_ref[0]

    def total(rows):
        return keep_ref[rows, :] + got_ref[rows, :].astype(WIDE)

    mine_ref[...] = total(at(x_index, half))
    x_ref[...] = total(at(1 - x_index, half)).astype(NARROW)
    y_ref[...] = total(slice(2 * half, 3 * half)).astype(NARROW)
    xy_ref[...] = total(slice(3 * half, 4 * half)).astype(NARROW)


def second_sum(place_ref, ins, outs):
    mine_ref, x_ref, y_ref, xy_ref = ins
    quarter = outs[0].shape[0]
    z_index = place_ref[1]
    for step in range(4):
        rows = at(z_index ^ step, quarter)
        total = mine_ref[rows, :] + x_ref[rows, :].astype(WIDE)
        total = total + (y_ref[rows, :].astype(WIDE) + xy_ref[rows, :].astype(WIDE))
        outs[step][...] = total.astype(outs[step].dtype)


def third_sum(place_ref, ins, outs):
    total = ins[0][...]
    for got in ins[1:]:
        total = total + got[...].astype(WIDE)
    outs[0][...] = total.astype(NARROW)


def join_z(place_ref, ins, outs):
    quarter = ins[0].shape[0]
    for step in range(4):
        outs[0][at(place_ref[1] ^ step, quarter), :] = ins[step][...]


def join_x(place_ref, ins, outs):
    half = ins[0].shape[0]
    for step in range(2):
        outs[0][at(place_ref[0] ^ step, half), :] = ins[step][...]


def collect_gates(parts):
    total = parts[0] + swap(parts[1], CORE)
    total = total + own_order(swap(parts[2], Y) + swap(parts[3], CORE | Y))
    for mask in (X, Z, 2 * Z):
        total = total + swap(total, mask)
    return total


def tiled_view(weight):
    rows, experts, columns = weight.shape
    return weight.reshape(rows, experts, columns // LANES, LANES).transpose(0, 2, 1, 3)


def odd_tiles(rows):
    tiles = -(-rows // 8)
    return 8 * (tiles + 1 - tiles % 2)


def split_body(w_ref, *refs):
    out_ref, flag_ref, wide_ref = refs[-3:]
    flag_ref[...] = jnp.zeros_like(flag_ref)
    rows, tiles, experts, _ = w_ref.shape
    held = tiles * experts
    stride = wide_ref.shape[1]
    wide_ref[:, :held, :] = w_ref.reshape(rows, held, LANES)[...].astype(WIDE)
    flat = wide_ref.reshape(rows * stride, LANES)
    for expert in range(experts):
        for tile in range(tiles):
            part = flat[pl.ds(tile * experts + expert, rows, stride), :]
            out_ref[expert, :, tile * LANES : (tile + 1) * LANES] = part.astype(NARROW)


def split_experts(view, start, rows, block, after):
    _, tiles, experts, _ = view.shape
    columns = tiles * LANES
    first = start // block
    return pl.pallas_call(
        split_body,
        out_shape=[jax.ShapeDtypeStruct((experts, rows, columns), NARROW), FLAG],
        grid=(rows // block,),
        in_specs=[
            pl.BlockSpec((block, tiles, experts, LANES), lambda i: (first + i, 0, 0, 0)),
            *[ANY] * len(after),
        ],
        out_specs=[
            pl.BlockSpec((experts, block, columns), lambda i: (0, i, 0)),
            pl.BlockSpec(FLAG.shape, lambda i: (0, 0)),
        ],
        scratch_shapes=[pltpu.VMEM((block, odd_tiles(tiles * experts), LANES), WIDE)],
        compiler_params=pltpu.CompilerParams(vmem_limit_bytes=56 * MIB),
        cost_estimate=pl.CostEstimate(
            flops=0, bytes_accessed=4 * experts * rows * columns, transcendentals=0
        ),
        name="split_experts",
    )(view, *after)


def forward_body(
    target_ref, gate_ref, w0_ref, w1_ref, v0_ref, v1_ref, *refs
):
    step = pl.program_id(0)
    pieces = refs[:-12]
    xs_ref, gs_ref, gp_ref, ag_ref, gate_out_ref, keep_ref, send_ref = refs[-12:-5]
    x_ref, g_ref, back_ref, pick_ref, sem = refs[-5:]

    @pl.when(step == 0)
    def _():
        copies = []
        for number, whole in enumerate((x_ref, g_ref)):
            begin = 0
            for piece in pieces[number * len(pieces) // 2 : (number + 1) * len(pieces) // 2]:
                count = piece.shape[0]
                copies.append(
                    pltpu.make_async_copy(piece, whole.at[begin : begin + count], sem.at[len(copies)])
                )
                begin += count
        for copy in copies:
            copy.start()
        for copy in copies:
            copy.wait()

    slots, model_width = xs_ref.shape[1:]
    tokens = x_ref.shape[0]
    half_d = w0_ref.shape[1]
    columns = 512
    target = target_ref[0]
    choose = lax.broadcasted_iota(jnp.int32, (slots, tokens), 0) == target
    pick = choose.astype(WIDE).astype(NARROW)
    rows = pl.ds(pl.multiple_of(step * slots, slots), slots)
    pick_ref[rows, :] = pick
    gate = jnp.sum(jnp.where(choose, gate_ref[0], 0.0), axis=1, keepdims=True)
    for begin in range(0, model_width, columns):
        part = slice(begin, begin + columns)
        xs_ref[0, :, part] = mm(pick, x_ref[:, part], NN).astype(NARROW)
        gs_ref[0, :, part] = mm(pick, g_ref[:, part], NN).astype(NARROW)
    pre_act = mm(xs_ref[0, :, :half_d], w0_ref[0], NN) + mm(xs_ref[0, :, half_d:], w1_ref[0], NN)
    squash = jax.nn.sigmoid(pre_act)
    active = pre_act * squash
    slope = gate * squash * (1.0 + pre_act * (1.0 - squash))
    ag_ref[0] = (gate * active).astype(NARROW)
    half_f = v0_ref.shape[1]
    gate_part = jnp.zeros((slots, 1), WIDE)
    for begin, v_ref in ((0, v0_ref), (half_f, v1_ref)):
        upstream = mm(gs_ref[0], v_ref[0], NT)
        part = slice(begin, begin + half_f)
        gate_part = gate_part + jnp.sum(active[:, part] * upstream, axis=1, keepdims=True)
        gp_ref[0, :, part] = (slope[:, part] * upstream).astype(NARROW)
    gate_out_ref[0] = jnp.sum(jnp.where(choose, gate_part, 0.0), axis=0, keepdims=True)
    for begin in range(0, model_width, columns):
        w_ref = w0_ref if begin < half_d else w1_ref
        inner = begin % half_d
        back = mm(gp_ref[0], w_ref[0, inner : inner + columns, :], NT)
        back_ref[rows, begin : begin + columns] = back.astype(NARROW)

    @pl.when(step == pl.num_programs(0) - 1)
    def _():
        quarter = tokens // 4
        for begin in range(0, model_width, columns):
            part = slice(begin, begin + columns)
            summed = mm(pick_ref[...], back_ref[:, part], TN)
            for pair in range(2):
                lower = 2 * pair * quarter
                keep_ref[pair * quarter : (pair + 1) * quarter, part] = summed[lower : lower + quarter]
                send_ref[pair * quarter : (pair + 1) * quarter, part] = summed[
                    lower + quarter : lower + 2 * quarter
                ].astype(NARROW)


def forward(target, gate_tok, x_pieces, g_pieces, w_parts, v_parts):
    experts, _, tokens = target.shape
    model_width = x_pieces[0].shape[1]
    hidden = w_parts[0].shape[2]
    slots = tokens // 128 * CAP
    whole = lambda i: (0, 0)
    expert = lambda i: (i, 0, 0)
    one = pl.Buffered(1)
    flops = 2 * slots * experts * model_width * (3 * hidden + 3 * tokens)
    weight_specs = [
        pl.BlockSpec((1,) + part.shape[1:], expert) for part in (*w_parts, *v_parts)
    ]
    return pl.pallas_call(
        forward_body,
        out_shape=[
            jax.ShapeDtypeStruct((experts, slots, model_width), NARROW),
            jax.ShapeDtypeStruct((experts, slots, model_width), NARROW),
            jax.ShapeDtypeStruct((experts, slots, hidden), NARROW),
            jax.ShapeDtypeStruct((experts, slots, hidden), NARROW),
            jax.ShapeDtypeStruct((experts, 1, tokens), WIDE),
            jax.ShapeDtypeStruct((tokens // 2, model_width), WIDE),
            jax.ShapeDtypeStruct((tokens // 2, model_width), NARROW),
        ],
        grid=(experts,),
        in_specs=[
            pl.BlockSpec((1, 1, tokens), expert),
            pl.BlockSpec((1, 1, tokens), expert),
            *weight_specs,
            *[ANY] * (len(x_pieces) + len(g_pieces)),
        ],
        out_specs=[
            pl.BlockSpec((1, slots, model_width), expert),
            pl.BlockSpec((1, slots, model_width), expert),
            pl.BlockSpec((1, slots, hidden), expert),
            pl.BlockSpec((1, slots, hidden), expert),
            pl.BlockSpec((1, 1, tokens), expert),
            pl.BlockSpec((tokens // 2, model_width), whole, pipeline_mode=one),
            pl.BlockSpec((tokens // 2, model_width), whole, pipeline_mode=one),
        ],
        scratch_shapes=[
            pltpu.VMEM((tokens, model_width), NARROW),
            pltpu.VMEM((tokens, model_width), NARROW),
            pltpu.VMEM((experts * slots, model_width), NARROW),
            pltpu.VMEM((experts * slots, tokens), NARROW),
            pltpu.SemaphoreType.DMA((len(x_pieces) + len(g_pieces),)),
        ],
        compiler_params=pltpu.CompilerParams(vmem_limit_bytes=58 * MIB),
        cost_estimate=pl.CostEstimate(
            flops=flops, bytes_accessed=4 * experts * model_width * hidden, transcendentals=0
        ),
        name="forward",
    )(target, gate_tok, *w_parts, *v_parts, *x_pieces, *g_pieces)


def outer_body(group, a_ref, b_ref, *refs):
    out_ref, flag_ref, wide_ref = refs[-3:]
    rows, tiles, experts, _ = out_ref.shape
    stride = wide_ref.shape[1]
    held = group * experts
    out = out_ref.reshape(rows, tiles * experts, LANES)
    flat = wide_ref.reshape(rows * stride, LANES)
    for begin in range(0, tiles, group):
        for expert in range(experts):
            part = mm(a_ref[expert], b_ref[expert, :, begin * LANES : (begin + group) * LANES], TN)
            for tile in range(group):
                flat[pl.ds(tile * experts + expert, rows, stride), :] = part[
                    :, tile * LANES : (tile + 1) * LANES
                ]
        out[:, begin * experts : begin * experts + held, :] = wide_ref[:, :held, :].astype(NARROW)
    flag_ref[...] = jnp.zeros_like(flag_ref)


def outer(a, b, holder, start, count, block, group, after):
    experts, slots, total = a.shape
    columns = b.shape[2]
    tiles = columns // LANES
    first = start // block
    extra = list(after) if holder is None else [holder, *after]
    return pl.pallas_call(
        functools.partial(outer_body, group),
        out_shape=[jax.ShapeDtypeStruct((total, tiles, experts, LANES), NARROW), FLAG],
        grid=(count // block,),
        in_specs=[
            pl.BlockSpec((experts, slots, block), lambda i: (0, 0, first + i)),
            pl.BlockSpec(
                (experts, slots, columns), lambda i: (0, 0, 0), pipeline_mode=pl.Buffered(1)
            ),
            *[ANY] * len(extra),
        ],
        out_specs=[
            pl.BlockSpec((block, tiles, experts, LANES), lambda i: (first + i, 0, 0, 0)),
            pl.BlockSpec(FLAG.shape, lambda i: (0, 0)),
        ],
        scratch_shapes=[pltpu.VMEM((block, odd_tiles(group * experts), LANES), WIDE)],
        input_output_aliases={} if holder is None else {2: 0},
        compiler_params=pltpu.CompilerParams(vmem_limit_bytes=40 * MIB),
        cost_estimate=pl.CostEstimate(
            flops=2 * experts * slots * count * columns,
            bytes_accessed=4 * experts * count * columns,
            transcendentals=0,
        ),
        name="weight_gradient",
    )(a, b, *extra)


def stored_view(tiled):
    rows, tiles, experts, _ = tiled.shape
    return tiled.transpose(0, 2, 1, 3).reshape(rows, experts, tiles * LANES)


def local(tokens, cotangent, expert_ids, gate_values, w_in, w_out):
    if not is_small():
        return local_general(tokens, cotangent, expert_ids, gate_values, w_in, w_out)
    tok_rows, model_width = tokens.shape
    top_count = expert_ids.shape[1]
    local_count = w_in.shape[1]
    hidden = w_in.shape[2]
    half = tok_rows // 2
    first = lax.axis_index("expert") * local_count
    fsdp = lax.axis_index("fsdp")
    x_index = fsdp % 2
    place = jnp.stack([x_index, fsdp // 2]).astype(jnp.int32)

    meta = jnp.concatenate([expert_ids.astype(WIDE), gate_values.astype(WIDE)], axis=1).T
    turned = own_order(meta)
    meta = jnp.stack([meta, swap(meta, CORE), swap(turned, Y), swap(turned, CORE | Y)])
    w_view, v_view = tiled_view(w_in), tiled_view(w_out)
    x_near = swap(lax.dynamic_slice_in_dim(tokens, x_index * half, half, axis=0), Y)
    g_near = swap(lax.dynamic_slice_in_dim(cotangent, x_index * half, half, axis=0), Y)
    x_core, g_core = swap(tokens, CORE), swap(cotangent, CORE)
    w_low, flag = split_experts(w_view, 0, model_width // 2, 256, [])
    (x_near,) = hold([x_near], [flag])
    x_far = swap(x_near, X)
    x_near_core = swap(x_near, CORE)
    w_high, flag = split_experts(w_view, model_width // 2, model_width // 2, 256, [x_near])
    x_far, g_near = hold([x_far, g_near], [flag])
    g_far = swap(g_near, X)
    g_near_core = swap(g_near, CORE)
    x_far_core = swap(x_far, CORE)
    v_low, flag = split_experts(v_view, 0, hidden // 2, 64, [x_far])
    (g_far,) = hold([g_far], [flag])
    g_far_core = swap(g_far, CORE)
    v_high, _ = split_experts(v_view, hidden // 2, hidden // 2, 64, [g_far])
    x_pieces = [tokens, x_core, x_near, x_far, x_near_core, x_far_core]
    g_pieces = [cotangent, g_core, g_near, g_far, g_near_core, g_far_core]

    ids, gates = meta[:, :top_count].astype(jnp.int32), meta[:, top_count:]
    blocks = ids.shape[0]
    names = first + jnp.arange(local_count, dtype=jnp.int32)
    named = ids[:, None] == names[None, :, None, None]
    hit = jnp.any(named, axis=2)
    gate_tok = jnp.sum(jnp.where(named, gates[:, None], 0.0), axis=2)
    earlier = jnp.tril(jnp.ones((tok_rows, tok_rows), WIDE), -1)
    position = jnp.einsum("tu,blu->blt", earlier, hit.astype(WIDE)).astype(jnp.int32)
    base = jnp.arange(blocks, dtype=jnp.int32)[:, None, None] * CAP
    target = jnp.where(hit, base + position, -1)

    def by_expert(value):
        return jnp.swapaxes(value, 0, 1).reshape(local_count, 1, blocks * tok_rows)

    xs, gs, gp, ag, gate_out, keep, send = forward(
        by_expert(target), by_expert(gate_tok), x_pieces, g_pieces, [w_low, w_high], [v_low, v_high]
    )
    gate_out = jnp.swapaxes(gate_out.reshape(local_count, blocks, tok_rows), 0, 1)
    gate_back = jnp.sum(jnp.where(named, gate_out[:, :, None], 0.0), axis=1)
    grad_gates = collect_gates(gate_back).T.astype(NARROW)

    def shape(rows, dtype):
        return jax.ShapeDtypeStruct((rows, model_width), dtype)

    def in_part(holder, number, after):
        rows = model_width // 4
        return outer(xs, gp, holder, number * rows, rows, 128, 6, after)

    def out_part(holder, number, after):
        rows = hidden // 3
        return outer(ag, gs, holder, number * rows, rows, 128, 8, after)

    got = swap(send, CORE)
    grad_in, flag = in_part(None, 0, [])
    mine, *sends = small_call(
        first_sum, place, [keep, got], [flag],
        [shape(half, WIDE)] + [shape(half, NARROW)] * 3, "first_sum",
    )
    got = [swap(part, mask) for part, mask in zip(sends, (X, Y, X | Y))]
    grad_in, flag = in_part(grad_in, 1, [mine])
    grad_in, flag = in_part(grad_in, 2, [flag])
    grad_in, flag = in_part(grad_in, 3, [flag])
    mine, *sends = small_call(
        second_sum, place, [mine, *got], [flag],
        [shape(half // 4, WIDE)] + [shape(half // 4, NARROW)] * 3, "second_sum",
    )
    got = [swap(part, mask * Z) for part, mask in zip(sends, (1, 2, 3))]
    grad_out, flag = out_part(None, 0, [mine])
    (final,) = small_call(
        third_sum, place, [mine, *got], [flag], [shape(half // 4, NARROW)], "third_sum"
    )
    got = [swap(final, mask * Z) for mask in (1, 2, 3)]
    grad_out, flag = out_part(grad_out, 1, [final])
    (near,) = small_call(join_z, place, [final, *got], [flag], [shape(half, NARROW)], "join_z")
    far = swap(near, X)
    grad_out, flag = out_part(grad_out, 2, [near])
    (grad_tokens,) = small_call(
        join_x, place, [near, far], [flag], [shape(tok_rows, NARROW)], "join_x"
    )
    return (grad_tokens, grad_gates, stored_view(grad_in), stored_view(grad_out))


def local_general(tokens, cotangent, expert_ids, gate_values, w_in, w_out):
    tok_rows, model_width = tokens.shape
    local_count = w_in.shape[1]
    first = lax.axis_index("expert") * local_count
    gather = functools.partial(lax.all_gather, axis_name="expert", axis=0)
    ids, gates = gather(expert_ids), gather(gate_values).astype(WIDE)
    x_blocks, g_blocks = gather(tokens), gather(cotangent)
    blocks = ids.shape[0]
    names = first + jnp.arange(local_count, dtype=jnp.int32)
    named = ids[:, None] == names[None, :, None, None]
    hit = jnp.any(named, axis=3)
    gate_tok = jnp.sum(jnp.where(named, gates[:, None], 0.0), axis=3)
    earlier = jnp.tril(jnp.ones((tok_rows, tok_rows), WIDE), -1)
    position = jnp.einsum("tu,blu->blt", earlier, hit.astype(WIDE)).astype(jnp.int32)
    slots = jnp.arange(CAP, dtype=jnp.int32)
    choose = hit[:, :, None] & (position[:, :, None] == slots[None, None, :, None])
    pick = choose.astype(NARROW)
    slot_x = jnp.einsum("blst,btd->lbsd", pick, x_blocks, preferred_element_type=WIDE).astype(NARROW)
    slot_g = jnp.einsum("blst,btd->lbsd", pick, g_blocks, preferred_element_type=WIDE).astype(NARROW)
    gate_slot = jnp.sum(jnp.where(choose, gate_tok[:, :, None], 0.0), axis=3)
    rows = blocks * CAP
    slot_x = slot_x.reshape(local_count, rows, model_width)
    slot_g = slot_g.reshape(local_count, rows, model_width)
    gate_slot = jnp.swapaxes(gate_slot, 0, 1).reshape(local_count, rows, 1)
    pre_act = jnp.einsum("lrd,dlf->lrf", slot_x, w_in, preferred_element_type=WIDE)
    upstream = jnp.einsum("lrd,fld->lrf", slot_g, w_out, preferred_element_type=WIDE)
    squash = jax.nn.sigmoid(pre_act)
    active = pre_act * squash
    gate_part = jnp.sum(active * upstream, axis=-1)
    act_gated = (gate_slot * active).astype(NARROW)
    grad_pre = (gate_slot * squash * (1.0 + pre_act * (1.0 - squash)) * upstream).astype(NARROW)
    gate_part = jnp.swapaxes(gate_part.reshape(local_count, blocks, CAP), 0, 1)
    gate_tok = jnp.sum(jnp.where(choose, gate_part[..., None], 0.0), axis=2)
    gate_back = jnp.sum(jnp.where(named, gate_tok[..., None], 0.0), axis=1)
    part_x = jnp.einsum("lrf,dlf->lrd", grad_pre, w_in, preferred_element_type=WIDE)
    part_x = part_x.astype(NARROW).reshape(local_count, blocks, CAP, model_width)
    token_part = jnp.einsum("blst,lbsd->btd", pick, part_x, preferred_element_type=WIDE)
    scatter = functools.partial(lax.psum_scatter, axis_name="expert", scatter_dimension=0)
    grad_tokens = lax.psum(scatter(token_part), "fsdp").astype(NARROW)
    grad_gates = lax.psum(scatter(gate_back), "fsdp").astype(NARROW)
    grad_in = jnp.einsum("lrd,lrf->dlf", slot_x, grad_pre, preferred_element_type=WIDE).astype(NARROW)
    grad_out = jnp.einsum("lrf,lrd->fld", act_gated, slot_g, preferred_element_type=WIDE).astype(NARROW)
    return (grad_tokens, grad_gates, grad_in, grad_out)


def solution(mesh):
    return jax.shard_map(
        local,
        mesh=mesh,
        in_specs=(
            P("expert", None),
            P("expert", None),
            P("expert", None),
            P("expert", None),
            P(None, "expert", "fsdp"),
            P("fsdp", "expert", None),
        ),
        out_specs=(
            P("expert", None),
            P("expert", None),
            P(None, "expert", "fsdp"),
            P("fsdp", "expert", None),
        ),
        check_vma=False,
    )
```

```python
import functools
import jax
import jax.numpy as jnp
import numpy as np
from jax import lax
from jax.experimental import pallas as pl
from jax.experimental.pallas import tpu as pltpu
from jax.sharding import PartitionSpec as P

EXPERTS = 16
CAP = 40
AXES = ("fsdp", "expert")
CORE, Y, X, Z = 1, 2, 4, 8
LANES = 128
NARROW, WIDE = jnp.bfloat16, jnp.float32
MIB = 1 << 20
TN = (((0,), (0,)), ((), ()))
NT = (((1,), (1,)), ((), ()))
NN = (((1,), (0,)), ((), ()))


def mm(a, b, dims):
    return lax.dot_general(a, b, dims, preferred_element_type=WIDE)


def swap(value, mask):
    size = lax.axis_size("fsdp") * lax.axis_size("expert")
    return lax.ppermute(value, AXES, [(i, i ^ mask) for i in range(size)])


def is_small():
    return lax.axis_size("fsdp") == 8 and lax.axis_size("expert") == 4


def own_order(rows):
    x_index = lax.axis_index("fsdp") % 2
    half = rows.shape[-1] // 2
    return jnp.where(
        x_index == 0, rows, jnp.concatenate([rows[..., half:], rows[..., :half]], axis=-1)
    )


ANY = pl.BlockSpec(memory_space=pl.ANY)
FLAG = jax.ShapeDtypeStruct((8, LANES), WIDE)


def small_call(body, place, inputs, after, outs, name, grant=12):
    given = len(inputs)

    def run(place_ref, *refs):
        body(place_ref, refs[:given], refs[given + len(after) :])

    def whole(array):
        return pl.BlockSpec(array.shape, lambda: (0,) * len(array.shape))

    return pl.pallas_call(
        run,
        out_shape=outs,
        in_specs=[pl.BlockSpec(memory_space=pltpu.SMEM)]
        + [whole(array) for array in inputs]
        + [ANY] * len(after),
        out_specs=[whole(out) for out in outs],
        compiler_params=pltpu.CompilerParams(vmem_limit_bytes=grant * MIB),
        cost_estimate=pl.CostEstimate(flops=0, bytes_accessed=1 << 20, transcendentals=0),
        name=name,
    )(place, *inputs, *after)


def hold(arrays, after):
    count = len(arrays)
    return pl.pallas_call(
        lambda *refs: None,
        out_shape=[jax.ShapeDtypeStruct(array.shape, array.dtype) for array in arrays],
        in_specs=[ANY] * (count + len(after)),
        out_specs=[ANY] * count,
        input_output_aliases={number: number for number in range(count)},
        cost_estimate=pl.CostEstimate(flops=0, bytes_accessed=1 << 18, transcendentals=0),
        name="hold",
    )(*arrays, *after)


def at(index, size):
    return pl.ds(pl.multiple_of(index * size, size), size)


def first_sum(place_ref, ins, outs):
    keep_ref, got_ref = ins
    mine_ref, x_ref, y_ref, xy_ref = outs
    half = mine_ref.shape[0]
    x_index = place_ref[0]

    def total(rows):
        return keep_ref[rows, :] + got_ref[rows, :].astype(WIDE)

    mine_ref[...] = total(at(x_index, half))
    x_ref[...] = total(at(1 - x_index, half)).astype(NARROW)
    y_ref[...] = total(slice(2 * half, 3 * half)).astype(NARROW)
    xy_ref[...] = total(slice(3 * half, 4 * half)).astype(NARROW)


def second_sum(place_ref, ins, outs):
    mine_ref, x_ref, y_ref, xy_ref = ins
    quarter = outs[0].shape[0]
    z_index = place_ref[1]
    for step in range(4):
        rows = at(z_index ^ step, quarter)
        total = mine_ref[rows, :] + x_ref[rows, :].astype(WIDE)
        total = total + (y_ref[rows, :].astype(WIDE) + xy_ref[rows, :].astype(WIDE))
        outs[step][...] = total.astype(outs[step].dtype)


def third_sum(place_ref, ins, outs):
    total = ins[0][...]
    for got in ins[1:]:
        total = total + got[...].astype(WIDE)
    outs[0][...] = total.astype(NARROW)


def join_z(place_ref, ins, outs):
    quarter = ins[0].shape[0]
    for step in range(4):
        outs[0][at(place_ref[1] ^ step, quarter), :] = ins[step][...]


def join_x(place_ref, ins, outs):
    half = ins[0].shape[0]
    model_width = outs[0].shape[1]
    for step in range(2):
        rows = at(place_ref[0] ^ step, half)
        outs[0][rows, :] = ins[step][:, :model_width]
        outs[1][rows, :] = ins[step][:, model_width:]


def sorter(rows, tiles, experts):
    size = rows * tiles * experts
    order = np.arange(size).reshape(rows, tiles, experts).transpose(2, 1, 0).reshape(-1)
    return jnp.asarray(np.eye(size, dtype=np.float32)[order], NARROW)


def tiled_view(weight):
    rows, experts, columns = weight.shape
    return weight.reshape(rows, experts, columns // LANES, LANES).transpose(0, 2, 1, 3)


def split_body(group, some, sort_ref, w_ref, *refs):
    out_ref, flag_ref = refs[-2:]
    flag_ref[...] = jnp.zeros_like(flag_ref)
    rows, tiles, experts, _ = w_ref.shape
    held = group * experts
    flat = w_ref.reshape(rows, tiles * experts, LANES)
    places = [(row, tile) for row in range(0, rows, some) for tile in range(0, tiles, group)]
    for pair in zip(places[::2], places[1::2]):
        blocks = [
            flat[row : row + some, tile * experts : tile * experts + held, :].reshape(
                some * held, LANES
            )
            for row, tile in pair
        ]
        result = mm(sort_ref[...], jnp.concatenate(blocks, axis=1), NN)
        for expert in range(experts):
            for tile in range(group):
                begin = (expert * group + tile) * some
                parts = [
                    result[begin : begin + some, side * LANES : (side + 1) * LANES]
                    for side in range(2)
                ]
                if some == 8:
                    row, first = pair[0][0], pair[0][1] + tile
                    out_ref[expert, row : row + 16, first * LANES : (first + 1) * LANES] = (
                        jnp.concatenate(parts, axis=0).astype(NARROW)
                    )
                else:
                    for (row, first), part in zip(pair, parts):
                        column = (first + tile) * LANES
                        out_ref[expert, row : row + some, column : column + LANES] = part.astype(
                            NARROW
                        )


def split_experts(view, sort, block, group, some, after):
    rows, tiles, experts, _ = view.shape
    columns = tiles * LANES
    return pl.pallas_call(
        functools.partial(split_body, group, some),
        out_shape=[jax.ShapeDtypeStruct((experts, rows, columns), NARROW), FLAG],
        grid=(rows // block,),
        in_specs=[
            pl.BlockSpec(sort.shape, lambda i: (0, 0)),
            pl.BlockSpec((block, tiles, experts, LANES), lambda i: (i, 0, 0, 0)),
            *[ANY] * len(after),
        ],
        out_specs=[
            pl.BlockSpec((experts, block, columns), lambda i: (0, i, 0)),
            pl.BlockSpec(FLAG.shape, lambda i: (0, 0)),
        ],
        compiler_params=pltpu.CompilerParams(vmem_limit_bytes=56 * MIB),
        cost_estimate=pl.CostEstimate(
            flops=0, bytes_accessed=4 * experts * rows * columns, transcendentals=0
        ),
        name="split_experts",
    )(sort, view, *after)


def fetch(pieces, whole, sem):
    copies, begin = [], 0
    for number, piece in enumerate(pieces):
        count = piece.shape[0]
        copies.append(
            pltpu.make_async_copy(piece, whole.at[begin : begin + count], sem.at[number])
        )
        begin += count
    for copy in copies:
        copy.start()
    for copy in copies:
        copy.wait()


def chosen(code_ref, slots):
    code = code_ref[0]
    tokens = code.shape[1]
    return lax.broadcasted_iota(jnp.int32, (slots, tokens), 0) == jnp.bitwise_and(code, 1023)


def forward_tokens_body(code_ref, gate_ref, w_ref, *refs):
    pieces, (xs_ref, ag_ref, active_ref, slope_ref, x_ref, sem) = refs[:-6], refs[-6:]
    slots, model_width = xs_ref.shape[1:]
    columns = 512
    pl.when(pl.program_id(0) == 0)(lambda: fetch(pieces, x_ref, sem))
    choose = chosen(code_ref, slots)
    pick = choose.astype(WIDE).astype(NARROW)
    gate = jnp.sum(jnp.where(choose, gate_ref[0], 0.0), axis=1, keepdims=True)
    for begin in range(0, model_width, columns):
        part = slice(begin, begin + columns)
        xs_ref[0, :, part] = mm(pick, x_ref[:, part], NN).astype(NARROW)
    pre_act = mm(xs_ref[0], w_ref[0], NN)
    squash = jax.nn.sigmoid(pre_act)
    active = pre_act * squash
    active_ref[0] = active
    ag_ref[0] = (gate * active).astype(NARROW)
    slope_ref[0] = gate * squash * (1.0 + pre_act * (1.0 - squash))


def forward_tokens(code, gate_tok, x_pieces, w_split):
    experts, model_width, hidden = w_split.shape
    tokens = code.shape[2]
    slots = tokens // 128 * CAP
    expert = lambda i: (i, 0, 0)
    shapes = [(model_width, NARROW), (hidden, NARROW), (hidden, WIDE), (hidden, WIDE)]
    return pl.pallas_call(
        forward_tokens_body,
        out_shape=[jax.ShapeDtypeStruct((experts, slots, width), dtype) for width, dtype in shapes],
        grid=(experts,),
        in_specs=[
            pl.BlockSpec((1, 1, tokens), expert),
            pl.BlockSpec((1, 1, tokens), expert),
            pl.BlockSpec((1, model_width, hidden), expert),
            *[ANY] * len(x_pieces),
        ],
        out_specs=[pl.BlockSpec((1, slots, width), expert) for width, _ in shapes],
        scratch_shapes=[
            pltpu.VMEM((tokens, model_width), NARROW),
            pltpu.SemaphoreType.DMA((len(x_pieces),)),
        ],
        compiler_params=pltpu.CompilerParams(vmem_limit_bytes=56 * MIB),
        cost_estimate=pl.CostEstimate(
            flops=2 * slots * experts * model_width * (hidden + tokens),
            bytes_accessed=2 * experts * model_width * hidden,
            transcendentals=0,
        ),
        name="forward_tokens",
    )(code, gate_tok, w_split, *x_pieces)


def forward_cotangents_body(code_ref, active_ref, slope_ref, w_ref, v_ref, *refs):
    pieces = refs[:-8]
    gs_ref, gp_ref, keep_ref, send_ref, g_ref, back_ref, pick_ref, sem = refs[-8:]
    step = pl.program_id(0)
    slots, model_width = gs_ref.shape[1:]
    columns = 512
    pl.when(step == 0)(lambda: fetch(pieces, g_ref, sem))
    choose = chosen(code_ref, slots)
    pick = choose.astype(WIDE).astype(NARROW)
    rows = pl.ds(pl.multiple_of(step * slots, slots), slots)
    pick_ref[rows, :] = pick
    for begin in range(0, model_width, columns):
        part = slice(begin, begin + columns)
        gs_ref[0, :, part] = mm(pick, g_ref[:, part], NN).astype(NARROW)
    upstream = mm(gs_ref[0], v_ref[0], NT)
    gate_part = jnp.sum(active_ref[0] * upstream, axis=1, keepdims=True)
    gp_ref[0] = (slope_ref[0] * upstream).astype(NARROW)
    for begin in range(0, model_width, columns):
        back = mm(gp_ref[0], w_ref[0, begin : begin + columns, :], NT)
        back_ref[rows, begin : begin + columns] = back.astype(NARROW)
    which = jnp.sum(
        jnp.where(choose, jnp.right_shift(code_ref[0], 10), 0), axis=1, keepdims=True
    )
    lane = lax.broadcasted_iota(jnp.int32, (slots, LANES), 1)
    high = gate_part.astype(NARROW).astype(WIDE)
    gates = jnp.where(lane == which, high, 0.0)
    gates = jnp.where(lane == which + LANES // 2, gate_part - high, gates)
    back_ref[rows, model_width:] = gates.astype(NARROW)

    @pl.when(step == pl.num_programs(0) - 1)
    def _():
        quarter = g_ref.shape[0] // 4
        for begin in range(0, model_width + LANES, columns):
            part = slice(begin, min(begin + columns, model_width + LANES))
            summed = mm(pick_ref[...], back_ref[:, part], TN)
            if begin == model_width:
                summed = summed + pltpu.roll(summed, LANES // 2, 1)
            for pair in range(2):
                lower = 2 * pair * quarter
                into = slice(pair * quarter, (pair + 1) * quarter)
                keep_ref[into, part] = summed[lower : lower + quarter]
                send_ref[into, part] = summed[lower + quarter : lower + 2 * quarter].astype(NARROW)


def forward_cotangents(code, active, slope, g_pieces, w_split, v_split):
    experts, model_width, hidden = w_split.shape
    tokens = code.shape[2]
    slots = tokens // 128 * CAP
    width = model_width + LANES
    expert = lambda i: (i, 0, 0)
    whole = lambda i: (0, 0)
    one = pl.Buffered(1)
    return pl.pallas_call(
        forward_cotangents_body,
        out_shape=[
            jax.ShapeDtypeStruct((experts, slots, model_width), NARROW),
            jax.ShapeDtypeStruct((experts, slots, hidden), NARROW),
            jax.ShapeDtypeStruct((tokens // 2, width), WIDE),
            jax.ShapeDtypeStruct((tokens // 2, width), NARROW),
        ],
        grid=(experts,),
        in_specs=[
            pl.BlockSpec((1, 1, tokens), expert),
            pl.BlockSpec((1, slots, hidden), expert),
            pl.BlockSpec((1, slots, hidden), expert),
            pl.BlockSpec((1, model_width, hidden), expert),
            pl.BlockSpec((1, hidden, model_width), expert),
            *[ANY] * len(g_pieces),
        ],
        out_specs=[
            pl.BlockSpec((1, slots, model_width), expert),
            pl.BlockSpec((1, slots, hidden), expert),
            pl.BlockSpec((tokens // 2, width), whole, pipeline_mode=one),
            pl.BlockSpec((tokens // 2, width), whole, pipeline_mode=one),
        ],
        scratch_shapes=[
            pltpu.VMEM((tokens, model_width), NARROW),
            pltpu.VMEM((experts * slots, width), NARROW),
            pltpu.VMEM((experts * slots, tokens), NARROW),
            pltpu.SemaphoreType.DMA((len(g_pieces),)),
        ],
        compiler_params=pltpu.CompilerParams(vmem_limit_bytes=56 * MIB),
        cost_estimate=pl.CostEstimate(
            flops=2 * slots * experts * model_width * (2 * hidden + 2 * tokens),
            bytes_accessed=4 * experts * model_width * hidden,
            transcendentals=0,
        ),
        name="forward_cotangents",
    )(code, active, slope, w_split, v_split, *g_pieces)


def outer_body(group, some, sort_ref, a_ref, b_ref, *refs):
    out_ref, flag_ref = refs[-2:]
    flag_ref[...] = jnp.zeros_like(flag_ref)
    rows, tiles, experts, _ = out_ref.shape
    held = group * experts
    out = out_ref.reshape(rows, tiles * experts, LANES)
    across = 1 if some == 8 else 2
    for tile in range(0, tiles, group * across):
        wide = group * across * LANES
        parts = [
            mm(a_ref[expert], b_ref[expert, :, tile * LANES : tile * LANES + wide], TN)
            for expert in range(experts)
        ]
        for row in range(0, rows, 16):
            pair = [(row, 0), (row + 8, 0)] if some == 8 else [(row, 0), (row, group)]
            blocks = [
                jnp.concatenate(
                    [
                        part[begin : begin + some, (first + inner) * LANES : (first + inner + 1) * LANES]
                        for part in parts
                        for inner in range(group)
                    ],
                    axis=0,
                )
                for begin, first in pair
            ]
            result = mm(sort_ref[...], jnp.concatenate(blocks, axis=1).astype(NARROW), NN)
            for side, (begin, first) in enumerate(pair):
                at_tile = (tile + first) * experts
                out[begin : begin + some, at_tile : at_tile + held, :] = (
                    result[:, side * LANES : (side + 1) * LANES]
                    .astype(NARROW)
                    .reshape(some, held, LANES)
                )


def outer(sort, a, b, holder, start, count, group, some, after):
    experts, slots, total = a.shape
    columns = b.shape[2]
    tiles = columns // LANES
    block = 128
    first = start // block
    extra = list(after) if holder is None else [holder, *after]
    return pl.pallas_call(
        functools.partial(outer_body, group, some),
        out_shape=[jax.ShapeDtypeStruct((total, tiles, experts, LANES), NARROW), FLAG],
        grid=(count // block,),
        in_specs=[
            pl.BlockSpec(sort.shape, lambda i: (0, 0)),
            pl.BlockSpec((experts, slots, block), lambda i: (0, 0, first + i)),
            pl.BlockSpec(
                (experts, slots, columns), lambda i: (0, 0, 0), pipeline_mode=pl.Buffered(1)
            ),
            *[ANY] * len(extra),
        ],
        out_specs=[
            pl.BlockSpec((block, tiles, experts, LANES), lambda i: (first + i, 0, 0, 0)),
            pl.BlockSpec(FLAG.shape, lambda i: (0, 0)),
        ],
        input_output_aliases={} if holder is None else {3: 0},
        compiler_params=pltpu.CompilerParams(vmem_limit_bytes=56 * MIB),
        cost_estimate=pl.CostEstimate(
            flops=2 * experts * slots * count * columns,
            bytes_accessed=4 * experts * count * columns,
            transcendentals=0,
        ),
        name="weight_gradient",
    )(sort, a, b, *extra)


def stored_view(tiled):
    rows, tiles, experts, _ = tiled.shape
    return tiled.transpose(0, 2, 1, 3).reshape(rows, experts, tiles * LANES)


def local(tokens, cotangent, expert_ids, gate_values, w_in, w_out):
    if not is_small():
        return local_general(tokens, cotangent, expert_ids, gate_values, w_in, w_out)
    tok_rows, model_width = tokens.shape
    top_count = expert_ids.shape[1]
    local_count = w_in.shape[1]
    hidden = w_in.shape[2]
    half = tok_rows // 2
    first = lax.axis_index("expert") * local_count
    fsdp = lax.axis_index("fsdp")
    x_index = fsdp % 2
    place = jnp.stack([x_index, fsdp // 2]).astype(jnp.int32)

    meta = jnp.concatenate([expert_ids.astype(WIDE), gate_values.astype(WIDE)], axis=1).T
    turned = own_order(meta)
    meta = jnp.stack([meta, swap(meta, CORE), swap(turned, Y), swap(turned, CORE | Y)])
    w_view, v_view = tiled_view(w_in), tiled_view(w_out)
    x_near = swap(lax.dynamic_slice_in_dim(tokens, x_index * half, half, axis=0), Y)
    g_near = swap(lax.dynamic_slice_in_dim(cotangent, x_index * half, half, axis=0), Y)
    x_core, g_core = swap(tokens, CORE), swap(cotangent, CORE)
    ids, gates = meta[:, :top_count].astype(jnp.int32), meta[:, top_count:]
    blocks = ids.shape[0]
    names = first + jnp.arange(local_count, dtype=jnp.int32)
    named = ids[:, None] == names[None, :, None, None]
    hit = jnp.any(named, axis=2)
    gate_tok = jnp.sum(jnp.where(named, gates[:, None], 0.0), axis=2)
    earlier = jnp.tril(jnp.ones((tok_rows, tok_rows), WIDE), -1)
    position = jnp.einsum("tu,blu->blt", earlier, hit.astype(WIDE)).astype(jnp.int32)
    base = jnp.arange(blocks, dtype=jnp.int32)[:, None, None] * CAP
    order = jnp.arange(top_count, dtype=jnp.int32)[None, None, :, None]
    which = jnp.sum(jnp.where(named, order, 0), axis=2)
    code = jnp.where(hit, base + position, 1023) + 1024 * which

    def by_expert(value):
        return jnp.swapaxes(value, 0, 1).reshape(local_count, 1, blocks * tok_rows)

    code, gate_tok = by_expert(code), by_expert(gate_tok)
    w_sort, v_sort = sorter(8, 6, local_count), sorter(16, 4, local_count)
    w_split, flag = split_experts(w_view, w_sort, 256, 6, 8, [])
    (x_near,) = hold([x_near], [flag])
    x_far = swap(x_near, X)
    x_near_core = swap(x_near, CORE)
    v_split, flag = split_experts(v_view, v_sort, 64, 4, 16, [x_near])
    x_far, g_near = hold([x_far, g_near], [flag])
    g_far = swap(g_near, X)
    g_near_core = swap(g_near, CORE)
    x_far_core = swap(x_far, CORE)
    x_pieces = [tokens, x_core, x_near, x_far, x_near_core, x_far_core]
    xs, ag, active, slope = forward_tokens(code, gate_tok, x_pieces, w_split)
    g_far_core = swap(g_far, CORE)
    g_pieces = [cotangent, g_core, g_near, g_far, g_near_core, g_far_core]
    gs, gp, keep, send = forward_cotangents(code, active, slope, g_pieces, w_split, v_split)
    w_back, v_back = w_sort.T, v_sort.T
    width = keep.shape[1]

    def shape(rows, dtype, columns=width):
        return jax.ShapeDtypeStruct((rows, columns), dtype)

    def in_part(holder, number, after):
        rows = model_width // 4
        return outer(w_back, xs, gp, holder, number * rows, rows, 6, 8, after)

    def out_part(holder, number, after):
        rows = hidden // 3
        return outer(v_back, ag, gs, holder, number * rows, rows, 4, 16, after)

    got = swap(send, CORE)
    grad_in, flag = in_part(None, 0, [])
    mine, *sends = small_call(
        first_sum, place, [keep, got], [flag],
        [shape(half, WIDE)] + [shape(half, NARROW)] * 3, "first_sum", 56,
    )
    got = [swap(part, mask) for part, mask in zip(sends, (X, Y, X | Y))]
    grad_in, flag = in_part(grad_in, 1, [mine])
    grad_in, flag = in_part(grad_in, 2, [flag])
    grad_in, flag = in_part(grad_in, 3, [flag])
    mine, *sends = small_call(
        second_sum, place, [mine, *got], [flag],
        [shape(half // 4, WIDE)] + [shape(half // 4, NARROW)] * 3, "second_sum",
    )
    got = [swap(part, mask * Z) for part, mask in zip(sends, (1, 2, 3))]
    grad_out, flag = out_part(None, 0, [mine])
    (final,) = small_call(
        third_sum, place, [mine, *got], [flag], [shape(half // 4, NARROW)], "third_sum"
    )
    got = [swap(final, mask * Z) for mask in (1, 2, 3)]
    grad_out, flag = out_part(grad_out, 1, [final])
    (near,) = small_call(join_z, place, [final, *got], [flag], [shape(half, NARROW)], "join_z")
    far = swap(near, X)
    grad_out, flag = out_part(grad_out, 2, [near])
    grad_tokens, grad_gates = small_call(
        join_x, place, [near, far], [flag],
        [shape(tok_rows, NARROW, model_width), shape(tok_rows, NARROW, LANES)], "join_x",
    )
    grad_gates = grad_gates[:, :top_count]
    return (grad_tokens, grad_gates, stored_view(grad_in), stored_view(grad_out))


def local_general(tokens, cotangent, expert_ids, gate_values, w_in, w_out):
    tok_rows, model_width = tokens.shape
    local_count = w_in.shape[1]
    first = lax.axis_index("expert") * local_count
    gather = functools.partial(lax.all_gather, axis_name="expert", axis=0)
    ids, gates = gather(expert_ids), gather(gate_values).astype(WIDE)
    x_blocks, g_blocks = gather(tokens), gather(cotangent)
    blocks = ids.shape[0]
    names = first + jnp.arange(local_count, dtype=jnp.int32)
    named = ids[:, None] == names[None, :, None, None]
    hit = jnp.any(named, axis=3)
    gate_tok = jnp.sum(jnp.where(named, gates[:, None], 0.0), axis=3)
    earlier = jnp.tril(jnp.ones((tok_rows, tok_rows), WIDE), -1)
    position = jnp.einsum("tu,blu->blt", earlier, hit.astype(WIDE)).astype(jnp.int32)
    slots = jnp.arange(CAP, dtype=jnp.int32)
    choose = hit[:, :, None] & (position[:, :, None] == slots[None, None, :, None])
    pick = choose.astype(NARROW)
    slot_x = jnp.einsum("blst,btd->lbsd", pick, x_blocks, preferred_element_type=WIDE).astype(NARROW)
    slot_g = jnp.einsum("blst,btd->lbsd", pick, g_blocks, preferred_element_type=WIDE).astype(NARROW)
    gate_slot = jnp.sum(jnp.where(choose, gate_tok[:, :, None], 0.0), axis=3)
    rows = blocks * CAP
    slot_x = slot_x.reshape(local_count, rows, model_width)
    slot_g = slot_g.reshape(local_count, rows, model_width)
    gate_slot = jnp.swapaxes(gate_slot, 0, 1).reshape(local_count, rows, 1)
    pre_act = jnp.einsum("lrd,dlf->lrf", slot_x, w_in, preferred_element_type=WIDE)
    upstream = jnp.einsum("lrd,fld->lrf", slot_g, w_out, preferred_element_type=WIDE)
    squash = jax.nn.sigmoid(pre_act)
    active = pre_act * squash
    gate_part = jnp.sum(active * upstream, axis=-1)
    act_gated = (gate_slot * active).astype(NARROW)
    grad_pre = (gate_slot * squash * (1.0 + pre_act * (1.0 - squash)) * upstream).astype(NARROW)
    gate_part = jnp.swapaxes(gate_part.reshape(local_count, blocks, CAP), 0, 1)
    gate_tok = jnp.sum(jnp.where(choose, gate_part[..., None], 0.0), axis=2)
    gate_back = jnp.sum(jnp.where(named, gate_tok[..., None], 0.0), axis=1)
    part_x = jnp.einsum("lrf,dlf->lrd", grad_pre, w_in, preferred_element_type=WIDE)
    part_x = part_x.astype(NARROW).reshape(local_count, blocks, CAP, model_width)
    token_part = jnp.einsum("blst,lbsd->btd", pick, part_x, preferred_element_type=WIDE)
    scatter = functools.partial(lax.psum_scatter, axis_name="expert", scatter_dimension=0)
    grad_tokens = lax.psum(scatter(token_part), "fsdp").astype(NARROW)
    grad_gates = lax.psum(scatter(gate_back), "fsdp").astype(NARROW)
    grad_in = jnp.einsum("lrd,lrf->dlf", slot_x, grad_pre, preferred_element_type=WIDE).astype(NARROW)
    grad_out = jnp.einsum("lrf,lrd->fld", act_gated, slot_g, preferred_element_type=WIDE).astype(NARROW)
    return (grad_tokens, grad_gates, grad_in, grad_out)


def solution(mesh):
    return jax.shard_map(
        local,
        mesh=mesh,
        in_specs=(
            P("expert", None),
            P("expert", None),
            P("expert", None),
            P("expert", None),
            P(None, "expert", "fsdp"),
            P("fsdp", "expert", None),
        ),
        out_specs=(
            P("expert", None),
            P("expert", None),
            P(None, "expert", "fsdp"),
            P("fsdp", "expert", None),
        ),
        check_vma=False,
    )
```

```python
import functools
import jax
import jax.numpy as jnp
import numpy as np
from jax import lax
from jax.experimental import pallas as pl
from jax.experimental.pallas import tpu as pltpu
from jax.sharding import PartitionSpec as P

EXPERTS = 16
CAP = 40
AXES = ("fsdp", "expert")
CORE, Y, X, Z = 1, 2, 4, 8
LANES = 128
NARROW, WIDE = jnp.bfloat16, jnp.float32
MIB = 1 << 20
TN = (((0,), (0,)), ((), ()))
NT = (((1,), (1,)), ((), ()))
NN = (((1,), (0,)), ((), ()))


def mm(a, b, dims):
    return lax.dot_general(a, b, dims, preferred_element_type=WIDE)


def swap(value, mask):
    size = lax.axis_size("fsdp") * lax.axis_size("expert")
    return lax.ppermute(value, AXES, [(i, i ^ mask) for i in range(size)])


def is_small():
    return lax.axis_size("fsdp") == 8 and lax.axis_size("expert") == 4


def own_order(rows):
    x_index = lax.axis_index("fsdp") % 2
    half = rows.shape[-1] // 2
    return jnp.where(
        x_index == 0, rows, jnp.concatenate([rows[..., half:], rows[..., :half]], axis=-1)
    )


ANY = pl.BlockSpec(memory_space=pl.ANY)
FLAG = jax.ShapeDtypeStruct((8, LANES), WIDE)


def small_call(body, place, inputs, after, outs, name, grant=12, steps=1):
    given = len(inputs)

    def run(place_ref, *refs):
        body(place_ref, refs[:given], refs[given + len(after) :])

    def whole(array):
        rows, columns = array.shape
        return pl.BlockSpec((rows, columns // steps), lambda i: (0, i))

    return pl.pallas_call(
        run,
        out_shape=outs,
        grid=(steps,),
        in_specs=[pl.BlockSpec(memory_space=pltpu.SMEM)]
        + [whole(array) for array in inputs]
        + [ANY] * len(after),
        out_specs=[whole(out) for out in outs],
        compiler_params=pltpu.CompilerParams(vmem_limit_bytes=grant * MIB),
        cost_estimate=pl.CostEstimate(flops=0, bytes_accessed=1 << 20, transcendentals=0),
        name=name,
    )(place, *inputs, *after)


def hold(arrays, after):
    count = len(arrays)
    return pl.pallas_call(
        lambda *refs: None,
        out_shape=[jax.ShapeDtypeStruct(array.shape, array.dtype) for array in arrays],
        in_specs=[ANY] * (count + len(after)),
        out_specs=[ANY] * count,
        input_output_aliases={number: number for number in range(count)},
        cost_estimate=pl.CostEstimate(flops=0, bytes_accessed=1 << 18, transcendentals=0),
        name="hold",
    )(*arrays, *after)


def at(index, size):
    return pl.ds(pl.multiple_of(index * size, size), size)


def first_sum(place_ref, ins, outs):
    keep_ref, got_ref = ins
    mine_ref, x_ref, y_ref, xy_ref = outs
    half = mine_ref.shape[0]
    x_index = place_ref[0]

    def total(rows):
        return keep_ref[rows, :] + got_ref[rows, :].astype(WIDE)

    mine_ref[...] = total(at(x_index, half))
    x_ref[...] = total(at(1 - x_index, half)).astype(NARROW)
    y_ref[...] = total(slice(2 * half, 3 * half)).astype(NARROW)
    xy_ref[...] = total(slice(3 * half, 4 * half)).astype(NARROW)


def second_sum(place_ref, ins, outs):
    mine_ref, x_ref, y_ref, xy_ref = ins
    quarter = outs[0].shape[0]
    z_index = place_ref[1]
    for step in range(4):
        rows = at(z_index ^ step, quarter)
        total = mine_ref[rows, :] + x_ref[rows, :].astype(WIDE)
        total = total + (y_ref[rows, :].astype(WIDE) + xy_ref[rows, :].astype(WIDE))
        outs[step][...] = total.astype(outs[step].dtype)


def third_sum(place_ref, ins, outs):
    total = ins[0][...]
    for got in ins[1:]:
        total = total + got[...].astype(WIDE)
    outs[0][...] = total.astype(NARROW)


def join_z(place_ref, ins, outs):
    quarter = ins[0].shape[0]
    for step in range(4):
        outs[0][at(place_ref[1] ^ step, quarter), :] = ins[step][...]


def join_x(place_ref, ins, outs):
    half = ins[0].shape[0]
    model_width = outs[0].shape[1]
    for step in range(2):
        rows = at(place_ref[0] ^ step, half)
        outs[0][rows, :] = ins[step][:, :model_width]
        outs[1][rows, :] = ins[step][:, model_width:]


def sorter(rows, tiles, experts):
    size = rows * tiles * experts
    order = np.arange(size).reshape(rows, tiles, experts).transpose(2, 1, 0).reshape(-1)
    return jnp.asarray(np.eye(size, dtype=np.float32)[order], NARROW)


def tiled_view(weight):
    rows, experts, columns = weight.shape
    return weight.reshape(rows, experts, columns // LANES, LANES).transpose(0, 2, 1, 3)


def staged(stages, outs, sem, compute):
    step, steps = pl.program_id(0), pl.num_programs(0)

    def copies(slot, at_step):
        return [
            pltpu.make_async_copy(source, target, sem.at[slot, number])
            for number, (source, target) in enumerate(outs(stages[slot], at_step))
        ]

    for slot in range(2):

        @pl.when(lax.rem(step, 2) == slot)
        def _():
            @pl.when(step >= 2)
            def _():
                for copy in copies(slot, step - 2):
                    copy.wait()

            compute(stages[slot])
            for copy in copies(slot, step):
                copy.start()

            @pl.when(step == steps - 1)
            def _():
                @pl.when(step >= 1)
                def _():
                    for copy in copies(1 - slot, step - 1):
                        copy.wait()

                for copy in copies(slot, step):
                    copy.wait()


def split_block(group, some, sort_ref, w_ref, out_ref, base):
    rows, tiles, experts, _ = w_ref.shape
    held = group * experts
    flat = w_ref.reshape(rows, tiles * experts, LANES)
    places = [(row, tile) for row in range(0, rows, some) for tile in range(0, tiles, group)]
    for pair in zip(places[::2], places[1::2]):
        blocks = [
            flat[row : row + some, tile * experts : tile * experts + held, :].reshape(
                some * held, LANES
            )
            for row, tile in pair
        ]
        result = mm(sort_ref[...], jnp.concatenate(blocks, axis=1), NN)
        for expert in range(experts):
            for tile in range(group):
                begin = (expert * group + tile) * some
                parts = [
                    result[begin : begin + some, side * LANES : (side + 1) * LANES]
                    for side in range(2)
                ]
                if some == 8:
                    row, first = base + pair[0][0], pair[0][1] + tile
                    out_ref[expert, row : row + 16, first * LANES : (first + 1) * LANES] = (
                        jnp.concatenate(parts, axis=0).astype(NARROW)
                    )
                else:
                    for (row, first), part in zip(pair, parts):
                        column = (first + tile) * LANES
                        out_ref[
                            expert, base + row : base + row + some, column : column + LANES
                        ] = part.astype(NARROW)


def split_experts(view, sort, block, group, some, after):
    rows, tiles, experts, _ = view.shape
    columns = tiles * LANES
    streams = 4
    part = block // streams

    def body(sort_ref, *refs):
        out_ref, flag_ref, low, high, sem = refs[-5:]
        flag_ref[...] = jnp.zeros_like(flag_ref)

        def outs(stage, step):
            into = pl.ds(pl.multiple_of(step * block, block), block)
            return [(stage.at[expert], out_ref.at[expert, into]) for expert in range(experts)]

        def compute(stage):
            for number in range(streams):
                split_block(group, some, sort_ref, refs[number], stage, number * part)

        staged((low, high), outs, sem, compute)

    def piece(number):
        return pl.BlockSpec(
            (part, tiles, experts, LANES), lambda i: (i * streams + number, 0, 0, 0)
        )

    return pl.pallas_call(
        body,
        out_shape=[jax.ShapeDtypeStruct((experts, rows, columns), NARROW), FLAG],
        grid=(rows // block,),
        in_specs=[
            pl.BlockSpec(sort.shape, lambda i: (0, 0)),
            *[piece(number) for number in range(streams)],
            *[ANY] * len(after),
        ],
        out_specs=[ANY, pl.BlockSpec(FLAG.shape, lambda i: (0, 0))],
        scratch_shapes=[
            pltpu.VMEM((experts, block, columns), NARROW),
            pltpu.VMEM((experts, block, columns), NARROW),
            pltpu.SemaphoreType.DMA((2, experts)),
        ],
        compiler_params=pltpu.CompilerParams(vmem_limit_bytes=56 * MIB),
        cost_estimate=pl.CostEstimate(
            flops=0, bytes_accessed=4 * experts * rows * columns, transcendentals=0
        ),
        name="split_experts",
    )(sort, *[view] * streams, *after)


def fetch(pieces, whole, sem):
    copies, begin = [], 0
    for number, piece in enumerate(pieces):
        count = piece.shape[0]
        copies.append(
            pltpu.make_async_copy(piece, whole.at[begin : begin + count], sem.at[number])
        )
        begin += count
    for copy in copies:
        copy.start()
    for copy in copies:
        copy.wait()


def chosen(code_ref, slots):
    code = code_ref[0]
    tokens = code.shape[1]
    return lax.broadcasted_iota(jnp.int32, (slots, tokens), 0) == jnp.bitwise_and(code, 1023)


def weight_parts(weights, streams):
    _, rows, columns = weights.shape
    specs = [
        pl.BlockSpec((1, rows // streams, columns), lambda i, number=number: (i, number, 0))
        for number in range(streams)
    ]
    return specs, [weights] * streams


def forward_tokens_body(code_ref, gate_ref, *refs):
    w_refs, refs = refs[:4], refs[4:]
    pieces, (xs_ref, ag_ref, active_ref, slope_ref, x_ref, sem) = refs[:-6], refs[-6:]
    slots, model_width = xs_ref.shape[1:]
    columns = 512
    pl.when(pl.program_id(0) == 0)(lambda: fetch(pieces, x_ref, sem))
    choose = chosen(code_ref, slots)
    pick = choose.astype(WIDE).astype(NARROW)
    gate = jnp.sum(jnp.where(choose, gate_ref[0], 0.0), axis=1, keepdims=True)
    for begin in range(0, model_width, columns):
        part = slice(begin, begin + columns)
        xs_ref[0, :, part] = mm(pick, x_ref[:, part], NN).astype(NARROW)
    pre_act, begin = 0.0, 0
    for w_ref in w_refs:
        end = begin + w_ref.shape[1]
        pre_act = pre_act + mm(xs_ref[0, :, begin:end], w_ref[0], NN)
        begin = end
    squash = jax.nn.sigmoid(pre_act)
    active = pre_act * squash
    active_ref[0] = active
    ag_ref[0] = (gate * active).astype(NARROW)
    slope_ref[0] = gate * squash * (1.0 + pre_act * (1.0 - squash))


def forward_tokens(code, gate_tok, x_pieces, w_split):
    experts, model_width, hidden = w_split.shape
    tokens = code.shape[2]
    slots = tokens // 128 * CAP
    expert = lambda i: (i, 0, 0)
    w_specs, w_operands = weight_parts(w_split, 4)
    shapes = [(model_width, NARROW), (hidden, NARROW), (hidden, WIDE), (hidden, WIDE)]
    return pl.pallas_call(
        forward_tokens_body,
        out_shape=[jax.ShapeDtypeStruct((experts, slots, width), dtype) for width, dtype in shapes],
        grid=(experts,),
        in_specs=[
            pl.BlockSpec((1, 1, tokens), expert),
            pl.BlockSpec((1, 1, tokens), expert),
            *w_specs,
            *[ANY] * len(x_pieces),
        ],
        out_specs=[pl.BlockSpec((1, slots, width), expert) for width, _ in shapes],
        scratch_shapes=[
            pltpu.VMEM((tokens, model_width), NARROW),
            pltpu.SemaphoreType.DMA((len(x_pieces),)),
        ],
        compiler_params=pltpu.CompilerParams(vmem_limit_bytes=56 * MIB),
        cost_estimate=pl.CostEstimate(
            flops=2 * slots * experts * model_width * (hidden + tokens),
            bytes_accessed=2 * experts * model_width * hidden,
            transcendentals=0,
        ),
        name="forward_tokens",
    )(code, gate_tok, *w_operands, *x_pieces)


def forward_cotangents_body(code_ref, active_ref, slope_ref, *refs):
    w_refs, v_refs, refs = refs[:3], refs[3:6], refs[6:]
    pieces = refs[:-8]
    gs_ref, gp_ref, keep_ref, send_ref, g_ref, back_ref, pick_ref, sem = refs[-8:]
    step = pl.program_id(0)
    slots, model_width = gs_ref.shape[1:]
    columns = 512
    pl.when(step == 0)(lambda: fetch(pieces, g_ref, sem))
    choose = chosen(code_ref, slots)
    pick = choose.astype(WIDE).astype(NARROW)
    rows = pl.ds(pl.multiple_of(step * slots, slots), slots)
    pick_ref[rows, :] = pick
    for begin in range(0, model_width, columns):
        part = slice(begin, begin + columns)
        gs_ref[0, :, part] = mm(pick, g_ref[:, part], NN).astype(NARROW)
    gate_part, begin = 0.0, 0
    for v_ref in v_refs:
        part = slice(begin, begin + v_ref.shape[1])
        upstream = mm(gs_ref[0], v_ref[0], NT)
        gate_part = gate_part + jnp.sum(active_ref[0, :, part] * upstream, axis=1, keepdims=True)
        gp_ref[0, :, part] = (slope_ref[0, :, part] * upstream).astype(NARROW)
        begin = part.stop
    for begin in range(0, model_width, columns):
        held = w_refs[0].shape[1]
        w_ref, inner = w_refs[begin // held], begin % held
        back = mm(gp_ref[0], w_ref[0, inner : inner + columns, :], NT)
        back_ref[rows, begin : begin + columns] = back.astype(NARROW)
    which = jnp.sum(
        jnp.where(choose, jnp.right_shift(code_ref[0], 10), 0), axis=1, keepdims=True
    )
    lane = lax.broadcasted_iota(jnp.int32, (slots, LANES), 1)
    high = gate_part.astype(NARROW).astype(WIDE)
    gates = jnp.where(lane == which, high, 0.0)
    gates = jnp.where(lane == which + LANES // 2, gate_part - high, gates)
    back_ref[rows, model_width:] = gates.astype(NARROW)

    @pl.when(step == pl.num_programs(0) - 1)
    def _():
        quarter = g_ref.shape[0] // 4
        for begin in range(0, model_width + LANES, columns):
            part = slice(begin, min(begin + columns, model_width + LANES))
            summed = mm(pick_ref[...], back_ref[:, part], TN)
            if begin == model_width:
                summed = summed + pltpu.roll(summed, LANES // 2, 1)
            for pair in range(2):
                lower = 2 * pair * quarter
                into = slice(pair * quarter, (pair + 1) * quarter)
                keep_ref[into, part] = summed[lower : lower + quarter]
                send_ref[into, part] = summed[lower + quarter : lower + 2 * quarter].astype(NARROW)


def forward_cotangents(code, active, slope, g_pieces, w_split, v_split):
    experts, model_width, hidden = w_split.shape
    tokens = code.shape[2]
    slots = tokens // 128 * CAP
    width = model_width + LANES
    expert = lambda i: (i, 0, 0)
    whole = lambda i: (0, 0)
    one = pl.Buffered(1)
    w_specs, w_operands = weight_parts(w_split, 3)
    v_specs, v_operands = weight_parts(v_split, 3)
    return pl.pallas_call(
        forward_cotangents_body,
        out_shape=[
            jax.ShapeDtypeStruct((experts, slots, model_width), NARROW),
            jax.ShapeDtypeStruct((experts, slots, hidden), NARROW),
            jax.ShapeDtypeStruct((tokens // 2, width), WIDE),
            jax.ShapeDtypeStruct((tokens // 2, width), NARROW),
        ],
        grid=(experts,),
        in_specs=[
            pl.BlockSpec((1, 1, tokens), expert),
            pl.BlockSpec((1, slots, hidden), expert),
            pl.BlockSpec((1, slots, hidden), expert),
            *w_specs,
            *v_specs,
            *[ANY] * len(g_pieces),
        ],
        out_specs=[
            pl.BlockSpec((1, slots, model_width), expert),
            pl.BlockSpec((1, slots, hidden), expert),
            pl.BlockSpec((tokens // 2, width), whole, pipeline_mode=one),
            pl.BlockSpec((tokens // 2, width), whole, pipeline_mode=one),
        ],
        scratch_shapes=[
            pltpu.VMEM((tokens, model_width), NARROW),
            pltpu.VMEM((experts * slots, width), NARROW),
            pltpu.VMEM((experts * slots, tokens), NARROW),
            pltpu.SemaphoreType.DMA((len(g_pieces),)),
        ],
        compiler_params=pltpu.CompilerParams(vmem_limit_bytes=56 * MIB),
        cost_estimate=pl.CostEstimate(
            flops=2 * slots * experts * model_width * (2 * hidden + 2 * tokens),
            bytes_accessed=4 * experts * model_width * hidden,
            transcendentals=0,
        ),
        name="forward_cotangents",
    )(code, active, slope, *w_operands, *v_operands, *g_pieces)


def odd_tiles(rows):
    tiles = -(-rows // 8)
    return 8 * (tiles + 1 - tiles % 2)


def outer_block(group, a_ref, b_ref, out_ref, wide_ref):
    rows, tiles, experts, _ = out_ref.shape
    stride = wide_ref.shape[1]
    held = group * experts
    out = out_ref.reshape(rows, tiles * experts, LANES)
    flat = wide_ref.reshape(rows * stride, LANES)
    for begin in range(0, tiles, group):
        for expert in range(experts):
            part = mm(a_ref[expert], b_ref[expert, :, begin * LANES : (begin + group) * LANES], TN)
            for tile in range(group):
                flat[pl.ds(tile * experts + expert, rows, stride), :] = part[
                    :, tile * LANES : (tile + 1) * LANES
                ]
        out[:, begin * experts : begin * experts + held, :] = wide_ref[:, :held, :].astype(NARROW)


def outer(a, b, holder, start, count, group, after):
    experts, slots, total = a.shape
    columns = b.shape[2]
    tiles = columns // LANES
    block, streams = 128, 4
    first = start // block
    part = block // streams
    extra = list(after) if holder is None else [holder, *after]

    def body(a_ref, b_ref, *refs):
        out_ref, flag_ref, wide_ref, low, high, sem = refs[-6:]
        flag_ref[...] = jnp.zeros_like(flag_ref)

        def outs(stage, step):
            return [
                (
                    stage.at[number * part : (number + 1) * part],
                    out_ref.at[pl.ds(start + step * block + number * part, part)],
                )
                for number in range(streams)
            ]

        staged(
            (low, high), outs, sem, lambda stage: outer_block(group, a_ref, b_ref, stage, wide_ref)
        )

    return pl.pallas_call(
        body,
        out_shape=[jax.ShapeDtypeStruct((total, tiles, experts, LANES), NARROW), FLAG],
        grid=(count // block,),
        in_specs=[
            pl.BlockSpec((experts, slots, block), lambda i: (0, 0, first + i)),
            pl.BlockSpec(
                (experts, slots, columns), lambda i: (0, 0, 0), pipeline_mode=pl.Buffered(1)
            ),
            *[ANY] * len(extra),
        ],
        out_specs=[ANY, pl.BlockSpec(FLAG.shape, lambda i: (0, 0))],
        scratch_shapes=[
            pltpu.VMEM((block, odd_tiles(group * experts), LANES), WIDE),
            pltpu.VMEM((block, tiles, experts, LANES), NARROW),
            pltpu.VMEM((block, tiles, experts, LANES), NARROW),
            pltpu.SemaphoreType.DMA((2, streams)),
        ],
        input_output_aliases={} if holder is None else {2: 0},
        compiler_params=pltpu.CompilerParams(vmem_limit_bytes=56 * MIB),
        cost_estimate=pl.CostEstimate(
            flops=2 * experts * slots * count * columns,
            bytes_accessed=4 * experts * count * columns,
            transcendentals=0,
        ),
        name="weight_gradient",
    )(a, b, *extra)


def stored_view(tiled):
    rows, tiles, experts, _ = tiled.shape
    return tiled.transpose(0, 2, 1, 3).reshape(rows, experts, tiles * LANES)


def local(tokens, cotangent, expert_ids, gate_values, w_in, w_out):
    if not is_small():
        return local_general(tokens, cotangent, expert_ids, gate_values, w_in, w_out)
    tok_rows, model_width = tokens.shape
    top_count = expert_ids.shape[1]
    local_count = w_in.shape[1]
    hidden = w_in.shape[2]
    half = tok_rows // 2
    first = lax.axis_index("expert") * local_count
    fsdp = lax.axis_index("fsdp")
    x_index = fsdp % 2
    place = jnp.stack([x_index, fsdp // 2]).astype(jnp.int32)

    meta = jnp.concatenate([expert_ids.astype(WIDE), gate_values.astype(WIDE)], axis=1).T
    turned = own_order(meta)
    meta = jnp.stack([meta, swap(meta, CORE), swap(turned, Y), swap(turned, CORE | Y)])
    w_view, v_view = tiled_view(w_in), tiled_view(w_out)
    x_near = swap(lax.dynamic_slice_in_dim(tokens, x_index * half, half, axis=0), Y)
    g_near = swap(lax.dynamic_slice_in_dim(cotangent, x_index * half, half, axis=0), Y)
    x_core, g_core = swap(tokens, CORE), swap(cotangent, CORE)
    ids, gates = meta[:, :top_count].astype(jnp.int32), meta[:, top_count:]
    blocks = ids.shape[0]
    names = first + jnp.arange(local_count, dtype=jnp.int32)
    named = ids[:, None] == names[None, :, None, None]
    hit = jnp.any(named, axis=2)
    gate_tok = jnp.sum(jnp.where(named, gates[:, None], 0.0), axis=2)
    earlier = jnp.tril(jnp.ones((tok_rows, tok_rows), WIDE), -1)
    position = jnp.einsum("tu,blu->blt", earlier, hit.astype(WIDE)).astype(jnp.int32)
    base = jnp.arange(blocks, dtype=jnp.int32)[:, None, None] * CAP
    order = jnp.arange(top_count, dtype=jnp.int32)[None, None, :, None]
    which = jnp.sum(jnp.where(named, order, 0), axis=2)
    code = jnp.where(hit, base + position, 1023) + 1024 * which

    def by_expert(value):
        return jnp.swapaxes(value, 0, 1).reshape(local_count, 1, blocks * tok_rows)

    code, gate_tok = by_expert(code), by_expert(gate_tok)
    w_sort, v_sort = sorter(8, 6, local_count), sorter(16, 4, local_count)
    w_split, flag = split_experts(w_view, w_sort, 256, 6, 8, [])
    (x_near,) = hold([x_near], [flag])
    x_far = swap(x_near, X)
    x_near_core = swap(x_near, CORE)
    v_split, flag = split_experts(v_view, v_sort, 64, 4, 16, [x_near])
    x_far, g_near = hold([x_far, g_near], [flag])
    g_far = swap(g_near, X)
    g_near_core = swap(g_near, CORE)
    x_far_core = swap(x_far, CORE)
    x_pieces = [tokens, x_core, x_near, x_far, x_near_core, x_far_core]
    xs, ag, active, slope = forward_tokens(code, gate_tok, x_pieces, w_split)
    g_far_core = swap(g_far, CORE)
    g_pieces = [cotangent, g_core, g_near, g_far, g_near_core, g_far_core]
    gs, gp, keep, send = forward_cotangents(code, active, slope, g_pieces, w_split, v_split)
    width = keep.shape[1]

    def shape(rows, dtype, columns=width):
        return jax.ShapeDtypeStruct((rows, columns), dtype)

    def in_part(holder, number, after):
        rows = model_width // 4
        return outer(xs, gp, holder, number * rows, rows, 6, after)

    def out_part(holder, number, after):
        rows = hidden // 3
        return outer(ag, gs, holder, number * rows, rows, 8, after)

    got = swap(send, CORE)
    grad_in, flag = in_part(None, 0, [])
    mine, *sends = small_call(
        first_sum, place, [keep, got], [flag],
        [shape(half, WIDE)] + [shape(half, NARROW)] * 3, "first_sum", 56, 5,
    )
    got = [swap(part, mask) for part, mask in zip(sends, (X, Y, X | Y))]
    grad_in, flag = in_part(grad_in, 1, [mine])
    grad_in, flag = in_part(grad_in, 2, [flag])
    grad_in, flag = in_part(grad_in, 3, [flag])
    mine, *sends = small_call(
        second_sum, place, [mine, *got], [flag],
        [shape(half // 4, WIDE)] + [shape(half // 4, NARROW)] * 3, "second_sum",
    )
    got = [swap(part, mask * Z) for part, mask in zip(sends, (1, 2, 3))]
    grad_out, flag = out_part(None, 0, [mine])
    (final,) = small_call(
        third_sum, place, [mine, *got], [flag], [shape(half // 4, NARROW)], "third_sum"
    )
    got = [swap(final, mask * Z) for mask in (1, 2, 3)]
    grad_out, flag = out_part(grad_out, 1, [final])
    (near,) = small_call(join_z, place, [final, *got], [flag], [shape(half, NARROW)], "join_z")
    far = swap(near, X)
    grad_out, flag = out_part(grad_out, 2, [near])
    grad_tokens, grad_gates = small_call(
        join_x, place, [near, far], [flag],
        [shape(tok_rows, NARROW, model_width), shape(tok_rows, NARROW, LANES)], "join_x",
    )
    grad_gates = grad_gates[:, :top_count]
    return (grad_tokens, grad_gates, stored_view(grad_in), stored_view(grad_out))


def local_general(tokens, cotangent, expert_ids, gate_values, w_in, w_out):
    tok_rows, model_width = tokens.shape
    local_count = w_in.shape[1]
    first = lax.axis_index("expert") * local_count
    gather = functools.partial(lax.all_gather, axis_name="expert", axis=0)
    ids, gates = gather(expert_ids), gather(gate_values).astype(WIDE)
    x_blocks, g_blocks = gather(tokens), gather(cotangent)
    blocks = ids.shape[0]
    names = first + jnp.arange(local_count, dtype=jnp.int32)
    named = ids[:, None] == names[None, :, None, None]
    hit = jnp.any(named, axis=3)
    gate_tok = jnp.sum(jnp.where(named, gates[:, None], 0.0), axis=3)
    earlier = jnp.tril(jnp.ones((tok_rows, tok_rows), WIDE), -1)
    position = jnp.einsum("tu,blu->blt", earlier, hit.astype(WIDE)).astype(jnp.int32)
    slots = jnp.arange(CAP, dtype=jnp.int32)
    choose = hit[:, :, None] & (position[:, :, None] == slots[None, None, :, None])
    pick = choose.astype(NARROW)
    slot_x = jnp.einsum("blst,btd->lbsd", pick, x_blocks, preferred_element_type=WIDE).astype(NARROW)
    slot_g = jnp.einsum("blst,btd->lbsd", pick, g_blocks, preferred_element_type=WIDE).astype(NARROW)
    gate_slot = jnp.sum(jnp.where(choose, gate_tok[:, :, None], 0.0), axis=3)
    rows = blocks * CAP
    slot_x = slot_x.reshape(local_count, rows, model_width)
    slot_g = slot_g.reshape(local_count, rows, model_width)
    gate_slot = jnp.swapaxes(gate_slot, 0, 1).reshape(local_count, rows, 1)
    pre_act = jnp.einsum("lrd,dlf->lrf", slot_x, w_in, preferred_element_type=WIDE)
    upstream = jnp.einsum("lrd,fld->lrf", slot_g, w_out, preferred_element_type=WIDE)
    squash = jax.nn.sigmoid(pre_act)
    active = pre_act * squash
    gate_part = jnp.sum(active * upstream, axis=-1)
    act_gated = (gate_slot * active).astype(NARROW)
    grad_pre = (gate_slot * squash * (1.0 + pre_act * (1.0 - squash)) * upstream).astype(NARROW)
    gate_part = jnp.swapaxes(gate_part.reshape(local_count, blocks, CAP), 0, 1)
    gate_tok = jnp.sum(jnp.where(choose, gate_part[..., None], 0.0), axis=2)
    gate_back = jnp.sum(jnp.where(named, gate_tok[..., None], 0.0), axis=1)
    part_x = jnp.einsum("lrf,dlf->lrd", grad_pre, w_in, preferred_element_type=WIDE)
    part_x = part_x.astype(NARROW).reshape(local_count, blocks, CAP, model_width)
    token_part = jnp.einsum("blst,lbsd->btd", pick, part_x, preferred_element_type=WIDE)
    scatter = functools.partial(lax.psum_scatter, axis_name="expert", scatter_dimension=0)
    grad_tokens = lax.psum(scatter(token_part), "fsdp").astype(NARROW)
    grad_gates = lax.psum(scatter(gate_back), "fsdp").astype(NARROW)
    grad_in = jnp.einsum("lrd,lrf->dlf", slot_x, grad_pre, preferred_element_type=WIDE).astype(NARROW)
    grad_out = jnp.einsum("lrf,lrd->fld", act_gated, slot_g, preferred_element_type=WIDE).astype(NARROW)
    return (grad_tokens, grad_gates, grad_in, grad_out)


def solution(mesh):
    return jax.shard_map(
        local,
        mesh=mesh,
        in_specs=(
            P("expert", None),
            P("expert", None),
            P("expert", None),
            P("expert", None),
            P(None, "expert", "fsdp"),
            P("fsdp", "expert", None),
        ),
        out_specs=(
            P("expert", None),
            P("expert", None),
            P(None, "expert", "fsdp"),
            P("fsdp", "expert", None),
        ),
        check_vma=False,
    )
```

```python
import functools
import jax
import jax.numpy as jnp
import numpy as np
from jax import lax
from jax.experimental import pallas as pl
from jax.experimental.pallas import tpu as pltpu
from jax.sharding import PartitionSpec as P

EXPERTS = 16
CAP = 40
AXES = ("fsdp", "expert")
CORE, Y, X, Z = 1, 2, 4, 8
LANES = 128
NARROW, WIDE = jnp.bfloat16, jnp.float32
MIB = 1 << 20
TN = (((0,), (0,)), ((), ()))
NT = (((1,), (1,)), ((), ()))
NN = (((1,), (0,)), ((), ()))


def mm(a, b, dims):
    return lax.dot_general(a, b, dims, preferred_element_type=WIDE)


def swap(value, mask):
    size = lax.axis_size("fsdp") * lax.axis_size("expert")
    return lax.ppermute(value, AXES, [(i, i ^ mask) for i in range(size)])


def is_small():
    return lax.axis_size("fsdp") == 8 and lax.axis_size("expert") == 4


def own_order(rows):
    x_index = lax.axis_index("fsdp") % 2
    half = rows.shape[-1] // 2
    return jnp.where(
        x_index == 0, rows, jnp.concatenate([rows[..., half:], rows[..., :half]], axis=-1)
    )


ANY = pl.BlockSpec(memory_space=pl.ANY)
FLAG = jax.ShapeDtypeStruct((8, LANES), WIDE)


def small_call(body, place, inputs, after, outs, name, grant=12, steps=1):
    given = len(inputs)

    def run(place_ref, *refs):
        body(place_ref, refs[:given], refs[given + len(after) :])

    def whole(array):
        rows, columns = array.shape
        return pl.BlockSpec((rows, columns // steps), lambda i: (0, i))

    return pl.pallas_call(
        run,
        out_shape=outs,
        grid=(steps,),
        in_specs=[pl.BlockSpec(memory_space=pltpu.SMEM)]
        + [whole(array) for array in inputs]
        + [ANY] * len(after),
        out_specs=[whole(out) for out in outs],
        compiler_params=pltpu.CompilerParams(vmem_limit_bytes=grant * MIB),
        cost_estimate=pl.CostEstimate(flops=0, bytes_accessed=1 << 20, transcendentals=0),
        name=name,
    )(place, *inputs, *after)


def hold(arrays, after):
    count = len(arrays)
    return pl.pallas_call(
        lambda *refs: None,
        out_shape=[jax.ShapeDtypeStruct(array.shape, array.dtype) for array in arrays],
        in_specs=[ANY] * (count + len(after)),
        out_specs=[ANY] * count,
        input_output_aliases={number: number for number in range(count)},
        cost_estimate=pl.CostEstimate(flops=0, bytes_accessed=1 << 18, transcendentals=0),
        name="hold",
    )(*arrays, *after)


def at(index, size):
    return pl.ds(pl.multiple_of(index * size, size), size)


def first_sum(place_ref, ins, outs):
    keep_ref, got_ref = ins
    mine_ref, x_ref, y_ref, xy_ref = outs
    half = mine_ref.shape[0]
    x_index = place_ref[0]

    def total(rows):
        return keep_ref[rows, :] + got_ref[rows, :].astype(WIDE)

    mine_ref[...] = total(at(x_index, half))
    x_ref[...] = total(at(1 - x_index, half)).astype(NARROW)
    y_ref[...] = total(slice(2 * half, 3 * half)).astype(NARROW)
    xy_ref[...] = total(slice(3 * half, 4 * half)).astype(NARROW)


def second_sum(place_ref, ins, outs):
    mine_ref, x_ref, y_ref, xy_ref = ins
    quarter = outs[0].shape[0]
    z_index = place_ref[1]
    for step in range(4):
        rows = at(z_index ^ step, quarter)
        total = mine_ref[rows, :] + x_ref[rows, :].astype(WIDE)
        total = total + (y_ref[rows, :].astype(WIDE) + xy_ref[rows, :].astype(WIDE))
        outs[step][...] = total.astype(outs[step].dtype)


def third_sum(place_ref, ins, outs):
    total = ins[0][...]
    for got in ins[1:]:
        total = total + got[...].astype(WIDE)
    outs[0][...] = total.astype(NARROW)


def join_z(place_ref, ins, outs):
    quarter = ins[0].shape[0]
    for step in range(4):
        outs[0][at(place_ref[1] ^ step, quarter), :] = ins[step][...]


def join_x(place_ref, ins, outs):
    half = ins[0].shape[0]
    model_width = outs[0].shape[1]
    for step in range(2):
        rows = at(place_ref[0] ^ step, half)
        outs[0][rows, :] = ins[step][:, :model_width]
        outs[1][rows, :] = ins[step][:, model_width:]


def sorter(rows, tiles, experts):
    size = rows * tiles * experts
    order = np.arange(size).reshape(rows, tiles, experts).transpose(2, 1, 0).reshape(-1)
    return jnp.asarray(np.eye(size, dtype=np.float32)[order], NARROW)


def tiled_view(weight):
    rows, experts, columns = weight.shape
    return weight.reshape(rows, experts, columns // LANES, LANES).transpose(0, 2, 1, 3)


def split_body(group, some, sort_ref, w_ref, *refs):
    out_ref, flag_ref = refs[-2:]
    flag_ref[...] = jnp.zeros_like(flag_ref)
    rows, tiles, experts, _ = w_ref.shape
    held = group * experts
    flat = w_ref.reshape(rows, tiles * experts, LANES)
    places = [(row, tile) for row in range(0, rows, some) for tile in range(0, tiles, group)]
    for pair in zip(places[::2], places[1::2]):
        blocks = [
            flat[row : row + some, tile * experts : tile * experts + held, :].reshape(
                some * held, LANES
            )
            for row, tile in pair
        ]
        result = mm(sort_ref[...], jnp.concatenate(blocks, axis=1), NN)
        for expert in range(experts):
            for tile in range(group):
                begin = (expert * group + tile) * some
                parts = [
                    result[begin : begin + some, side * LANES : (side + 1) * LANES]
                    for side in range(2)
                ]
                if some == 8:
                    row, first = pair[0][0], pair[0][1] + tile
                    out_ref[expert, row : row + 16, first * LANES : (first + 1) * LANES] = (
                        jnp.concatenate(parts, axis=0).astype(NARROW)
                    )
                else:
                    for (row, first), part in zip(pair, parts):
                        column = (first + tile) * LANES
                        out_ref[expert, row : row + some, column : column + LANES] = part.astype(
                            NARROW
                        )


def split_experts(view, sort, start, rows, block, group, some, after):
    _, tiles, experts, _ = view.shape
    columns = tiles * LANES
    first = start // block
    return pl.pallas_call(
        functools.partial(split_body, group, some),
        out_shape=[jax.ShapeDtypeStruct((experts, rows, columns), NARROW), FLAG],
        grid=(rows // block,),
        in_specs=[
            pl.BlockSpec(sort.shape, lambda i: (0, 0)),
            pl.BlockSpec((block, tiles, experts, LANES), lambda i: (first + i, 0, 0, 0)),
            *[ANY] * len(after),
        ],
        out_specs=[
            pl.BlockSpec((experts, block, columns), lambda i: (0, i, 0)),
            pl.BlockSpec(FLAG.shape, lambda i: (0, 0)),
        ],
        compiler_params=pltpu.CompilerParams(vmem_limit_bytes=56 * MIB),
        cost_estimate=pl.CostEstimate(
            flops=0, bytes_accessed=4 * experts * rows * columns, transcendentals=0
        ),
        name="split_experts",
    )(sort, view, *after)


def fetch(pieces, whole, sem):
    copies, begin = [], 0
    for number, piece in enumerate(pieces):
        count = piece.shape[0]
        if begin == whole.shape[0]:
            break
        copies.append(
            pltpu.make_async_copy(piece, whole.at[begin : begin + count], sem.at[number])
        )
        begin += count
    for copy in copies:
        copy.start()
    for copy in copies:
        copy.wait()


def chosen(code, slots):
    tokens = code.shape[1]
    return lax.broadcasted_iota(jnp.int32, (slots, tokens), 0) == jnp.bitwise_and(code, 1023)


def weight_parts(weights, streams):
    specs, operands = [], []
    for array in weights:
        _, rows, columns = array.shape
        for number in range(streams):
            specs.append(
                pl.BlockSpec((1, rows // streams, columns), lambda i, number=number: (i, number, 0))
            )
            operands.append(array)
    return specs, operands


def gather_slots(code_ref, whole_ref, pick_ref, slot_ref):
    experts, _, tokens = code_ref.shape
    slots = pick_ref.shape[0] // experts
    model_width = whole_ref.shape[1]
    columns = 256
    for expert in range(experts):
        pick_ref[expert * slots : (expert + 1) * slots, :] = (
            chosen(code_ref[expert], slots).astype(WIDE).astype(NARROW)
        )
    for begin in range(0, model_width, columns):
        part = slice(begin, begin + columns)
        slot_ref[:, part] = mm(pick_ref[...], whole_ref[:, part], NN).astype(NARROW)


def forward_tokens_body(code_ref, gate_ref, *refs):
    w_refs, refs = refs[:2], refs[2:]
    pieces, refs = refs[:-9], refs[-9:]
    xs_ref, ag_ref, active_ref, slope_ref, x_ref, slot_ref, pick_ref, sem, out_sem = refs
    step = pl.program_id(0)
    slots = ag_ref.shape[1]
    out = pltpu.make_async_copy(slot_ref, xs_ref, out_sem)

    @pl.when(step == 0)
    def _():
        fetch(pieces, x_ref, sem)
        gather_slots(code_ref, x_ref, pick_ref, slot_ref)
        out.start()

    choose = chosen(code_ref[step], slots)
    gate = jnp.sum(jnp.where(choose, gate_ref[step], 0.0), axis=1, keepdims=True)
    rows = pl.ds(pl.multiple_of(step * slots, slots), slots)
    pre_act, begin = 0.0, 0
    for w_ref in w_refs:
        end = begin + w_ref.shape[1]
        pre_act = pre_act + mm(slot_ref[rows, begin:end], w_ref[0], NN)
        begin = end
    squash = jax.nn.sigmoid(pre_act)
    active = pre_act * squash
    active_ref[0] = active
    ag_ref[0] = (gate * active).astype(NARROW)
    slope_ref[0] = gate * squash * (1.0 + pre_act * (1.0 - squash))
    pl.when(step == pl.num_programs(0) - 1)(out.wait)


def forward_tokens(code, gate_tok, x_pieces, w_split):
    experts, model_width, hidden = w_split.shape
    tokens = code.shape[2]
    slots = tokens // 128 * CAP
    expert = lambda i: (i, 0, 0)
    all_experts = pl.BlockSpec((experts, 1, tokens), lambda i: (0, 0, 0))
    w_specs, w_operands = weight_parts([w_split], 2)
    shapes = [(hidden, NARROW), (hidden, WIDE), (hidden, WIDE)]
    return pl.pallas_call(
        forward_tokens_body,
        out_shape=[jax.ShapeDtypeStruct((experts * slots, model_width), NARROW)]
        + [jax.ShapeDtypeStruct((experts, slots, width), dtype) for width, dtype in shapes],
        grid=(experts,),
        in_specs=[all_experts, all_experts, *w_specs, *[ANY] * len(x_pieces)],
        out_specs=[ANY] + [pl.BlockSpec((1, slots, width), expert) for width, _ in shapes],
        scratch_shapes=[
            pltpu.VMEM((tokens, model_width), NARROW),
            pltpu.VMEM((experts * slots, model_width), NARROW),
            pltpu.VMEM((experts * slots, tokens), NARROW),
            pltpu.SemaphoreType.DMA((len(x_pieces),)),
            pltpu.SemaphoreType.DMA(()),
        ],
        compiler_params=pltpu.CompilerParams(vmem_limit_bytes=56 * MIB),
        cost_estimate=pl.CostEstimate(
            flops=2 * slots * experts * model_width * (hidden + tokens),
            bytes_accessed=2 * experts * model_width * hidden,
            transcendentals=0,
        ),
        name="forward_tokens",
    )(code, gate_tok, *w_operands, *x_pieces)


def forward_cotangents_body(code_ref, active_ref, slope_ref, *refs):
    w_refs, v_refs, refs = refs[:2], refs[2:4], refs[4:]
    pieces, refs = refs[:-10], refs[-10:]
    gs_ref, gp_ref, keep_ref, send_ref, g_ref, slot_ref, back_ref, pick_ref, sem, out_sem = refs
    step = pl.program_id(0)
    slots = gp_ref.shape[1]
    model_width = g_ref.shape[1]
    columns = 512
    out = pltpu.make_async_copy(slot_ref, gs_ref, out_sem)

    @pl.when(step == 0)
    def _():
        fetch(pieces, g_ref, sem)
        gather_slots(code_ref, g_ref, pick_ref, slot_ref)
        out.start()

    code = code_ref[step]
    rows = pl.ds(pl.multiple_of(step * slots, slots), slots)
    gate_part, begin = 0.0, 0
    for v_ref in v_refs:
        part = slice(begin, begin + v_ref.shape[1])
        upstream = mm(slot_ref[rows, :], v_ref[0], NT)
        gate_part = gate_part + jnp.sum(active_ref[0, :, part] * upstream, axis=1, keepdims=True)
        gp_ref[0, :, part] = (slope_ref[0, :, part] * upstream).astype(NARROW)
        begin = part.stop
    for begin in range(0, model_width, columns):
        held = w_refs[0].shape[1]
        w_ref, inner = w_refs[begin // held], begin % held
        back = mm(gp_ref[0], w_ref[0, inner : inner + columns, :], NT)
        back_ref[rows, begin : begin + columns] = back.astype(NARROW)
    which = jnp.sum(
        jnp.where(chosen(code, slots), jnp.right_shift(code, 10), 0), axis=1, keepdims=True
    )
    lane = lax.broadcasted_iota(jnp.int32, (slots, LANES), 1)
    high = gate_part.astype(NARROW).astype(WIDE)
    gates = jnp.where(lane == which, high, 0.0)
    gates = jnp.where(lane == which + LANES // 2, gate_part - high, gates)
    back_ref[rows, model_width:] = gates.astype(NARROW)

    @pl.when(step == pl.num_programs(0) - 1)
    def _():
        out.wait()
        quarter = g_ref.shape[0] // 4
        for begin in range(0, model_width + LANES, columns):
            part = slice(begin, min(begin + columns, model_width + LANES))
            summed = mm(pick_ref[...], back_ref[:, part], TN)
            if begin == model_width:
                summed = summed + pltpu.roll(summed, LANES // 2, 1)
            for pair in range(2):
                lower = 2 * pair * quarter
                into = slice(pair * quarter, (pair + 1) * quarter)
                keep_ref[into, part] = summed[lower : lower + quarter]
                send_ref[into, part] = summed[lower + quarter : lower + 2 * quarter].astype(NARROW)


def forward_cotangents(code, active, slope, g_pieces, w_split, v_split):
    experts, model_width, hidden = w_split.shape
    tokens = code.shape[2]
    slots = tokens // 128 * CAP
    width = model_width + LANES
    expert = lambda i: (i, 0, 0)
    whole = lambda i: (0, 0)
    one = pl.Buffered(1)
    w_specs, w_operands = weight_parts([w_split], 2)
    v_specs, v_operands = weight_parts(v_split, 1)
    return pl.pallas_call(
        forward_cotangents_body,
        out_shape=[
            jax.ShapeDtypeStruct((experts * slots, model_width), NARROW),
            jax.ShapeDtypeStruct((experts, slots, hidden), NARROW),
            jax.ShapeDtypeStruct((tokens // 2, width), WIDE),
            jax.ShapeDtypeStruct((tokens // 2, width), NARROW),
        ],
        grid=(experts,),
        in_specs=[
            pl.BlockSpec((experts, 1, tokens), lambda i: (0, 0, 0)),
            pl.BlockSpec((1, slots, hidden), expert),
            pl.BlockSpec((1, slots, hidden), expert),
            *w_specs,
            *v_specs,
            *[ANY] * len(g_pieces),
        ],
        out_specs=[
            ANY,
            pl.BlockSpec((1, slots, hidden), expert),
            pl.BlockSpec((tokens // 2, width), whole, pipeline_mode=one),
            pl.BlockSpec((tokens // 2, width), whole, pipeline_mode=one),
        ],
        scratch_shapes=[
            pltpu.VMEM((tokens, model_width), NARROW),
            pltpu.VMEM((experts * slots, model_width), NARROW),
            pltpu.VMEM((experts * slots, width), NARROW),
            pltpu.VMEM((experts * slots, tokens), NARROW),
            pltpu.SemaphoreType.DMA((len(g_pieces),)),
            pltpu.SemaphoreType.DMA(()),
        ],
        compiler_params=pltpu.CompilerParams(vmem_limit_bytes=56 * MIB),
        cost_estimate=pl.CostEstimate(
            flops=2 * slots * experts * model_width * (2 * hidden + 2 * tokens),
            bytes_accessed=4 * experts * model_width * hidden,
            transcendentals=0,
        ),
        name="forward_cotangents",
    )(code, active, slope, *w_operands, *v_operands, *g_pieces)


def odd_tiles(rows):
    tiles = -(-rows // 8)
    return 8 * (tiles + 1 - tiles % 2)


def outer_body(group, a_ref, b_ref, *refs):
    out_ref, flag_ref, wide_ref = refs[-3:]
    flag_ref[...] = jnp.zeros_like(flag_ref)
    rows, tiles, experts, _ = out_ref.shape
    stride = wide_ref.shape[1]
    held = group * experts
    out = out_ref.reshape(rows, tiles * experts, LANES)
    flat = wide_ref.reshape(rows * stride, LANES)
    for begin in range(0, tiles, group):
        for expert in range(experts):
            part = mm(a_ref[expert], b_ref[expert, :, begin * LANES : (begin + group) * LANES], TN)
            for tile in range(group):
                flat[pl.ds(tile * experts + expert, rows, stride), :] = part[
                    :, tile * LANES : (tile + 1) * LANES
                ]
        out[:, begin * experts : begin * experts + held, :] = wide_ref[:, :held, :].astype(NARROW)


def outer(a, b, holder, start, count, block, group, after):
    experts, slots, total = a.shape
    columns = b.shape[2]
    tiles = columns // LANES
    first = start // block
    extra = list(after) if holder is None else [holder, *after]
    return pl.pallas_call(
        functools.partial(outer_body, group),
        out_shape=[jax.ShapeDtypeStruct((total, tiles, experts, LANES), NARROW), FLAG],
        grid=(count // block,),
        in_specs=[
            pl.BlockSpec((experts, slots, block), lambda i: (0, 0, first + i)),
            pl.BlockSpec(
                (experts, slots, columns), lambda i: (0, 0, 0), pipeline_mode=pl.Buffered(1)
            ),
            *[ANY] * len(extra),
        ],
        out_specs=[
            pl.BlockSpec((block, tiles, experts, LANES), lambda i: (first + i, 0, 0, 0)),
            pl.BlockSpec(FLAG.shape, lambda i: (0, 0)),
        ],
        scratch_shapes=[pltpu.VMEM((block, odd_tiles(group * experts), LANES), WIDE)],
        input_output_aliases={} if holder is None else {2: 0},
        compiler_params=pltpu.CompilerParams(vmem_limit_bytes=40 * MIB),
        cost_estimate=pl.CostEstimate(
            flops=2 * experts * slots * count * columns,
            bytes_accessed=4 * experts * count * columns,
            transcendentals=0,
        ),
        name="weight_gradient",
    )(a, b, *extra)


def stored_view(tiled):
    rows, tiles, experts, _ = tiled.shape
    return tiled.transpose(0, 2, 1, 3).reshape(rows, experts, tiles * LANES)


def local(tokens, cotangent, expert_ids, gate_values, w_in, w_out):
    if not is_small():
        return local_general(tokens, cotangent, expert_ids, gate_values, w_in, w_out)
    tok_rows, model_width = tokens.shape
    top_count = expert_ids.shape[1]
    local_count = w_in.shape[1]
    hidden = w_in.shape[2]
    half = tok_rows // 2
    first = lax.axis_index("expert") * local_count
    fsdp = lax.axis_index("fsdp")
    x_index = fsdp % 2
    place = jnp.stack([x_index, fsdp // 2]).astype(jnp.int32)

    meta = jnp.concatenate([expert_ids.astype(WIDE), gate_values.astype(WIDE)], axis=1).T
    turned = own_order(meta)
    meta = jnp.stack([meta, swap(meta, CORE), swap(turned, Y), swap(turned, CORE | Y)])
    w_view, v_view = tiled_view(w_in), tiled_view(w_out)
    x_near = swap(lax.dynamic_slice_in_dim(tokens, x_index * half, half, axis=0), Y)
    g_near = swap(lax.dynamic_slice_in_dim(cotangent, x_index * half, half, axis=0), Y)
    x_core, g_core = swap(tokens, CORE), swap(cotangent, CORE)
    ids, gates = meta[:, :top_count].astype(jnp.int32), meta[:, top_count:]
    blocks = ids.shape[0]
    names = first + jnp.arange(local_count, dtype=jnp.int32)
    named = ids[:, None] == names[None, :, None, None]
    hit = jnp.any(named, axis=2)
    gate_tok = jnp.sum(jnp.where(named, gates[:, None], 0.0), axis=2)
    earlier = jnp.tril(jnp.ones((tok_rows, tok_rows), WIDE), -1)
    position = jnp.einsum("tu,blu->blt", earlier, hit.astype(WIDE)).astype(jnp.int32)
    base = jnp.arange(blocks, dtype=jnp.int32)[:, None, None] * CAP
    order = jnp.arange(top_count, dtype=jnp.int32)[None, None, :, None]
    which = jnp.sum(jnp.where(named, order, 0), axis=2)
    code = jnp.where(hit, base + position, 1023) + 1024 * which

    def by_expert(value):
        return jnp.swapaxes(value, 0, 1).reshape(local_count, 1, blocks * tok_rows)

    code, gate_tok = by_expert(code), by_expert(gate_tok)
    w_sort, v_sort = sorter(8, 6, local_count), sorter(16, 4, local_count)
    w_split, flag = split_experts(w_view, w_sort, 0, model_width, 256, 6, 8, [])
    (x_near,) = hold([x_near], [flag])
    x_far = swap(x_near, X)
    x_near_core = swap(x_near, CORE)
    v_low, flag = split_experts(v_view, v_sort, 0, hidden // 2, 64, 4, 16, [x_near])
    x_far, g_near = hold([x_far, g_near], [flag])
    g_far = swap(g_near, X)
    g_near_core = swap(g_near, CORE)
    x_far_core = swap(x_far, CORE)
    v_high, flag = split_experts(v_view, v_sort, hidden // 2, hidden // 2, 64, 4, 16, [x_far])
    x_pieces = [tokens, x_core, x_near, x_far, x_near_core, x_far_core]
    (g_far,) = hold([g_far], [flag])
    g_far_core = swap(g_far, CORE)
    xs, ag, active, slope = forward_tokens(code, gate_tok, [*x_pieces, g_far], w_split)
    g_pieces = [cotangent, g_core, g_near, g_far, g_near_core, g_far_core]
    gs, gp, keep, send = forward_cotangents(
        code, active, slope, g_pieces, w_split, [v_low, v_high]
    )
    xs, gs = xs.reshape(local_count, -1, model_width), gs.reshape(local_count, -1, model_width)
    width = keep.shape[1]

    def shape(rows, dtype, columns=width):
        return jax.ShapeDtypeStruct((rows, columns), dtype)

    def in_part(holder, number, after):
        rows = model_width // 4
        return outer(xs, gp, holder, number * rows, rows, 256, 6, after)

    def out_part(holder, number, after):
        rows = hidden // 3
        return outer(ag, gs, holder, number * rows, rows, 128, 8, after)

    got = swap(send, CORE)
    grad_in, flag = in_part(None, 0, [])
    mine, *sends = small_call(
        first_sum, place, [keep, got], [flag],
        [shape(half, WIDE)] + [shape(half, NARROW)] * 3, "first_sum", 32,
    )
    got = [swap(part, mask) for part, mask in zip(sends, (X, Y, X | Y))]
    grad_in, flag = in_part(grad_in, 1, [mine])
    grad_in, flag = in_part(grad_in, 2, [flag])
    grad_in, flag = in_part(grad_in, 3, [flag])
    mine, *sends = small_call(
        second_sum, place, [mine, *got], [flag],
        [shape(half // 4, WIDE)] + [shape(half // 4, NARROW)] * 3, "second_sum",
    )
    got = [swap(part, mask * Z) for part, mask in zip(sends, (1, 2, 3))]
    grad_out, flag = out_part(None, 0, [mine])
    (final,) = small_call(
        third_sum, place, [mine, *got], [flag], [shape(half // 4, NARROW)], "third_sum"
    )
    got = [swap(final, mask * Z) for mask in (1, 2, 3)]
    grad_out, flag = out_part(grad_out, 1, [final])
    (near,) = small_call(join_z, place, [final, *got], [flag], [shape(half, NARROW)], "join_z")
    far = swap(near, X)
    grad_out, flag = out_part(grad_out, 2, [near])
    grad_tokens, grad_gates = small_call(
        join_x, place, [near, far], [flag],
        [shape(tok_rows, NARROW, model_width), shape(tok_rows, NARROW, LANES)], "join_x",
    )
    grad_gates = grad_gates[:, :top_count]
    return (grad_tokens, grad_gates, stored_view(grad_in), stored_view(grad_out))


def local_general(tokens, cotangent, expert_ids, gate_values, w_in, w_out):
    tok_rows, model_width = tokens.shape
    local_count = w_in.shape[1]
    first = lax.axis_index("expert") * local_count
    gather = functools.partial(lax.all_gather, axis_name="expert", axis=0)
    ids, gates = gather(expert_ids), gather(gate_values).astype(WIDE)
    x_blocks, g_blocks = gather(tokens), gather(cotangent)
    blocks = ids.shape[0]
    names = first + jnp.arange(local_count, dtype=jnp.int32)
    named = ids[:, None] == names[None, :, None, None]
    hit = jnp.any(named, axis=3)
    gate_tok = jnp.sum(jnp.where(named, gates[:, None], 0.0), axis=3)
    earlier = jnp.tril(jnp.ones((tok_rows, tok_rows), WIDE), -1)
    position = jnp.einsum("tu,blu->blt", earlier, hit.astype(WIDE)).astype(jnp.int32)
    slots = jnp.arange(CAP, dtype=jnp.int32)
    choose = hit[:, :, None] & (position[:, :, None] == slots[None, None, :, None])
    pick = choose.astype(NARROW)
    slot_x = jnp.einsum("blst,btd->lbsd", pick, x_blocks, preferred_element_type=WIDE).astype(NARROW)
    slot_g = jnp.einsum("blst,btd->lbsd", pick, g_blocks, preferred_element_type=WIDE).astype(NARROW)
    gate_slot = jnp.sum(jnp.where(choose, gate_tok[:, :, None], 0.0), axis=3)
    rows = blocks * CAP
    slot_x = slot_x.reshape(local_count, rows, model_width)
    slot_g = slot_g.reshape(local_count, rows, model_width)
    gate_slot = jnp.swapaxes(gate_slot, 0, 1).reshape(local_count, rows, 1)
    pre_act = jnp.einsum("lrd,dlf->lrf", slot_x, w_in, preferred_element_type=WIDE)
    upstream = jnp.einsum("lrd,fld->lrf", slot_g, w_out, preferred_element_type=WIDE)
    squash = jax.nn.sigmoid(pre_act)
    active = pre_act * squash
    gate_part = jnp.sum(active * upstream, axis=-1)
    act_gated = (gate_slot * active).astype(NARROW)
    grad_pre = (gate_slot * squash * (1.0 + pre_act * (1.0 - squash)) * upstream).astype(NARROW)
    gate_part = jnp.swapaxes(gate_part.reshape(local_count, blocks, CAP), 0, 1)
    gate_tok = jnp.sum(jnp.where(choose, gate_part[..., None], 0.0), axis=2)
    gate_back = jnp.sum(jnp.where(named, gate_tok[..., None], 0.0), axis=1)
    part_x = jnp.einsum("lrf,dlf->lrd", grad_pre, w_in, preferred_element_type=WIDE)
    part_x = part_x.astype(NARROW).reshape(local_count, blocks, CAP, model_width)
    token_part = jnp.einsum("blst,lbsd->btd", pick, part_x, preferred_element_type=WIDE)
    scatter = functools.partial(lax.psum_scatter, axis_name="expert", scatter_dimension=0)
    grad_tokens = lax.psum(scatter(token_part), "fsdp").astype(NARROW)
    grad_gates = lax.psum(scatter(gate_back), "fsdp").astype(NARROW)
    grad_in = jnp.einsum("lrd,lrf->dlf", slot_x, grad_pre, preferred_element_type=WIDE).astype(NARROW)
    grad_out = jnp.einsum("lrf,lrd->fld", act_gated, slot_g, preferred_element_type=WIDE).astype(NARROW)
    return (grad_tokens, grad_gates, grad_in, grad_out)


def solution(mesh):
    return jax.shard_map(
        local,
        mesh=mesh,
        in_specs=(
            P("expert", None),
            P("expert", None),
            P("expert", None),
            P("expert", None),
            P(None, "expert", "fsdp"),
            P("fsdp", "expert", None),
        ),
        out_specs=(
            P("expert", None),
            P("expert", None),
            P(None, "expert", "fsdp"),
            P("fsdp", "expert", None),
        ),
        check_vma=False,
    )
```

```python
import functools
import jax
import jax.numpy as jnp
import numpy as np
from jax import lax
from jax.experimental import pallas as pl
from jax.experimental.pallas import tpu as pltpu
from jax.sharding import PartitionSpec as P

EXPERTS = 16
CAP = 40
AXES = ("fsdp", "expert")
CORE, Y, X, Z = 1, 2, 4, 8
LANES = 128
NARROW, WIDE = jnp.bfloat16, jnp.float32
MIB = 1 << 20
TN = (((0,), (0,)), ((), ()))
NT = (((1,), (1,)), ((), ()))
NN = (((1,), (0,)), ((), ()))


def mm(a, b, dims):
    return lax.dot_general(a, b, dims, preferred_element_type=WIDE)


def swap(value, mask):
    size = lax.axis_size("fsdp") * lax.axis_size("expert")
    return lax.ppermute(value, AXES, [(i, i ^ mask) for i in range(size)])


def is_small():
    return lax.axis_size("fsdp") == 8 and lax.axis_size("expert") == 4


def own_order(rows):
    x_index = lax.axis_index("fsdp") % 2
    half = rows.shape[-1] // 2
    return jnp.where(
        x_index == 0, rows, jnp.concatenate([rows[..., half:], rows[..., :half]], axis=-1)
    )


ANY = pl.BlockSpec(memory_space=pl.ANY)
FLAG = jax.ShapeDtypeStruct((8, LANES), WIDE)


def small_call(body, place, inputs, after, outs, name, grant=12, steps=1):
    given = len(inputs)

    def run(place_ref, *refs):
        body(place_ref, refs[:given], refs[given + len(after) :])

    def whole(array):
        rows, columns = array.shape
        return pl.BlockSpec((rows, columns // steps), lambda i: (0, i))

    return pl.pallas_call(
        run,
        out_shape=outs,
        grid=(steps,),
        in_specs=[pl.BlockSpec(memory_space=pltpu.SMEM)]
        + [whole(array) for array in inputs]
        + [ANY] * len(after),
        out_specs=[whole(out) for out in outs],
        compiler_params=pltpu.CompilerParams(vmem_limit_bytes=grant * MIB),
        cost_estimate=pl.CostEstimate(flops=0, bytes_accessed=1 << 20, transcendentals=0),
        name=name,
    )(place, *inputs, *after)


def hold(arrays, after):
    count = len(arrays)
    return pl.pallas_call(
        lambda *refs: None,
        out_shape=[jax.ShapeDtypeStruct(array.shape, array.dtype) for array in arrays],
        in_specs=[ANY] * (count + len(after)),
        out_specs=[ANY] * count,
        input_output_aliases={number: number for number in range(count)},
        cost_estimate=pl.CostEstimate(flops=0, bytes_accessed=1 << 18, transcendentals=0),
        name="hold",
    )(*arrays, *after)


def at(index, size):
    return pl.ds(pl.multiple_of(index * size, size), size)


def first_sum(place_ref, ins, outs):
    keep_ref, got_ref = ins
    mine_ref, x_ref, y_ref, xy_ref = outs
    half = mine_ref.shape[0]
    x_index = place_ref[0]

    def total(rows):
        return keep_ref[rows, :] + got_ref[rows, :].astype(WIDE)

    mine_ref[...] = total(at(x_index, half))
    x_ref[...] = total(at(1 - x_index, half)).astype(NARROW)
    y_ref[...] = total(slice(2 * half, 3 * half)).astype(NARROW)
    xy_ref[...] = total(slice(3 * half, 4 * half)).astype(NARROW)


def second_sum(place_ref, ins, outs):
    mine_ref, x_ref, y_ref, xy_ref = ins
    quarter = outs[0].shape[0]
    z_index = place_ref[1]
    for step in range(4):
        rows = at(z_index ^ step, quarter)
        total = mine_ref[rows, :] + x_ref[rows, :].astype(WIDE)
        total = total + (y_ref[rows, :].astype(WIDE) + xy_ref[rows, :].astype(WIDE))
        outs[step][...] = total.astype(outs[step].dtype)


def third_sum(place_ref, ins, outs):
    total = ins[0][...]
    for got in ins[1:]:
        total = total + got[...].astype(WIDE)
    outs[0][...] = total.astype(NARROW)


def join_z(place_ref, ins, outs):
    quarter = ins[0].shape[0]
    for step in range(4):
        outs[0][at(place_ref[1] ^ step, quarter), :] = ins[step][...]


def join_x(place_ref, ins, outs):
    half = ins[0].shape[0]
    model_width = outs[0].shape[1]
    for step in range(2):
        rows = at(place_ref[0] ^ step, half)
        outs[0][rows, :] = ins[step][:, :model_width]
        outs[1][rows, :] = ins[step][:, model_width:]


def sorter(rows, tiles, experts):
    size = rows * tiles * experts
    order = np.arange(size).reshape(rows, tiles, experts).transpose(2, 1, 0).reshape(-1)
    return jnp.asarray(np.eye(size, dtype=np.float32)[order], NARROW)


def tiled_view(weight):
    rows, experts, columns = weight.shape
    return weight.reshape(rows, experts, columns // LANES, LANES).transpose(0, 2, 1, 3)


def split_body(group, some, sort_ref, w_ref, *refs):
    out_ref, flag_ref = refs[-2:]
    flag_ref[...] = jnp.zeros_like(flag_ref)
    rows, tiles, experts, _ = w_ref.shape
    held = group * experts
    flat = w_ref.reshape(rows, tiles * experts, LANES)
    places = [(row, tile) for row in range(0, rows, some) for tile in range(0, tiles, group)]
    for pair in zip(places[::2], places[1::2]):
        blocks = [
            flat[row : row + some, tile * experts : tile * experts + held, :].reshape(
                some * held, LANES
            )
            for row, tile in pair
        ]
        result = mm(sort_ref[...], jnp.concatenate(blocks, axis=1), NN)
        for expert in range(experts):
            for tile in range(group):
                begin = (expert * group + tile) * some
                parts = [
                    result[begin : begin + some, side * LANES : (side + 1) * LANES]
                    for side in range(2)
                ]
                if some == 8:
                    row, first = pair[0][0], pair[0][1] + tile
                    out_ref[expert, row : row + 16, first * LANES : (first + 1) * LANES] = (
                        jnp.concatenate(parts, axis=0).astype(NARROW)
                    )
                else:
                    for (row, first), part in zip(pair, parts):
                        column = (first + tile) * LANES
                        out_ref[expert, row : row + some, column : column + LANES] = part.astype(
                            NARROW
                        )


def split_experts(view, sort, start, rows, block, group, some, after):
    _, tiles, experts, _ = view.shape
    columns = tiles * LANES
    first = start // block
    return pl.pallas_call(
        functools.partial(split_body, group, some),
        out_shape=[jax.ShapeDtypeStruct((experts, rows, columns), NARROW), FLAG],
        grid=(rows // block,),
        in_specs=[
            pl.BlockSpec(sort.shape, lambda i: (0, 0)),
            pl.BlockSpec((block, tiles, experts, LANES), lambda i: (first + i, 0, 0, 0)),
            *[ANY] * len(after),
        ],
        out_specs=[
            pl.BlockSpec((experts, block, columns), lambda i: (0, i, 0)),
            pl.BlockSpec(FLAG.shape, lambda i: (0, 0)),
        ],
        compiler_params=pltpu.CompilerParams(vmem_limit_bytes=56 * MIB),
        cost_estimate=pl.CostEstimate(
            flops=0, bytes_accessed=4 * experts * rows * columns, transcendentals=0
        ),
        name="split_experts",
    )(sort, view, *after)


def route_body(first_ref, *refs):
    metas, (code_ref, gate_ref) = refs[:-2], refs[-2:]
    experts = code_ref.shape[0]
    top_count = metas[0].shape[0] // 2
    row = lax.broadcasted_iota(jnp.int32, (LANES, LANES), 0)
    column = lax.broadcasted_iota(jnp.int32, (LANES, LANES), 1)
    earlier = (row < column).astype(WIDE).astype(NARROW)
    choice = lax.broadcasted_iota(jnp.int32, (top_count, LANES), 0)
    for block, meta_ref in enumerate(metas):
        lanes = slice(block * LANES, (block + 1) * LANES)
        ids = meta_ref[:top_count, :].astype(jnp.int32)
        gates = meta_ref[top_count:, :]
        named = [ids == first_ref[0] + expert for expert in range(experts)]
        hits = [jnp.sum(name.astype(WIDE), axis=0, keepdims=True) for name in named]
        before = mm(jnp.concatenate(hits, axis=0).astype(NARROW), earlier, NN).astype(jnp.int32)
        for expert in range(experts):
            which = jnp.sum(jnp.where(named[expert], choice, 0), axis=0, keepdims=True)
            slot = before[expert : expert + 1] + block * CAP
            code_ref[expert, :, lanes] = jnp.where(hits[expert] > 0.5, slot, 1023) + 1024 * which
            gate_ref[expert, :, lanes] = jnp.sum(
                jnp.where(named[expert], gates, 0.0), axis=0, keepdims=True
            )


def route(first, metas, experts):
    shape = (experts, 1, len(metas) * LANES)
    return pl.pallas_call(
        route_body,
        out_shape=[jax.ShapeDtypeStruct(shape, jnp.int32), jax.ShapeDtypeStruct(shape, WIDE)],
        in_specs=[pl.BlockSpec(memory_space=pltpu.SMEM)]
        + [pl.BlockSpec(memory_space=pltpu.VMEM)] * len(metas),
        out_specs=[pl.BlockSpec(memory_space=pltpu.VMEM)] * 2,
        cost_estimate=pl.CostEstimate(flops=0, bytes_accessed=1 << 18, transcendentals=0),
        name="route",
    )(first, *metas)


def fetch(pieces, whole, sem):
    copies, begin = [], 0
    for number, piece in enumerate(pieces):
        count = piece.shape[0]
        if begin == whole.shape[0]:
            break
        copies.append(
            pltpu.make_async_copy(piece, whole.at[begin : begin + count], sem.at[number])
        )
        begin += count
    for copy in copies:
        copy.start()
    for copy in copies:
        copy.wait()


def chosen(code, slots):
    tokens = code.shape[1]
    return lax.broadcasted_iota(jnp.int32, (slots, tokens), 0) == jnp.bitwise_and(code, 1023)


def weight_parts(weights, streams):
    specs, operands = [], []
    for array in weights:
        _, rows, columns = array.shape
        for number in range(streams):
            specs.append(
                pl.BlockSpec((1, rows // streams, columns), lambda i, number=number: (i, number, 0))
            )
            operands.append(array)
    return specs, operands


def block_picks(code_ref):
    experts, _, tokens = code_ref.shape
    slot = lax.broadcasted_iota(jnp.int32, (CAP, LANES), 0)
    picks = []
    for block in range(tokens // LANES):
        lanes = slice(block * LANES, (block + 1) * LANES)
        codes = [jnp.bitwise_and(code_ref[expert, :, lanes], 1023) for expert in range(experts)]
        found = [(slot + block * CAP == code).astype(WIDE) for code in codes]
        picks.append(jnp.concatenate(found, axis=0).astype(NARROW))
    return picks


def gather_slots(code_ref, whole_ref, wide_ref, slot_ref):
    experts = code_ref.shape[0]
    slots = slot_ref.shape[0] // experts
    columns = wide_ref.shape[1]
    picks = block_picks(code_ref)
    for begin in range(0, whole_ref.shape[1], columns):
        part = slice(begin, begin + columns)
        for block, pick in enumerate(picks):
            found = mm(pick, whole_ref[block * LANES : (block + 1) * LANES, part], NN)
            for expert in range(experts):
                row = expert * slots + block * CAP
                wide_ref[row : row + CAP, :] = found[expert * CAP : (expert + 1) * CAP]
        slot_ref[:, part] = wide_ref[...].astype(NARROW)


def forward_tokens_body(code_ref, gate_ref, *refs):
    w_refs, refs = refs[:2], refs[2:]
    pieces, refs = refs[:-8], refs[-8:]
    xs_ref, ag_ref, active_ref, slope_ref, x_ref, slot_ref, wide_ref, sem = refs
    step = pl.program_id(0)
    slots = ag_ref.shape[1]

    @pl.when(step == 0)
    def _():
        fetch(pieces, x_ref, sem)
        gather_slots(code_ref, x_ref, wide_ref, slot_ref)

    choose = chosen(code_ref[step], slots)
    gate = jnp.sum(jnp.where(choose, gate_ref[step], 0.0), axis=1, keepdims=True)
    rows = pl.ds(pl.multiple_of(step * slots, slots), slots)
    xs_ref[0] = slot_ref[rows, :]
    pre_act, begin = 0.0, 0
    for w_ref in w_refs:
        end = begin + w_ref.shape[1]
        pre_act = pre_act + mm(slot_ref[rows, begin:end], w_ref[0], NN)
        begin = end
    squash = jax.nn.sigmoid(pre_act)
    active = pre_act * squash
    active_ref[0] = active
    ag_ref[0] = (gate * active).astype(NARROW)
    slope_ref[0] = gate * squash * (1.0 + pre_act * (1.0 - squash))


def forward_tokens(code, gate_tok, x_pieces, w_split):
    experts, model_width, hidden = w_split.shape
    tokens = code.shape[2]
    slots = tokens // 128 * CAP
    expert = lambda i: (i, 0, 0)
    all_experts = pl.BlockSpec((experts, 1, tokens), lambda i: (0, 0, 0))
    w_specs, w_operands = weight_parts([w_split], 2)
    shapes = [(model_width, NARROW), (hidden, NARROW), (hidden, WIDE), (hidden, WIDE)]
    return pl.pallas_call(
        forward_tokens_body,
        out_shape=[jax.ShapeDtypeStruct((experts, slots, width), dtype) for width, dtype in shapes],
        grid=(experts,),
        in_specs=[all_experts, all_experts, *w_specs, *[ANY] * len(x_pieces)],
        out_specs=[pl.BlockSpec((1, slots, width), expert) for width, _ in shapes],
        scratch_shapes=[
            pltpu.VMEM((tokens, model_width), NARROW),
            pltpu.VMEM((experts * slots, model_width), NARROW),
            pltpu.VMEM((experts * slots, 512), WIDE),
            pltpu.SemaphoreType.DMA((len(x_pieces),)),
        ],
        compiler_params=pltpu.CompilerParams(vmem_limit_bytes=56 * MIB),
        cost_estimate=pl.CostEstimate(
            flops=2 * slots * experts * model_width * (hidden + tokens),
            bytes_accessed=2 * experts * model_width * hidden,
            transcendentals=0,
        ),
        name="forward_tokens",
    )(code, gate_tok, *w_operands, *x_pieces)


def forward_cotangents_body(code_ref, active_ref, slope_ref, *refs):
    w_refs, v_refs, refs = refs[:2], refs[2:4], refs[4:]
    pieces, refs = refs[:-9], refs[-9:]
    gs_ref, gp_ref, keep_ref, send_ref, g_ref, slot_ref, wide_ref, back_ref, sem = refs
    step = pl.program_id(0)
    slots = gp_ref.shape[1]
    model_width = g_ref.shape[1]
    columns = 512

    @pl.when(step == 0)
    def _():
        fetch(pieces, g_ref, sem)
        gather_slots(code_ref, g_ref, wide_ref, slot_ref)

    code = code_ref[step]
    rows = pl.ds(pl.multiple_of(step * slots, slots), slots)
    gs_ref[0] = slot_ref[rows, :]
    gate_part, begin = 0.0, 0
    for v_ref in v_refs:
        part = slice(begin, begin + v_ref.shape[1])
        upstream = mm(slot_ref[rows, :], v_ref[0], NT)
        gate_part = gate_part + jnp.sum(active_ref[0, :, part] * upstream, axis=1, keepdims=True)
        gp_ref[0, :, part] = (slope_ref[0, :, part] * upstream).astype(NARROW)
        begin = part.stop
    for begin in range(0, model_width, columns):
        held = w_refs[0].shape[1]
        w_ref, inner = w_refs[begin // held], begin % held
        back = mm(gp_ref[0], w_ref[0, inner : inner + columns, :], NT)
        back_ref[rows, begin : begin + columns] = back
    which = jnp.sum(
        jnp.where(chosen(code, slots), jnp.right_shift(code, 10), 0), axis=1, keepdims=True
    )
    lane = lax.broadcasted_iota(jnp.int32, (slots, LANES), 1)
    high = gate_part.astype(NARROW).astype(WIDE)
    gates = jnp.where(lane == which, high, 0.0)
    gates = jnp.where(lane == which + LANES // 2, gate_part - high, gates)
    back_ref[rows, model_width:] = gates

    @pl.when(step == pl.num_programs(0) - 1)
    def _():
        experts = code_ref.shape[0]
        picks = block_picks(code_ref)
        for begin in range(0, model_width + LANES, columns):
            part = slice(begin, min(begin + columns, model_width + LANES))
            for block, pick in enumerate(picks):
                starts = [expert * slots + block * CAP for expert in range(experts)]
                held = [back_ref[start : start + CAP, part] for start in starts]
                summed = mm(pick, jnp.concatenate(held, axis=0).astype(NARROW), TN)
                if begin == model_width:
                    summed = summed + pltpu.roll(summed, LANES // 2, 1)
                into = slice(block // 2 * LANES, (block // 2 + 1) * LANES)
                if block % 2 == 0:
                    keep_ref[into, part] = summed
                else:
                    send_ref[into, part] = summed.astype(NARROW)


def forward_cotangents(code, active, slope, g_pieces, w_split, v_split):
    experts, model_width, hidden = w_split.shape
    tokens = code.shape[2]
    slots = tokens // 128 * CAP
    width = model_width + LANES
    expert = lambda i: (i, 0, 0)
    whole = lambda i: (0, 0)
    one = pl.Buffered(1)
    w_specs, w_operands = weight_parts([w_split], 2)
    v_specs, v_operands = weight_parts(v_split, 1)
    return pl.pallas_call(
        forward_cotangents_body,
        out_shape=[
            jax.ShapeDtypeStruct((experts, slots, model_width), NARROW),
            jax.ShapeDtypeStruct((experts, slots, hidden), NARROW),
            jax.ShapeDtypeStruct((tokens // 2, width), WIDE),
            jax.ShapeDtypeStruct((tokens // 2, width), NARROW),
        ],
        grid=(experts,),
        in_specs=[
            pl.BlockSpec((experts, 1, tokens), lambda i: (0, 0, 0)),
            pl.BlockSpec((1, slots, hidden), expert),
            pl.BlockSpec((1, slots, hidden), expert),
            *w_specs,
            *v_specs,
            *[ANY] * len(g_pieces),
        ],
        out_specs=[
            pl.BlockSpec((1, slots, model_width), expert),
            pl.BlockSpec((1, slots, hidden), expert),
            pl.BlockSpec((tokens // 2, width), whole, pipeline_mode=one),
            pl.BlockSpec((tokens // 2, width), whole, pipeline_mode=one),
        ],
        scratch_shapes=[
            pltpu.VMEM((tokens, model_width), NARROW),
            pltpu.VMEM((experts * slots, model_width), NARROW),
            pltpu.VMEM((experts * slots, 512), WIDE),
            pltpu.VMEM((experts * slots, width), WIDE),
            pltpu.SemaphoreType.DMA((len(g_pieces),)),
        ],
        compiler_params=pltpu.CompilerParams(vmem_limit_bytes=56 * MIB),
        cost_estimate=pl.CostEstimate(
            flops=2 * slots * experts * model_width * (2 * hidden + 2 * tokens),
            bytes_accessed=4 * experts * model_width * hidden,
            transcendentals=0,
        ),
        name="forward_cotangents",
    )(code, active, slope, *w_operands, *v_operands, *g_pieces)


def odd_tiles(rows):
    tiles = -(-rows // 8)
    return 8 * (tiles + 1 - tiles % 2)


def outer_body(group, a_ref, b_ref, *refs):
    out_ref, flag_ref, wide_ref = refs[-3:]
    flag_ref[...] = jnp.zeros_like(flag_ref)
    rows, tiles, experts, _ = out_ref.shape
    stride = wide_ref.shape[1]
    held = group * experts
    out = out_ref.reshape(rows, tiles * experts, LANES)
    flat = wide_ref.reshape(rows * stride, LANES)
    for begin in range(0, tiles, group):
        for expert in range(experts):
            part = mm(a_ref[expert], b_ref[expert, :, begin * LANES : (begin + group) * LANES], TN)
            for tile in range(group):
                flat[pl.ds(tile * experts + expert, rows, stride), :] = part[
                    :, tile * LANES : (tile + 1) * LANES
                ]
        out[:, begin * experts : begin * experts + held, :] = wide_ref[:, :held, :].astype(NARROW)


def outer(a, b, holder, start, count, block, group, after):
    experts, slots, total = a.shape
    columns = b.shape[2]
    tiles = columns // LANES
    first = start // block
    extra = list(after) if holder is None else [holder, *after]
    return pl.pallas_call(
        functools.partial(outer_body, group),
        out_shape=[jax.ShapeDtypeStruct((total, tiles, experts, LANES), NARROW), FLAG],
        grid=(count // block,),
        in_specs=[
            pl.BlockSpec((experts, slots, block), lambda i: (0, 0, first + i)),
            pl.BlockSpec(
                (experts, slots, columns), lambda i: (0, 0, 0), pipeline_mode=pl.Buffered(1)
            ),
            *[ANY] * len(extra),
        ],
        out_specs=[
            pl.BlockSpec((block, tiles, experts, LANES), lambda i: (first + i, 0, 0, 0)),
            pl.BlockSpec(FLAG.shape, lambda i: (0, 0)),
        ],
        scratch_shapes=[pltpu.VMEM((block, odd_tiles(group * experts), LANES), WIDE)],
        input_output_aliases={} if holder is None else {2: 0},
        compiler_params=pltpu.CompilerParams(vmem_limit_bytes=40 * MIB),
        cost_estimate=pl.CostEstimate(
            flops=2 * experts * slots * count * columns,
            bytes_accessed=4 * experts * count * columns,
            transcendentals=0,
        ),
        name="weight_gradient",
    )(a, b, *extra)


def stored_view(tiled):
    rows, tiles, experts, _ = tiled.shape
    return tiled.transpose(0, 2, 1, 3).reshape(rows, experts, tiles * LANES)


def local(tokens, cotangent, expert_ids, gate_values, w_in, w_out):
    if not is_small():
        return local_general(tokens, cotangent, expert_ids, gate_values, w_in, w_out)
    tok_rows, model_width = tokens.shape
    top_count = expert_ids.shape[1]
    local_count = w_in.shape[1]
    hidden = w_in.shape[2]
    half = tok_rows // 2
    first = lax.axis_index("expert") * local_count
    fsdp = lax.axis_index("fsdp")
    x_index = fsdp % 2
    place = jnp.stack([x_index, fsdp // 2]).astype(jnp.int32)

    meta = jnp.concatenate([expert_ids.astype(WIDE), gate_values.astype(WIDE)], axis=1).T
    turned = own_order(meta)
    metas = [meta, swap(meta, CORE), swap(turned, Y), swap(turned, CORE | Y)]
    w_view, v_view = tiled_view(w_in), tiled_view(w_out)
    x_near = swap(lax.dynamic_slice_in_dim(tokens, x_index * half, half, axis=0), Y)
    g_near = swap(lax.dynamic_slice_in_dim(cotangent, x_index * half, half, axis=0), Y)
    x_core, g_core = swap(tokens, CORE), swap(cotangent, CORE)
    w_sort, v_sort = sorter(8, 6, local_count), sorter(16, 4, local_count)
    w_split, flag = split_experts(w_view, w_sort, 0, model_width, 256, 6, 8, [])
    x_near, *others = hold([x_near, *metas[1:]], [flag])
    code, gate_tok = route(first.astype(jnp.int32).reshape(1), [metas[0], *others], local_count)
    x_far = swap(x_near, X)
    x_near_core = swap(x_near, CORE)
    v_low, flag = split_experts(v_view, v_sort, 0, hidden // 2, 64, 4, 16, [x_near, code])
    x_far, g_near = hold([x_far, g_near], [flag])
    g_far = swap(g_near, X)
    g_near_core = swap(g_near, CORE)
    x_far_core = swap(x_far, CORE)
    v_high, flag = split_experts(v_view, v_sort, hidden // 2, hidden // 2, 64, 4, 16, [x_far])
    x_pieces = [tokens, x_core, x_near, x_far, x_near_core, x_far_core]
    (g_far,) = hold([g_far], [flag])
    g_far_core = swap(g_far, CORE)
    xs, ag, active, slope = forward_tokens(code, gate_tok, [*x_pieces, g_far], w_split)
    g_pieces = [cotangent, g_core, g_near, g_far, g_near_core, g_far_core]
    gs, gp, keep, send = forward_cotangents(
        code, active, slope, g_pieces, w_split, [v_low, v_high]
    )
    width = keep.shape[1]

    def shape(rows, dtype, columns=width):
        return jax.ShapeDtypeStruct((rows, columns), dtype)

    def in_part(holder, number, after):
        rows = model_width // 4
        return outer(xs, gp, holder, number * rows, rows, 256, 6, after)

    def out_part(holder, number, after):
        rows = hidden // 3
        return outer(ag, gs, holder, number * rows, rows, 128, 8, after)

    got = swap(send, CORE)
    mine, *sends = small_call(
        first_sum, place, [keep, got], [],
        [shape(half, WIDE)] + [shape(half, NARROW)] * 3, "first_sum", 32,
    )
    got = [swap(part, mask) for part, mask in zip(sends, (X, Y, X | Y))]
    grad_in, flag = in_part(None, 0, [mine])
    grad_in, flag = in_part(grad_in, 1, [flag])
    grad_in, flag = in_part(grad_in, 2, [flag])
    grad_in, flag = in_part(grad_in, 3, [flag])
    mine, *sends = small_call(
        second_sum, place, [mine, *got], [flag],
        [shape(half // 4, WIDE)] + [shape(half // 4, NARROW)] * 3, "second_sum",
    )
    got = [swap(part, mask * Z) for part, mask in zip(sends, (1, 2, 3))]
    grad_out, flag = out_part(None, 0, [mine])
    (final,) = small_call(
        third_sum, place, [mine, *got], [flag], [shape(half // 4, NARROW)], "third_sum"
    )
    got = [swap(final, mask * Z) for mask in (1, 2, 3)]
    grad_out, flag = out_part(grad_out, 1, [final])
    (near,) = small_call(join_z, place, [final, *got], [flag], [shape(half, NARROW)], "join_z")
    far = swap(near, X)
    grad_out, flag = out_part(grad_out, 2, [near])
    grad_tokens, grad_gates = small_call(
        join_x, place, [near, far], [flag],
        [shape(tok_rows, NARROW, model_width), shape(tok_rows, NARROW, LANES)], "join_x",
    )
    grad_gates = grad_gates[:, :top_count]
    return (grad_tokens, grad_gates, stored_view(grad_in), stored_view(grad_out))


def local_general(tokens, cotangent, expert_ids, gate_values, w_in, w_out):
    tok_rows, model_width = tokens.shape
    local_count = w_in.shape[1]
    first = lax.axis_index("expert") * local_count
    gather = functools.partial(lax.all_gather, axis_name="expert", axis=0)
    ids, gates = gather(expert_ids), gather(gate_values).astype(WIDE)
    x_blocks, g_blocks = gather(tokens), gather(cotangent)
    blocks = ids.shape[0]
    names = first + jnp.arange(local_count, dtype=jnp.int32)
    named = ids[:, None] == names[None, :, None, None]
    hit = jnp.any(named, axis=3)
    gate_tok = jnp.sum(jnp.where(named, gates[:, None], 0.0), axis=3)
    earlier = jnp.tril(jnp.ones((tok_rows, tok_rows), WIDE), -1)
    position = jnp.einsum("tu,blu->blt", earlier, hit.astype(WIDE)).astype(jnp.int32)
    slots = jnp.arange(CAP, dtype=jnp.int32)
    choose = hit[:, :, None] & (position[:, :, None] == slots[None, None, :, None])
    pick = choose.astype(NARROW)
    slot_x = jnp.einsum("blst,btd->lbsd", pick, x_blocks, preferred_element_type=WIDE).astype(NARROW)
    slot_g = jnp.einsum("blst,btd->lbsd", pick, g_blocks, preferred_element_type=WIDE).astype(NARROW)
    gate_slot = jnp.sum(jnp.where(choose, gate_tok[:, :, None], 0.0), axis=3)
    rows = blocks * CAP
    slot_x = slot_x.reshape(local_count, rows, model_width)
    slot_g = slot_g.reshape(local_count, rows, model_width)
    gate_slot = jnp.swapaxes(gate_slot, 0, 1).reshape(local_count, rows, 1)
    pre_act = jnp.einsum("lrd,dlf->lrf", slot_x, w_in, preferred_element_type=WIDE)
    upstream = jnp.einsum("lrd,fld->lrf", slot_g, w_out, preferred_element_type=WIDE)
    squash = jax.nn.sigmoid(pre_act)
    active = pre_act * squash
    gate_part = jnp.sum(active * upstream, axis=-1)
    act_gated = (gate_slot * active).astype(NARROW)
    grad_pre = (gate_slot * squash * (1.0 + pre_act * (1.0 - squash)) * upstream).astype(NARROW)
    gate_part = jnp.swapaxes(gate_part.reshape(local_count, blocks, CAP), 0, 1)
    gate_tok = jnp.sum(jnp.where(choose, gate_part[..., None], 0.0), axis=2)
    gate_back = jnp.sum(jnp.where(named, gate_tok[..., None], 0.0), axis=1)
    part_x = jnp.einsum("lrf,dlf->lrd", grad_pre, w_in, preferred_element_type=WIDE)
    part_x = part_x.astype(NARROW).reshape(local_count, blocks, CAP, model_width)
    token_part = jnp.einsum("blst,lbsd->btd", pick, part_x, preferred_element_type=WIDE)
    scatter = functools.partial(lax.psum_scatter, axis_name="expert", scatter_dimension=0)
    grad_tokens = lax.psum(scatter(token_part), "fsdp").astype(NARROW)
    grad_gates = lax.psum(scatter(gate_back), "fsdp").astype(NARROW)
    grad_in = jnp.einsum("lrd,lrf->dlf", slot_x, grad_pre, preferred_element_type=WIDE).astype(NARROW)
    grad_out = jnp.einsum("lrf,lrd->fld", act_gated, slot_g, preferred_element_type=WIDE).astype(NARROW)
    return (grad_tokens, grad_gates, grad_in, grad_out)


def solution(mesh):
    return jax.shard_map(
        local,
        mesh=mesh,
        in_specs=(
            P("expert", None),
            P("expert", None),
            P("expert", None),
            P("expert", None),
            P(None, "expert", "fsdp"),
            P("fsdp", "expert", None),
        ),
        out_specs=(
            P("expert", None),
            P("expert", None),
            P(None, "expert", "fsdp"),
            P("fsdp", "expert", None),
        ),
        check_vma=False,
    )
```

```python
import functools
import jax
import jax.numpy as jnp
import numpy as np
from jax import lax
from jax.experimental import pallas as pl
from jax.experimental.pallas import tpu as pltpu
from jax.sharding import PartitionSpec as P

EXPERTS = 16
CAP = 40
AXES = ("fsdp", "expert")
CORE, Y, X, Z = 1, 2, 4, 8
LANES = 128
NARROW, WIDE = jnp.bfloat16, jnp.float32
MIB = 1 << 20
TN = (((0,), (0,)), ((), ()))
NT = (((1,), (1,)), ((), ()))
NN = (((1,), (0,)), ((), ()))


def mm(a, b, dims):
    return lax.dot_general(a, b, dims, preferred_element_type=WIDE)


def swap(value, mask):
    size = lax.axis_size("fsdp") * lax.axis_size("expert")
    return lax.ppermute(value, AXES, [(i, i ^ mask) for i in range(size)])


def is_small():
    return lax.axis_size("fsdp") == 8 and lax.axis_size("expert") == 4


def own_order(rows):
    x_index = lax.axis_index("fsdp") % 2
    half = rows.shape[-1] // 2
    return jnp.where(
        x_index == 0, rows, jnp.concatenate([rows[..., half:], rows[..., :half]], axis=-1)
    )


ANY = pl.BlockSpec(memory_space=pl.ANY)
FLAG = jax.ShapeDtypeStruct((8, LANES), WIDE)


def small_call(body, place, inputs, after, outs, name, grant=12, steps=1):
    given = len(inputs)

    def run(place_ref, *refs):
        body(place_ref, refs[:given], refs[given + len(after) :])

    def whole(array):
        rows, columns = array.shape
        return pl.BlockSpec((rows, columns // steps), lambda i: (0, i))

    return pl.pallas_call(
        run,
        out_shape=outs,
        grid=(steps,),
        in_specs=[pl.BlockSpec(memory_space=pltpu.SMEM)]
        + [whole(array) for array in inputs]
        + [ANY] * len(after),
        out_specs=[whole(out) for out in outs],
        compiler_params=pltpu.CompilerParams(vmem_limit_bytes=grant * MIB),
        cost_estimate=pl.CostEstimate(flops=0, bytes_accessed=1 << 20, transcendentals=0),
        name=name,
    )(place, *inputs, *after)


def hold(arrays, after):
    count = len(arrays)
    return pl.pallas_call(
        lambda *refs: None,
        out_shape=[jax.ShapeDtypeStruct(array.shape, array.dtype) for array in arrays],
        in_specs=[ANY] * (count + len(after)),
        out_specs=[ANY] * count,
        input_output_aliases={number: number for number in range(count)},
        cost_estimate=pl.CostEstimate(flops=0, bytes_accessed=1 << 18, transcendentals=0),
        name="hold",
    )(*arrays, *after)


def at(index, size):
    return pl.ds(pl.multiple_of(index * size, size), size)


def first_sum(place_ref, ins, outs):
    keep_ref, got_ref = ins
    mine_ref, x_ref, y_ref, xy_ref = outs
    half = mine_ref.shape[0]
    x_index = place_ref[0]

    def total(rows):
        return keep_ref[rows, :] + got_ref[rows, :].astype(WIDE)

    mine_ref[...] = total(at(x_index, half))
    x_ref[...] = total(at(1 - x_index, half)).astype(NARROW)
    y_ref[...] = total(slice(2 * half, 3 * half)).astype(NARROW)
    xy_ref[...] = total(slice(3 * half, 4 * half)).astype(NARROW)


def second_sum(place_ref, ins, outs):
    mine_ref, x_ref, y_ref, xy_ref = ins
    quarter = outs[0].shape[0]
    z_index = place_ref[1]
    for step in range(4):
        rows = at(z_index ^ step, quarter)
        total = mine_ref[rows, :] + x_ref[rows, :].astype(WIDE)
        total = total + (y_ref[rows, :].astype(WIDE) + xy_ref[rows, :].astype(WIDE))
        outs[step][...] = total.astype(outs[step].dtype)


def third_sum(place_ref, ins, outs):
    total = ins[0][...]
    for got in ins[1:]:
        total = total + got[...].astype(WIDE)
    outs[0][...] = total.astype(NARROW)


def join_z(place_ref, ins, outs):
    quarter = ins[0].shape[0]
    for step in range(4):
        outs[0][at(place_ref[1] ^ step, quarter), :] = ins[step][...]


def join_x(place_ref, ins, outs):
    half = ins[0].shape[0]
    model_width = outs[0].shape[1]
    for step in range(2):
        rows = at(place_ref[0] ^ step, half)
        outs[0][rows, :] = ins[step][:, :model_width]
        outs[1][rows, :] = ins[step][:, model_width:]


def sorter(rows, tiles, experts):
    size = rows * tiles * experts
    order = np.arange(size).reshape(rows, tiles, experts).transpose(2, 1, 0).reshape(-1)
    return jnp.asarray(np.eye(size, dtype=np.float32)[order], NARROW)


def tiled_view(weight):
    rows, experts, columns = weight.shape
    return weight.reshape(rows, experts, columns // LANES, LANES).transpose(0, 2, 1, 3)


def odd_tiles(rows):
    tiles = -(-rows // 8)
    return 8 * (tiles + 1 - tiles % 2)


def split_body(group, some, sort_ref, w_ref, *refs):
    out_ref, flag_ref, wide_ref = refs[-3:]
    flag_ref[...] = jnp.zeros_like(flag_ref)
    rows, tiles, experts, _ = w_ref.shape
    held = group * experts
    flat = w_ref.reshape(rows, tiles * experts, LANES)
    stride = wide_ref.shape[1]
    wide = wide_ref.reshape(wide_ref.shape[0] * stride, LANES)

    def matmul(pair):
        blocks = [
            flat[row : row + some, tile * experts : tile * experts + held, :].reshape(
                some * held, LANES
            )
            for row, tile in pair
        ]
        result = mm(sort_ref[...], jnp.concatenate(blocks, axis=1), NN)
        for expert in range(experts):
            for tile in range(group):
                begin = (expert * group + tile) * some
                parts = [
                    result[begin : begin + some, side * LANES : (side + 1) * LANES]
                    for side in range(2)
                ]
                if some == 8:
                    row, first = pair[0][0], pair[0][1] + tile
                    out_ref[expert, row : row + 16, first * LANES : (first + 1) * LANES] = (
                        jnp.concatenate(parts, axis=0).astype(NARROW)
                    )
                else:
                    for (row, first), part in zip(pair, parts):
                        column = (first + tile) * LANES
                        out_ref[expert, row : row + some, column : column + LANES] = part.astype(
                            NARROW
                        )

    for row in range(0, rows, 32):
        other, base = row + 16, row // 2
        wide_ref[base : base + 16, : tiles * experts, :] = flat[other : other + 16].astype(WIDE)
        places = [
            (first, tile) for first in range(row, other, some) for tile in range(0, tiles, group)
        ]
        pairs = list(zip(places[::2], places[1::2]))
        combos = [(expert, tile) for expert in range(experts) for tile in range(tiles)]
        share = len(combos) // len(pairs)
        for number, pair in enumerate(pairs):
            matmul(pair)
            for expert, tile in combos[number * share : (number + 1) * share]:
                part = wide[pl.ds(base * stride + tile * experts + expert, 16, stride), :]
                out_ref[expert, other : other + 16, tile * LANES : (tile + 1) * LANES] = (
                    part.astype(NARROW)
                )


def split_experts(view, sort, start, rows, block, group, some, after):
    _, tiles, experts, _ = view.shape
    columns = tiles * LANES
    first = start // block
    return pl.pallas_call(
        functools.partial(split_body, group, some),
        out_shape=[jax.ShapeDtypeStruct((experts, rows, columns), NARROW), FLAG],
        grid=(rows // block,),
        in_specs=[
            pl.BlockSpec(sort.shape, lambda i: (0, 0)),
            pl.BlockSpec((block, tiles, experts, LANES), lambda i: (first + i, 0, 0, 0)),
            *[ANY] * len(after),
        ],
        out_specs=[
            pl.BlockSpec((experts, block, columns), lambda i: (0, i, 0)),
            pl.BlockSpec(FLAG.shape, lambda i: (0, 0)),
        ],
        scratch_shapes=[pltpu.VMEM((block // 2, odd_tiles(tiles * experts), LANES), WIDE)],
        compiler_params=pltpu.CompilerParams(vmem_limit_bytes=56 * MIB),
        cost_estimate=pl.CostEstimate(
            flops=0, bytes_accessed=4 * experts * rows * columns, transcendentals=0
        ),
        name="split_experts",
    )(sort, view, *after)


def route_body(first_ref, *refs):
    metas, (code_ref, gate_ref) = refs[:-2], refs[-2:]
    experts = code_ref.shape[0]
    top_count = metas[0].shape[0] // 2
    row = lax.broadcasted_iota(jnp.int32, (LANES, LANES), 0)
    column = lax.broadcasted_iota(jnp.int32, (LANES, LANES), 1)
    earlier = (row < column).astype(WIDE).astype(NARROW)
    choice = lax.broadcasted_iota(jnp.int32, (top_count, LANES), 0)
    for block, meta_ref in enumerate(metas):
        lanes = slice(block * LANES, (block + 1) * LANES)
        ids = meta_ref[:top_count, :].astype(jnp.int32)
        gates = meta_ref[top_count:, :]
        named = [ids == first_ref[0] + expert for expert in range(experts)]
        hits = [jnp.sum(name.astype(WIDE), axis=0, keepdims=True) for name in named]
        before = mm(jnp.concatenate(hits, axis=0).astype(NARROW), earlier, NN).astype(jnp.int32)
        for expert in range(experts):
            which = jnp.sum(jnp.where(named[expert], choice, 0), axis=0, keepdims=True)
            slot = before[expert : expert + 1] + block * CAP
            code_ref[expert, :, lanes] = jnp.where(hits[expert] > 0.5, slot, 1023) + 1024 * which
            gate_ref[expert, :, lanes] = jnp.sum(
                jnp.where(named[expert], gates, 0.0), axis=0, keepdims=True
            )


def route(first, metas, experts):
    shape = (experts, 1, len(metas) * LANES)
    return pl.pallas_call(
        route_body,
        out_shape=[jax.ShapeDtypeStruct(shape, jnp.int32), jax.ShapeDtypeStruct(shape, WIDE)],
        in_specs=[pl.BlockSpec(memory_space=pltpu.SMEM)]
        + [pl.BlockSpec(memory_space=pltpu.VMEM)] * len(metas),
        out_specs=[pl.BlockSpec(memory_space=pltpu.VMEM)] * 2,
        cost_estimate=pl.CostEstimate(flops=0, bytes_accessed=1 << 18, transcendentals=0),
        name="route",
    )(first, *metas)


def fetch(pieces, whole, sem):
    copies, begin = [], 0
    for number, piece in enumerate(pieces):
        count = piece.shape[0]
        if begin == whole.shape[0]:
            break
        copies.append(
            pltpu.make_async_copy(piece, whole.at[begin : begin + count], sem.at[number])
        )
        begin += count
    for copy in copies:
        copy.start()
    for copy in copies:
        copy.wait()


def chosen(code, slots):
    tokens = code.shape[1]
    return lax.broadcasted_iota(jnp.int32, (slots, tokens), 0) == jnp.bitwise_and(code, 1023)


def weight_parts(weights, streams):
    specs, operands = [], []
    for array in weights:
        _, rows, columns = array.shape
        for number in range(streams):
            specs.append(
                pl.BlockSpec((1, rows // streams, columns), lambda i, number=number: (i, number, 0))
            )
            operands.append(array)
    return specs, operands


def block_picks(code_ref):
    experts, _, tokens = code_ref.shape
    slot = lax.broadcasted_iota(jnp.int32, (CAP, LANES), 0)
    picks = []
    for block in range(tokens // LANES):
        lanes = slice(block * LANES, (block + 1) * LANES)
        codes = [jnp.bitwise_and(code_ref[expert, :, lanes], 1023) for expert in range(experts)]
        found = [(slot + block * CAP == code).astype(WIDE) for code in codes]
        picks.append(jnp.concatenate(found, axis=0).astype(NARROW))
    return picks


def gather_slots(code_ref, whole_ref, wide_ref, slot_ref):
    experts = code_ref.shape[0]
    slots = slot_ref.shape[0] // experts
    columns = wide_ref.shape[1]
    picks = block_picks(code_ref)
    for begin in range(0, whole_ref.shape[1], columns):
        part = slice(begin, begin + columns)
        for block, pick in enumerate(picks):
            found = mm(pick, whole_ref[block * LANES : (block + 1) * LANES, part], NN)
            for expert in range(experts):
                row = expert * slots + block * CAP
                wide_ref[row : row + CAP, :] = found[expert * CAP : (expert + 1) * CAP]
        slot_ref[:, part] = wide_ref[...].astype(NARROW)


def forward_tokens_body(code_ref, gate_ref, *refs):
    w_refs, refs = refs[:2], refs[2:]
    pieces, refs = refs[:-8], refs[-8:]
    xs_ref, ag_ref, active_ref, slope_ref, x_ref, slot_ref, wide_ref, sem = refs
    step = pl.program_id(0)
    slots = ag_ref.shape[1]

    @pl.when(step == 0)
    def _():
        fetch(pieces, x_ref, sem)
        gather_slots(code_ref, x_ref, wide_ref, slot_ref)

    choose = chosen(code_ref[step], slots)
    gate = jnp.sum(jnp.where(choose, gate_ref[step], 0.0), axis=1, keepdims=True)
    rows = pl.ds(pl.multiple_of(step * slots, slots), slots)
    xs_ref[0] = slot_ref[rows, :]
    pre_act, begin = 0.0, 0
    for w_ref in w_refs:
        end = begin + w_ref.shape[1]
        pre_act = pre_act + mm(slot_ref[rows, begin:end], w_ref[0], NN)
        begin = end
    squash = jax.nn.sigmoid(pre_act)
    active = pre_act * squash
    active_ref[0] = active
    ag_ref[0] = (gate * active).astype(NARROW)
    slope_ref[0] = gate * squash * (1.0 + pre_act * (1.0 - squash))


def forward_tokens(code, gate_tok, x_pieces, w_split):
    experts, model_width, hidden = w_split.shape
    tokens = code.shape[2]
    slots = tokens // 128 * CAP
    expert = lambda i: (i, 0, 0)
    all_experts = pl.BlockSpec((experts, 1, tokens), lambda i: (0, 0, 0))
    w_specs, w_operands = weight_parts([w_split], 2)
    shapes = [(model_width, NARROW), (hidden, NARROW), (hidden, WIDE), (hidden, WIDE)]
    return pl.pallas_call(
        forward_tokens_body,
        out_shape=[jax.ShapeDtypeStruct((experts, slots, width), dtype) for width, dtype in shapes],
        grid=(experts,),
        in_specs=[all_experts, all_experts, *w_specs, *[ANY] * len(x_pieces)],
        out_specs=[pl.BlockSpec((1, slots, width), expert) for width, _ in shapes],
        scratch_shapes=[
            pltpu.VMEM((tokens, model_width), NARROW),
            pltpu.VMEM((experts * slots, model_width), NARROW),
            pltpu.VMEM((experts * slots, 512), WIDE),
            pltpu.SemaphoreType.DMA((len(x_pieces),)),
        ],
        compiler_params=pltpu.CompilerParams(vmem_limit_bytes=56 * MIB),
        cost_estimate=pl.CostEstimate(
            flops=2 * slots * experts * model_width * (hidden + tokens),
            bytes_accessed=2 * experts * model_width * hidden,
            transcendentals=0,
        ),
        name="forward_tokens",
    )(code, gate_tok, *w_operands, *x_pieces)


def forward_cotangents_body(code_ref, active_ref, slope_ref, *refs):
    w_refs, v_refs, refs = refs[:2], refs[2:4], refs[4:]
    pieces, refs = refs[:-9], refs[-9:]
    gs_ref, gp_ref, keep_ref, send_ref, g_ref, slot_ref, wide_ref, back_ref, sem = refs
    step = pl.program_id(0)
    slots = gp_ref.shape[1]
    model_width = g_ref.shape[1]
    columns = 512

    @pl.when(step == 0)
    def _():
        fetch(pieces, g_ref, sem)
        gather_slots(code_ref, g_ref, wide_ref, slot_ref)

    code = code_ref[step]
    rows = pl.ds(pl.multiple_of(step * slots, slots), slots)
    gs_ref[0] = slot_ref[rows, :]
    gate_part, begin = 0.0, 0
    for v_ref in v_refs:
        part = slice(begin, begin + v_ref.shape[1])
        upstream = mm(slot_ref[rows, :], v_ref[0], NT)
        gate_part = gate_part + jnp.sum(active_ref[0, :, part] * upstream, axis=1, keepdims=True)
        gp_ref[0, :, part] = (slope_ref[0, :, part] * upstream).astype(NARROW)
        begin = part.stop
    for begin in range(0, model_width, columns):
        held = w_refs[0].shape[1]
        w_ref, inner = w_refs[begin // held], begin % held
        back = mm(gp_ref[0], w_ref[0, inner : inner + columns, :], NT)
        back_ref[rows, begin : begin + columns] = back
    which = jnp.sum(
        jnp.where(chosen(code, slots), jnp.right_shift(code, 10), 0), axis=1, keepdims=True
    )
    lane = lax.broadcasted_iota(jnp.int32, (slots, LANES), 1)
    high = gate_part.astype(NARROW).astype(WIDE)
    gates = jnp.where(lane == which, high, 0.0)
    gates = jnp.where(lane == which + LANES // 2, gate_part - high, gates)
    back_ref[rows, model_width:] = gates

    @pl.when(step == pl.num_programs(0) - 1)
    def _():
        experts = code_ref.shape[0]
        picks = block_picks(code_ref)
        for begin in range(0, model_width + LANES, columns):
            part = slice(begin, min(begin + columns, model_width + LANES))
            for block, pick in enumerate(picks):
                starts = [expert * slots + block * CAP for expert in range(experts)]
                held = [back_ref[start : start + CAP, part] for start in starts]
                summed = mm(pick, jnp.concatenate(held, axis=0).astype(NARROW), TN)
                if begin == model_width:
                    summed = summed + pltpu.roll(summed, LANES // 2, 1)
                into = slice(block // 2 * LANES, (block // 2 + 1) * LANES)
                if block % 2 == 0:
                    keep_ref[into, part] = summed
                else:
                    send_ref[into, part] = summed.astype(NARROW)


def forward_cotangents(code, active, slope, g_pieces, w_split, v_split):
    experts, model_width, hidden = w_split.shape
    tokens = code.shape[2]
    slots = tokens // 128 * CAP
    width = model_width + LANES
    expert = lambda i: (i, 0, 0)
    whole = lambda i: (0, 0)
    one = pl.Buffered(1)
    w_specs, w_operands = weight_parts([w_split], 2)
    v_specs, v_operands = weight_parts(v_split, 1)
    return pl.pallas_call(
        forward_cotangents_body,
        out_shape=[
            jax.ShapeDtypeStruct((experts, slots, model_width), NARROW),
            jax.ShapeDtypeStruct((experts, slots, hidden), NARROW),
            jax.ShapeDtypeStruct((tokens // 2, width), WIDE),
            jax.ShapeDtypeStruct((tokens // 2, width), NARROW),
        ],
        grid=(experts,),
        in_specs=[
            pl.BlockSpec((experts, 1, tokens), lambda i: (0, 0, 0)),
            pl.BlockSpec((1, slots, hidden), expert),
            pl.BlockSpec((1, slots, hidden), expert),
            *w_specs,
            *v_specs,
            *[ANY] * len(g_pieces),
        ],
        out_specs=[
            pl.BlockSpec((1, slots, model_width), expert),
            pl.BlockSpec((1, slots, hidden), expert),
            pl.BlockSpec((tokens // 2, width), whole, pipeline_mode=one),
            pl.BlockSpec((tokens // 2, width), whole, pipeline_mode=one),
        ],
        scratch_shapes=[
            pltpu.VMEM((tokens, model_width), NARROW),
            pltpu.VMEM((experts * slots, model_width), NARROW),
            pltpu.VMEM((experts * slots, 512), WIDE),
            pltpu.VMEM((experts * slots, width), WIDE),
            pltpu.SemaphoreType.DMA((len(g_pieces),)),
        ],
        compiler_params=pltpu.CompilerParams(vmem_limit_bytes=48 * MIB),
        cost_estimate=pl.CostEstimate(
            flops=2 * slots * experts * model_width * (2 * hidden + 2 * tokens),
            bytes_accessed=4 * experts * model_width * hidden,
            transcendentals=0,
        ),
        name="forward_cotangents",
    )(code, active, slope, *w_operands, *v_operands, *g_pieces)


def outer_body(group, a_ref, b_ref, *refs):
    out_ref, flag_ref, wide_ref = refs[-3:]
    flag_ref[...] = jnp.zeros_like(flag_ref)
    rows, tiles, experts, _ = out_ref.shape
    stride = wide_ref.shape[1]
    held = group * experts
    out = out_ref.reshape(rows, tiles * experts, LANES)
    flat = wide_ref.reshape(rows * stride, LANES)
    for begin in range(0, tiles, group):
        for expert in range(experts):
            part = mm(a_ref[expert], b_ref[expert, :, begin * LANES : (begin + group) * LANES], TN)
            for tile in range(group):
                flat[pl.ds(tile * experts + expert, rows, stride), :] = part[
                    :, tile * LANES : (tile + 1) * LANES
                ]
        out[:, begin * experts : begin * experts + held, :] = wide_ref[:, :held, :].astype(NARROW)


def outer(a, b, holder, start, count, block, group, after):
    experts, slots, total = a.shape
    columns = b.shape[2]
    tiles = columns // LANES
    first = start // block
    extra = list(after) if holder is None else [holder, *after]
    return pl.pallas_call(
        functools.partial(outer_body, group),
        out_shape=[jax.ShapeDtypeStruct((total, tiles, experts, LANES), NARROW), FLAG],
        grid=(count // block,),
        in_specs=[
            pl.BlockSpec((experts, slots, block), lambda i: (0, 0, first + i)),
            pl.BlockSpec(
                (experts, slots, columns), lambda i: (0, 0, 0), pipeline_mode=pl.Buffered(1)
            ),
            *[ANY] * len(extra),
        ],
        out_specs=[
            pl.BlockSpec((block, tiles, experts, LANES), lambda i: (first + i, 0, 0, 0)),
            pl.BlockSpec(FLAG.shape, lambda i: (0, 0)),
        ],
        scratch_shapes=[pltpu.VMEM((block, odd_tiles(group * experts), LANES), WIDE)],
        input_output_aliases={} if holder is None else {2: 0},
        compiler_params=pltpu.CompilerParams(vmem_limit_bytes=40 * MIB),
        cost_estimate=pl.CostEstimate(
            flops=2 * experts * slots * count * columns,
            bytes_accessed=4 * experts * count * columns,
            transcendentals=0,
        ),
        name="weight_gradient",
    )(a, b, *extra)


def stored_view(tiled):
    rows, tiles, experts, _ = tiled.shape
    return tiled.transpose(0, 2, 1, 3).reshape(rows, experts, tiles * LANES)


def local(tokens, cotangent, expert_ids, gate_values, w_in, w_out):
    if not is_small():
        return local_general(tokens, cotangent, expert_ids, gate_values, w_in, w_out)
    tok_rows, model_width = tokens.shape
    top_count = expert_ids.shape[1]
    local_count = w_in.shape[1]
    hidden = w_in.shape[2]
    half = tok_rows // 2
    first = lax.axis_index("expert") * local_count
    fsdp = lax.axis_index("fsdp")
    x_index = fsdp % 2
    place = jnp.stack([x_index, fsdp // 2]).astype(jnp.int32)

    meta = jnp.concatenate([expert_ids.astype(WIDE), gate_values.astype(WIDE)], axis=1).T
    turned = own_order(meta)
    metas = [meta, swap(meta, CORE), swap(turned, Y), swap(turned, CORE | Y)]
    w_view, v_view = tiled_view(w_in), tiled_view(w_out)
    x_near = swap(lax.dynamic_slice_in_dim(tokens, x_index * half, half, axis=0), Y)
    g_near = swap(lax.dynamic_slice_in_dim(cotangent, x_index * half, half, axis=0), Y)
    x_core, g_core = swap(tokens, CORE), swap(cotangent, CORE)
    w_sort, v_sort = sorter(8, 6, local_count), sorter(16, 4, local_count)
    w_split, flag = split_experts(w_view, w_sort, 0, model_width, 256, 6, 8, [])
    x_near, *others = hold([x_near, *metas[1:]], [flag])
    code, gate_tok = route(first.astype(jnp.int32).reshape(1), [metas[0], *others], local_count)
    x_far = swap(x_near, X)
    x_near_core = swap(x_near, CORE)
    v_low, flag = split_experts(v_view, v_sort, 0, hidden // 2, 64, 4, 16, [x_near, code])
    x_far, g_near = hold([x_far, g_near], [flag])
    g_far = swap(g_near, X)
    g_near_core = swap(g_near, CORE)
    x_far_core = swap(x_far, CORE)
    v_high, flag = split_experts(v_view, v_sort, hidden // 2, hidden // 2, 64, 4, 16, [x_far])
    x_pieces = [tokens, x_core, x_near, x_far, x_near_core, x_far_core]
    (g_far,) = hold([g_far], [flag])
    g_far_core = swap(g_far, CORE)
    xs, ag, active, slope = forward_tokens(code, gate_tok, [*x_pieces, g_far], w_split)
    g_pieces = [cotangent, g_core, g_near, g_far, g_near_core, g_far_core]
    gs, gp, keep, send = forward_cotangents(
        code, active, slope, g_pieces, w_split, [v_low, v_high]
    )
    width = keep.shape[1]

    def shape(rows, dtype, columns=width):
        return jax.ShapeDtypeStruct((rows, columns), dtype)

    def in_part(holder, number, after):
        rows = model_width // 4
        return outer(xs, gp, holder, number * rows, rows, 256, 6, after)

    def out_part(holder, number, after):
        rows = hidden // 3
        return outer(ag, gs, holder, number * rows, rows, 128, 8, after)

    got = swap(send, CORE)
    mine, *sends = small_call(
        first_sum, place, [keep, got], [],
        [shape(half, WIDE)] + [shape(half, NARROW)] * 3, "first_sum", 32,
    )
    got = [swap(part, mask) for part, mask in zip(sends, (X, Y, X | Y))]
    grad_in, flag = in_part(None, 0, [mine])
    grad_in, flag = in_part(grad_in, 1, [flag])
    grad_in, flag = in_part(grad_in, 2, [flag])
    grad_in, flag = in_part(grad_in, 3, [flag])
    mine, *sends = small_call(
        second_sum, place, [mine, *got], [flag],
        [shape(half // 4, WIDE)] + [shape(half // 4, NARROW)] * 3, "second_sum",
    )
    got = [swap(part, mask * Z) for part, mask in zip(sends, (1, 2, 3))]
    grad_out, flag = out_part(None, 0, [mine])
    (final,) = small_call(
        third_sum, place, [mine, *got], [flag], [shape(half // 4, NARROW)], "third_sum"
    )
    got = [swap(final, mask * Z) for mask in (1, 2, 3)]
    grad_out, flag = out_part(grad_out, 1, [final])
    (near,) = small_call(join_z, place, [final, *got], [flag], [shape(half, NARROW)], "join_z")
    far = swap(near, X)
    grad_out, flag = out_part(grad_out, 2, [near])
    grad_tokens, grad_gates = small_call(
        join_x, place, [near, far], [flag],
        [shape(tok_rows, NARROW, model_width), shape(tok_rows, NARROW, LANES)], "join_x",
    )
    grad_gates = grad_gates[:, :top_count]
    return (grad_tokens, grad_gates, stored_view(grad_in), stored_view(grad_out))


def local_general(tokens, cotangent, expert_ids, gate_values, w_in, w_out):
    tok_rows, model_width = tokens.shape
    local_count = w_in.shape[1]
    first = lax.axis_index("expert") * local_count
    gather = functools.partial(lax.all_gather, axis_name="expert", axis=0)
    ids, gates = gather(expert_ids), gather(gate_values).astype(WIDE)
    x_blocks, g_blocks = gather(tokens), gather(cotangent)
    blocks = ids.shape[0]
    names = first + jnp.arange(local_count, dtype=jnp.int32)
    named = ids[:, None] == names[None, :, None, None]
    hit = jnp.any(named, axis=3)
    gate_tok = jnp.sum(jnp.where(named, gates[:, None], 0.0), axis=3)
    earlier = jnp.tril(jnp.ones((tok_rows, tok_rows), WIDE), -1)
    position = jnp.einsum("tu,blu->blt", earlier, hit.astype(WIDE)).astype(jnp.int32)
    slots = jnp.arange(CAP, dtype=jnp.int32)
    choose = hit[:, :, None] & (position[:, :, None] == slots[None, None, :, None])
    pick = choose.astype(NARROW)
    slot_x = jnp.einsum("blst,btd->lbsd", pick, x_blocks, preferred_element_type=WIDE).astype(NARROW)
    slot_g = jnp.einsum("blst,btd->lbsd", pick, g_blocks, preferred_element_type=WIDE).astype(NARROW)
    gate_slot = jnp.sum(jnp.where(choose, gate_tok[:, :, None], 0.0), axis=3)
    rows = blocks * CAP
    slot_x = slot_x.reshape(local_count, rows, model_width)
    slot_g = slot_g.reshape(local_count, rows, model_width)
    gate_slot = jnp.swapaxes(gate_slot, 0, 1).reshape(local_count, rows, 1)
    pre_act = jnp.einsum("lrd,dlf->lrf", slot_x, w_in, preferred_element_type=WIDE)
    upstream = jnp.einsum("lrd,fld->lrf", slot_g, w_out, preferred_element_type=WIDE)
    squash = jax.nn.sigmoid(pre_act)
    active = pre_act * squash
    gate_part = jnp.sum(active * upstream, axis=-1)
    act_gated = (gate_slot * active).astype(NARROW)
    grad_pre = (gate_slot * squash * (1.0 + pre_act * (1.0 - squash)) * upstream).astype(NARROW)
    gate_part = jnp.swapaxes(gate_part.reshape(local_count, blocks, CAP), 0, 1)
    gate_tok = jnp.sum(jnp.where(choose, gate_part[..., None], 0.0), axis=2)
    gate_back = jnp.sum(jnp.where(named, gate_tok[..., None], 0.0), axis=1)
    part_x = jnp.einsum("lrf,dlf->lrd", grad_pre, w_in, preferred_element_type=WIDE)
    part_x = part_x.astype(NARROW).reshape(local_count, blocks, CAP, model_width)
    token_part = jnp.einsum("blst,lbsd->btd", pick, part_x, preferred_element_type=WIDE)
    scatter = functools.partial(lax.psum_scatter, axis_name="expert", scatter_dimension=0)
    grad_tokens = lax.psum(scatter(token_part), "fsdp").astype(NARROW)
    grad_gates = lax.psum(scatter(gate_back), "fsdp").astype(NARROW)
    grad_in = jnp.einsum("lrd,lrf->dlf", slot_x, grad_pre, preferred_element_type=WIDE).astype(NARROW)
    grad_out = jnp.einsum("lrf,lrd->fld", act_gated, slot_g, preferred_element_type=WIDE).astype(NARROW)
    return (grad_tokens, grad_gates, grad_in, grad_out)


def solution(mesh):
    return jax.shard_map(
        local,
        mesh=mesh,
        in_specs=(
            P("expert", None),
            P("expert", None),
            P("expert", None),
            P("expert", None),
            P(None, "expert", "fsdp"),
            P("fsdp", "expert", None),
        ),
        out_specs=(
            P("expert", None),
            P("expert", None),
            P(None, "expert", "fsdp"),
            P("fsdp", "expert", None),
        ),
        check_vma=False,
    )
```

```python
import functools
import jax
import jax.numpy as jnp
import numpy as np
from jax import lax
from jax.experimental import pallas as pl
from jax.experimental.pallas import tpu as pltpu
from jax.sharding import PartitionSpec as P

EXPERTS = 16
CAP = 40
AXES = ("fsdp", "expert")
CORE, Y, X, Z = 1, 2, 4, 8
LANES = 128
NARROW, WIDE = jnp.bfloat16, jnp.float32
MIB = 1 << 20
TN = (((0,), (0,)), ((), ()))
NT = (((1,), (1,)), ((), ()))
NN = (((1,), (0,)), ((), ()))


def mm(a, b, dims):
    return lax.dot_general(a, b, dims, preferred_element_type=WIDE)


def swap(value, mask):
    size = lax.axis_size("fsdp") * lax.axis_size("expert")
    return lax.ppermute(value, AXES, [(i, i ^ mask) for i in range(size)])


def is_small():
    return lax.axis_size("fsdp") == 8 and lax.axis_size("expert") == 4


def own_order(rows):
    x_index = lax.axis_index("fsdp") % 2
    half = rows.shape[-1] // 2
    return jnp.where(
        x_index == 0, rows, jnp.concatenate([rows[..., half:], rows[..., :half]], axis=-1)
    )


ANY = pl.BlockSpec(memory_space=pl.ANY)
FLAG = jax.ShapeDtypeStruct((8, LANES), WIDE)


def small_call(body, place, inputs, after, outs, name, grant=12, steps=1):
    given = len(inputs)

    def run(place_ref, *refs):
        body(place_ref, refs[:given], refs[given + len(after) :])

    def whole(array):
        rows, columns = array.shape
        return pl.BlockSpec((rows, columns // steps), lambda i: (0, i))

    return pl.pallas_call(
        run,
        out_shape=outs,
        grid=(steps,),
        in_specs=[pl.BlockSpec(memory_space=pltpu.SMEM)]
        + [whole(array) for array in inputs]
        + [ANY] * len(after),
        out_specs=[whole(out) for out in outs],
        compiler_params=pltpu.CompilerParams(vmem_limit_bytes=grant * MIB),
        cost_estimate=pl.CostEstimate(flops=0, bytes_accessed=1 << 20, transcendentals=0),
        name=name,
    )(place, *inputs, *after)


def hold(arrays, after):
    count = len(arrays)
    return pl.pallas_call(
        lambda *refs: None,
        out_shape=[jax.ShapeDtypeStruct(array.shape, array.dtype) for array in arrays],
        in_specs=[ANY] * (count + len(after)),
        out_specs=[ANY] * count,
        input_output_aliases={number: number for number in range(count)},
        cost_estimate=pl.CostEstimate(flops=0, bytes_accessed=1 << 18, transcendentals=0),
        name="hold",
    )(*arrays, *after)


def at(index, size):
    return pl.ds(pl.multiple_of(index * size, size), size)


def first_sum(place_ref, ins, outs):
    keep_ref, got_ref = ins
    mine_ref, x_ref, y_ref, xy_ref = outs
    half = mine_ref.shape[0]
    x_index = place_ref[0]

    def total(rows):
        return keep_ref[rows, :] + got_ref[rows, :].astype(WIDE)

    mine_ref[...] = total(at(x_index, half))
    x_ref[...] = total(at(1 - x_index, half)).astype(NARROW)
    y_ref[...] = total(slice(2 * half, 3 * half)).astype(NARROW)
    xy_ref[...] = total(slice(3 * half, 4 * half)).astype(NARROW)


def second_sum(place_ref, ins, outs):
    mine_ref, x_ref, y_ref, xy_ref = ins
    quarter = outs[0].shape[0]
    z_index = place_ref[1]
    for step in range(4):
        rows = at(z_index ^ step, quarter)
        total = mine_ref[rows, :] + x_ref[rows, :].astype(WIDE)
        total = total + (y_ref[rows, :].astype(WIDE) + xy_ref[rows, :].astype(WIDE))
        outs[step][...] = total.astype(outs[step].dtype)


def third_sum(place_ref, ins, outs):
    total = ins[0][...]
    for got in ins[1:]:
        total = total + got[...].astype(WIDE)
    outs[0][...] = total.astype(NARROW)


def join_z(place_ref, ins, outs):
    quarter = ins[0].shape[0]
    for step in range(4):
        outs[0][at(place_ref[1] ^ step, quarter), :] = ins[step][...]


def join_x(place_ref, ins, outs):
    half = ins[0].shape[0]
    model_width = outs[0].shape[1]
    for step in range(2):
        rows = at(place_ref[0] ^ step, half)
        outs[0][rows, :] = ins[step][:, :model_width]
        outs[1][rows, :] = ins[step][:, model_width:]


def sorter(rows, tiles, experts):
    size = rows * tiles * experts
    order = np.arange(size).reshape(rows, tiles, experts).transpose(2, 1, 0).reshape(-1)
    return jnp.asarray(np.eye(size, dtype=np.float32)[order], NARROW)


def tiled_view(weight):
    rows, experts, columns = weight.shape
    return weight.reshape(rows, experts, columns // LANES, LANES).transpose(0, 2, 1, 3)


def odd_tiles(rows):
    tiles = -(-rows // 8)
    return 8 * (tiles + 1 - tiles % 2)


def split_body(group, some, sort_ref, w_ref, *refs):
    out_ref, flag_ref, wide_ref = refs[-3:]
    flag_ref[...] = jnp.zeros_like(flag_ref)
    rows, tiles, experts, _ = w_ref.shape
    held = group * experts
    flat = w_ref.reshape(rows, tiles * experts, LANES)
    stride = wide_ref.shape[1]
    wide = wide_ref.reshape(wide_ref.shape[0] * stride, LANES)

    def matmul(pair):
        blocks = [
            flat[row : row + some, tile * experts : tile * experts + held, :].reshape(
                some * held, LANES
            )
            for row, tile in pair
        ]
        result = mm(sort_ref[...], jnp.concatenate(blocks, axis=1), NN)
        for expert in range(experts):
            for tile in range(group):
                begin = (expert * group + tile) * some
                parts = [
                    result[begin : begin + some, side * LANES : (side + 1) * LANES]
                    for side in range(2)
                ]
                if some == 8:
                    row, first = pair[0][0], pair[0][1] + tile
                    out_ref[expert, row : row + 16, first * LANES : (first + 1) * LANES] = (
                        jnp.concatenate(parts, axis=0).astype(NARROW)
                    )
                else:
                    for (row, first), part in zip(pair, parts):
                        column = (first + tile) * LANES
                        out_ref[expert, row : row + some, column : column + LANES] = part.astype(
                            NARROW
                        )

    for row in range(0, rows, 32):
        other, base = row + 16, row // 2
        wide_ref[base : base + 16, : tiles * experts, :] = flat[other : other + 16].astype(WIDE)
        places = [
            (first, tile) for first in range(row, other, some) for tile in range(0, tiles, group)
        ]
        pairs = list(zip(places[::2], places[1::2]))
        combos = [(expert, tile) for expert in range(experts) for tile in range(tiles)]
        share = len(combos) // len(pairs)
        for number, pair in enumerate(pairs):
            matmul(pair)
            for expert, tile in combos[number * share : (number + 1) * share]:
                part = wide[pl.ds(base * stride + tile * experts + expert, 16, stride), :]
                out_ref[expert, other : other + 16, tile * LANES : (tile + 1) * LANES] = (
                    part.astype(NARROW)
                )


def split_experts(view, sort, start, rows, block, group, some, after, grant=56):
    _, tiles, experts, _ = view.shape
    columns = tiles * LANES
    first = start // block
    return pl.pallas_call(
        functools.partial(split_body, group, some),
        out_shape=[jax.ShapeDtypeStruct((experts, rows, columns), NARROW), FLAG],
        grid=(rows // block,),
        in_specs=[
            pl.BlockSpec(sort.shape, lambda i: (0, 0)),
            pl.BlockSpec((block, tiles, experts, LANES), lambda i: (first + i, 0, 0, 0)),
            *[ANY] * len(after),
        ],
        out_specs=[
            pl.BlockSpec((experts, block, columns), lambda i: (0, i, 0)),
            pl.BlockSpec(FLAG.shape, lambda i: (0, 0)),
        ],
        scratch_shapes=[pltpu.VMEM((block // 2, odd_tiles(tiles * experts), LANES), WIDE)],
        compiler_params=pltpu.CompilerParams(vmem_limit_bytes=grant * MIB),
        cost_estimate=pl.CostEstimate(
            flops=0, bytes_accessed=4 * experts * rows * columns, transcendentals=0
        ),
        name="split_experts",
    )(sort, view, *after)


def route_body(first_ref, *refs):
    metas, (code_ref, gate_ref) = refs[:-2], refs[-2:]
    experts = code_ref.shape[0]
    top_count = metas[0].shape[0] // 2
    row = lax.broadcasted_iota(jnp.int32, (LANES, LANES), 0)
    column = lax.broadcasted_iota(jnp.int32, (LANES, LANES), 1)
    earlier = (row < column).astype(WIDE).astype(NARROW)
    choice = lax.broadcasted_iota(jnp.int32, (top_count, LANES), 0)
    for block, meta_ref in enumerate(metas):
        lanes = slice(block * LANES, (block + 1) * LANES)
        ids = meta_ref[:top_count, :].astype(jnp.int32)
        gates = meta_ref[top_count:, :]
        named = [ids == first_ref[0] + expert for expert in range(experts)]
        hits = [jnp.sum(name.astype(WIDE), axis=0, keepdims=True) for name in named]
        before = mm(jnp.concatenate(hits, axis=0).astype(NARROW), earlier, NN).astype(jnp.int32)
        for expert in range(experts):
            which = jnp.sum(jnp.where(named[expert], choice, 0), axis=0, keepdims=True)
            slot = before[expert : expert + 1] + block * CAP
            code_ref[expert, :, lanes] = jnp.where(hits[expert] > 0.5, slot, 1023) + 1024 * which
            gate_ref[expert, :, lanes] = jnp.sum(
                jnp.where(named[expert], gates, 0.0), axis=0, keepdims=True
            )


def route(first, metas, experts):
    shape = (experts, 1, len(metas) * LANES)
    return pl.pallas_call(
        route_body,
        out_shape=[jax.ShapeDtypeStruct(shape, jnp.int32), jax.ShapeDtypeStruct(shape, WIDE)],
        in_specs=[pl.BlockSpec(memory_space=pltpu.SMEM)]
        + [pl.BlockSpec(memory_space=pltpu.VMEM)] * len(metas),
        out_specs=[pl.BlockSpec(memory_space=pltpu.VMEM)] * 2,
        cost_estimate=pl.CostEstimate(flops=0, bytes_accessed=1 << 18, transcendentals=0),
        name="route",
    )(first, *metas)


def fetch(pieces, whole, sem):
    copies, begin = [], 0
    for number, piece in enumerate(pieces):
        count = piece.shape[0]
        if begin == whole.shape[0]:
            break
        copies.append(
            pltpu.make_async_copy(piece, whole.at[begin : begin + count], sem.at[number])
        )
        begin += count
    for copy in copies:
        copy.start()
    for copy in copies:
        copy.wait()


def chosen(code, slots):
    tokens = code.shape[1]
    return lax.broadcasted_iota(jnp.int32, (slots, tokens), 0) == jnp.bitwise_and(code, 1023)


def weight_parts(weights, streams):
    specs, operands = [], []
    for array in weights:
        _, rows, columns = array.shape
        for number in range(streams):
            specs.append(
                pl.BlockSpec((1, rows // streams, columns), lambda i, number=number: (i, number, 0))
            )
            operands.append(array)
    return specs, operands


def block_picks(code_ref):
    experts, _, tokens = code_ref.shape
    slot = lax.broadcasted_iota(jnp.int32, (CAP, LANES), 0)
    picks = []
    for block in range(tokens // LANES):
        lanes = slice(block * LANES, (block + 1) * LANES)
        codes = [jnp.bitwise_and(code_ref[expert, :, lanes], 1023) for expert in range(experts)]
        found = [(slot + block * CAP == code).astype(WIDE) for code in codes]
        picks.append(jnp.concatenate(found, axis=0).astype(NARROW))
    return picks


def gather_slots(code_ref, whole_ref, wide_ref, slot_ref):
    experts = code_ref.shape[0]
    slots = slot_ref.shape[0] // experts
    columns = wide_ref.shape[1]
    picks = block_picks(code_ref)
    for begin in range(0, whole_ref.shape[1], columns):
        part = slice(begin, begin + columns)
        for block, pick in enumerate(picks):
            found = mm(pick, whole_ref[block * LANES : (block + 1) * LANES, part], NN)
            for expert in range(experts):
                row = expert * slots + block * CAP
                wide_ref[row : row + CAP, :] = found[expert * CAP : (expert + 1) * CAP]
        slot_ref[:, part] = wide_ref[...].astype(NARROW)


def forward_tokens_body(code_ref, gate_ref, *refs):
    w_refs, refs = refs[:2], refs[2:]
    pieces, refs = refs[:-8], refs[-8:]
    xs_ref, ag_ref, active_ref, slope_ref, x_ref, slot_ref, wide_ref, sem = refs
    step = pl.program_id(0)
    slots = ag_ref.shape[1]

    @pl.when(step == 0)
    def _():
        fetch(pieces, x_ref, sem)
        gather_slots(code_ref, x_ref, wide_ref, slot_ref)

    choose = chosen(code_ref[step], slots)
    gate = jnp.sum(jnp.where(choose, gate_ref[step], 0.0), axis=1, keepdims=True)
    rows = pl.ds(pl.multiple_of(step * slots, slots), slots)
    xs_ref[0] = slot_ref[rows, :]
    pre_act, begin = 0.0, 0
    for w_ref in w_refs:
        end = begin + w_ref.shape[1]
        pre_act = pre_act + mm(slot_ref[rows, begin:end], w_ref[0], NN)
        begin = end
    squash = jax.nn.sigmoid(pre_act)
    active = pre_act * squash
    active_ref[0] = active
    ag_ref[0] = (gate * active).astype(NARROW)
    slope_ref[0] = gate * squash * (1.0 + pre_act * (1.0 - squash))


def forward_tokens(code, gate_tok, x_pieces, w_split):
    experts, model_width, hidden = w_split.shape
    tokens = code.shape[2]
    slots = tokens // 128 * CAP
    expert = lambda i: (i, 0, 0)
    all_experts = pl.BlockSpec((experts, 1, tokens), lambda i: (0, 0, 0))
    w_specs, w_operands = weight_parts([w_split], 2)
    shapes = [(model_width, NARROW), (hidden, NARROW), (hidden, WIDE), (hidden, WIDE)]
    return pl.pallas_call(
        forward_tokens_body,
        out_shape=[jax.ShapeDtypeStruct((experts, slots, width), dtype) for width, dtype in shapes],
        grid=(experts,),
        in_specs=[all_experts, all_experts, *w_specs, *[ANY] * len(x_pieces)],
        out_specs=[pl.BlockSpec((1, slots, width), expert) for width, _ in shapes],
        scratch_shapes=[
            pltpu.VMEM((tokens, model_width), NARROW),
            pltpu.VMEM((experts * slots, model_width), NARROW),
            pltpu.VMEM((experts * slots, 512), WIDE),
            pltpu.SemaphoreType.DMA((len(x_pieces),)),
        ],
        compiler_params=pltpu.CompilerParams(vmem_limit_bytes=42 * MIB),
        cost_estimate=pl.CostEstimate(
            flops=2 * slots * experts * model_width * (hidden + tokens),
            bytes_accessed=2 * experts * model_width * hidden,
            transcendentals=0,
        ),
        name="forward_tokens",
    )(code, gate_tok, *w_operands, *x_pieces)


def forward_cotangents_body(code_ref, active_ref, slope_ref, *refs):
    w_refs, v_refs, refs = refs[:2], refs[2:4], refs[4:]
    pieces, refs = refs[:-9], refs[-9:]
    gs_ref, gp_ref, keep_ref, send_ref, g_ref, slot_ref, wide_ref, back_ref, sem = refs
    step = pl.program_id(0)
    slots = gp_ref.shape[1]
    model_width = g_ref.shape[1]
    columns = 512

    @pl.when(step == 0)
    def _():
        fetch(pieces, g_ref, sem)
        gather_slots(code_ref, g_ref, wide_ref, slot_ref)

    code = code_ref[step]
    rows = pl.ds(pl.multiple_of(step * slots, slots), slots)
    gs_ref[0] = slot_ref[rows, :]
    gate_part, begin = 0.0, 0
    for v_ref in v_refs:
        part = slice(begin, begin + v_ref.shape[1])
        upstream = mm(slot_ref[rows, :], v_ref[0], NT)
        gate_part = gate_part + jnp.sum(active_ref[0, :, part] * upstream, axis=1, keepdims=True)
        gp_ref[0, :, part] = (slope_ref[0, :, part] * upstream).astype(NARROW)
        begin = part.stop
    for begin in range(0, model_width, columns):
        held = w_refs[0].shape[1]
        w_ref, inner = w_refs[begin // held], begin % held
        back = mm(gp_ref[0], w_ref[0, inner : inner + columns, :], NT)
        back_ref[rows, begin : begin + columns] = back
    which = jnp.sum(
        jnp.where(chosen(code, slots), jnp.right_shift(code, 10), 0), axis=1, keepdims=True
    )
    lane = lax.broadcasted_iota(jnp.int32, (slots, LANES), 1)
    high = gate_part.astype(NARROW).astype(WIDE)
    gates = jnp.where(lane == which, high, 0.0)
    gates = jnp.where(lane == which + LANES // 2, gate_part - high, gates)
    back_ref[rows, model_width:] = gates

    @pl.when(step == pl.num_programs(0) - 1)
    def _():
        experts = code_ref.shape[0]
        picks = block_picks(code_ref)
        for begin in range(0, model_width + LANES, columns):
            part = slice(begin, min(begin + columns, model_width + LANES))
            for block, pick in enumerate(picks):
                starts = [expert * slots + block * CAP for expert in range(experts)]
                held = [back_ref[start : start + CAP, part] for start in starts]
                summed = mm(pick, jnp.concatenate(held, axis=0).astype(NARROW), TN)
                if begin == model_width:
                    summed = summed + pltpu.roll(summed, LANES // 2, 1)
                into = slice(block // 2 * LANES, (block // 2 + 1) * LANES)
                if block % 2 == 0:
                    keep_ref[into, part] = summed
                else:
                    send_ref[into, part] = summed.astype(NARROW)


def forward_cotangents(code, active, slope, g_pieces, w_split, v_split):
    experts, model_width, hidden = w_split.shape
    tokens = code.shape[2]
    slots = tokens // 128 * CAP
    width = model_width + LANES
    expert = lambda i: (i, 0, 0)
    whole = lambda i: (0, 0)
    one = pl.Buffered(1)
    w_specs, w_operands = weight_parts([w_split], 2)
    v_specs, v_operands = weight_parts(v_split, 1)
    return pl.pallas_call(
        forward_cotangents_body,
        out_shape=[
            jax.ShapeDtypeStruct((experts, slots, model_width), NARROW),
            jax.ShapeDtypeStruct((experts, slots, hidden), NARROW),
            jax.ShapeDtypeStruct((tokens // 2, width), WIDE),
            jax.ShapeDtypeStruct((tokens // 2, width), NARROW),
        ],
        grid=(experts,),
        in_specs=[
            pl.BlockSpec((experts, 1, tokens), lambda i: (0, 0, 0)),
            pl.BlockSpec((1, slots, hidden), expert),
            pl.BlockSpec((1, slots, hidden), expert),
            *w_specs,
            *v_specs,
            *[ANY] * len(g_pieces),
        ],
        out_specs=[
            pl.BlockSpec((1, slots, model_width), expert),
            pl.BlockSpec((1, slots, hidden), expert),
            pl.BlockSpec((tokens // 2, width), whole, pipeline_mode=one),
            pl.BlockSpec((tokens // 2, width), whole, pipeline_mode=one),
        ],
        scratch_shapes=[
            pltpu.VMEM((tokens, model_width), NARROW),
            pltpu.VMEM((experts * slots, model_width), NARROW),
            pltpu.VMEM((experts * slots, 512), WIDE),
            pltpu.VMEM((experts * slots, width), WIDE),
            pltpu.SemaphoreType.DMA((len(g_pieces),)),
        ],
        compiler_params=pltpu.CompilerParams(vmem_limit_bytes=46 * MIB),
        cost_estimate=pl.CostEstimate(
            flops=2 * slots * experts * model_width * (2 * hidden + 2 * tokens),
            bytes_accessed=4 * experts * model_width * hidden,
            transcendentals=0,
        ),
        name="forward_cotangents",
    )(code, active, slope, *w_operands, *v_operands, *g_pieces)


def outer_body(group, a_ref, b_ref, *refs):
    out_ref, flag_ref, wide_ref = refs[-3:]
    flag_ref[...] = jnp.zeros_like(flag_ref)
    rows, tiles, experts, _ = out_ref.shape
    stride = wide_ref.shape[1]
    held = group * experts
    out = out_ref.reshape(rows, tiles * experts, LANES)
    flat = wide_ref.reshape(rows * stride, LANES)
    for begin in range(0, tiles, group):
        for expert in range(experts):
            part = mm(a_ref[expert], b_ref[expert, :, begin * LANES : (begin + group) * LANES], TN)
            for tile in range(group):
                flat[pl.ds(tile * experts + expert, rows, stride), :] = part[
                    :, tile * LANES : (tile + 1) * LANES
                ]
        out[:, begin * experts : begin * experts + held, :] = wide_ref[:, :held, :].astype(NARROW)


def outer(a, b, holder, start, count, block, group, after):
    experts, slots, total = a.shape
    columns = b.shape[2]
    tiles = columns // LANES
    first = start // block
    extra = list(after) if holder is None else [holder, *after]
    return pl.pallas_call(
        functools.partial(outer_body, group),
        out_shape=[jax.ShapeDtypeStruct((total, tiles, experts, LANES), NARROW), FLAG],
        grid=(count // block,),
        in_specs=[
            pl.BlockSpec((experts, slots, block), lambda i: (0, 0, first + i)),
            pl.BlockSpec(
                (experts, slots, columns), lambda i: (0, 0, 0), pipeline_mode=pl.Buffered(1)
            ),
            *[ANY] * len(extra),
        ],
        out_specs=[
            pl.BlockSpec((block, tiles, experts, LANES), lambda i: (first + i, 0, 0, 0)),
            pl.BlockSpec(FLAG.shape, lambda i: (0, 0)),
        ],
        scratch_shapes=[pltpu.VMEM((block, odd_tiles(group * experts), LANES), WIDE)],
        input_output_aliases={} if holder is None else {2: 0},
        compiler_params=pltpu.CompilerParams(vmem_limit_bytes=40 * MIB),
        cost_estimate=pl.CostEstimate(
            flops=2 * experts * slots * count * columns,
            bytes_accessed=4 * experts * count * columns,
            transcendentals=0,
        ),
        name="weight_gradient",
    )(a, b, *extra)


def stored_view(tiled):
    rows, tiles, experts, _ = tiled.shape
    return tiled.transpose(0, 2, 1, 3).reshape(rows, experts, tiles * LANES)


def local(tokens, cotangent, expert_ids, gate_values, w_in, w_out):
    if not is_small():
        return local_general(tokens, cotangent, expert_ids, gate_values, w_in, w_out)
    tok_rows, model_width = tokens.shape
    top_count = expert_ids.shape[1]
    local_count = w_in.shape[1]
    hidden = w_in.shape[2]
    half = tok_rows // 2
    first = lax.axis_index("expert") * local_count
    fsdp = lax.axis_index("fsdp")
    x_index = fsdp % 2
    place = jnp.stack([x_index, fsdp // 2]).astype(jnp.int32)

    meta = jnp.concatenate([expert_ids.astype(WIDE), gate_values.astype(WIDE)], axis=1).T
    turned = own_order(meta)
    metas = [meta, swap(meta, CORE), swap(turned, Y), swap(turned, CORE | Y)]
    w_view, v_view = tiled_view(w_in), tiled_view(w_out)
    x_near = swap(lax.dynamic_slice_in_dim(tokens, x_index * half, half, axis=0), Y)
    g_near = swap(lax.dynamic_slice_in_dim(cotangent, x_index * half, half, axis=0), Y)
    x_core, g_core = swap(tokens, CORE), swap(cotangent, CORE)
    w_sort, v_sort = sorter(8, 6, local_count), sorter(16, 4, local_count)
    w_split, flag = split_experts(w_view, w_sort, 0, model_width, 256, 6, 8, [])
    x_near, *others = hold([x_near, *metas[1:]], [flag])
    code, gate_tok = route(first.astype(jnp.int32).reshape(1), [metas[0], *others], local_count)
    x_far = swap(x_near, X)
    x_near_core = swap(x_near, CORE)
    v_low, flag = split_experts(v_view, v_sort, 0, hidden // 2, 64, 4, 16, [x_near, code])
    x_far, g_near = hold([x_far, g_near], [flag])
    g_far = swap(g_near, X)
    g_near_core = swap(g_near, CORE)
    x_far_core = swap(x_far, CORE)
    v_high, flag = split_experts(v_view, v_sort, hidden // 2, hidden // 2, 64, 4, 16, [x_far], 46)
    x_pieces = [tokens, x_core, x_near, x_far, x_near_core, x_far_core]
    (g_far,) = hold([g_far], [flag])
    g_far_core = swap(g_far, CORE)
    xs, ag, active, slope = forward_tokens(code, gate_tok, [*x_pieces, g_far], w_split)
    g_pieces = [cotangent, g_core, g_near, g_far, g_near_core, g_far_core]
    gs, gp, keep, send = forward_cotangents(
        code, active, slope, g_pieces, w_split, [v_low, v_high]
    )
    width = keep.shape[1]

    def shape(rows, dtype, columns=width):
        return jax.ShapeDtypeStruct((rows, columns), dtype)

    def in_part(holder, number, after):
        rows = model_width // 4
        return outer(xs, gp, holder, number * rows, rows, 256, 6, after)

    def out_part(holder, number, after):
        rows = hidden // 3
        return outer(ag, gs, holder, number * rows, rows, 128, 8, after)

    got = swap(send, CORE)
    mine, *sends = small_call(
        first_sum, place, [keep, got], [],
        [shape(half, WIDE)] + [shape(half, NARROW)] * 3, "first_sum", 32,
    )
    got = [swap(part, mask) for part, mask in zip(sends, (X, Y, X | Y))]
    grad_in, flag = in_part(None, 0, [mine])
    grad_in, flag = in_part(grad_in, 1, [flag])
    grad_in, flag = in_part(grad_in, 2, [flag])
    grad_in, flag = in_part(grad_in, 3, [flag])
    mine, *sends = small_call(
        second_sum, place, [mine, *got], [flag],
        [shape(half // 4, WIDE)] + [shape(half // 4, NARROW)] * 3, "second_sum",
    )
    got = [swap(part, mask * Z) for part, mask in zip(sends, (1, 2, 3))]
    grad_out, flag = out_part(None, 0, [mine])
    (final,) = small_call(
        third_sum, place, [mine, *got], [flag], [shape(half // 4, NARROW)], "third_sum"
    )
    got = [swap(final, mask * Z) for mask in (1, 2, 3)]
    grad_out, flag = out_part(grad_out, 1, [final])
    (near,) = small_call(join_z, place, [final, *got], [flag], [shape(half, NARROW)], "join_z")
    far = swap(near, X)
    grad_out, flag = out_part(grad_out, 2, [near])
    grad_tokens, grad_gates = small_call(
        join_x, place, [near, far], [flag],
        [shape(tok_rows, NARROW, model_width), shape(tok_rows, NARROW, LANES)], "join_x",
    )
    grad_gates = grad_gates[:, :top_count]
    return (grad_tokens, grad_gates, stored_view(grad_in), stored_view(grad_out))


def local_general(tokens, cotangent, expert_ids, gate_values, w_in, w_out):
    tok_rows, model_width = tokens.shape
    local_count = w_in.shape[1]
    first = lax.axis_index("expert") * local_count
    gather = functools.partial(lax.all_gather, axis_name="expert", axis=0)
    ids, gates = gather(expert_ids), gather(gate_values).astype(WIDE)
    x_blocks, g_blocks = gather(tokens), gather(cotangent)
    blocks = ids.shape[0]
    names = first + jnp.arange(local_count, dtype=jnp.int32)
    named = ids[:, None] == names[None, :, None, None]
    hit = jnp.any(named, axis=3)
    gate_tok = jnp.sum(jnp.where(named, gates[:, None], 0.0), axis=3)
    earlier = jnp.tril(jnp.ones((tok_rows, tok_rows), WIDE), -1)
    position = jnp.einsum("tu,blu->blt", earlier, hit.astype(WIDE)).astype(jnp.int32)
    slots = jnp.arange(CAP, dtype=jnp.int32)
    choose = hit[:, :, None] & (position[:, :, None] == slots[None, None, :, None])
    pick = choose.astype(NARROW)
    slot_x = jnp.einsum("blst,btd->lbsd", pick, x_blocks, preferred_element_type=WIDE).astype(NARROW)
    slot_g = jnp.einsum("blst,btd->lbsd", pick, g_blocks, preferred_element_type=WIDE).astype(NARROW)
    gate_slot = jnp.sum(jnp.where(choose, gate_tok[:, :, None], 0.0), axis=3)
    rows = blocks * CAP
    slot_x = slot_x.reshape(local_count, rows, model_width)
    slot_g = slot_g.reshape(local_count, rows, model_width)
    gate_slot = jnp.swapaxes(gate_slot, 0, 1).reshape(local_count, rows, 1)
    pre_act = jnp.einsum("lrd,dlf->lrf", slot_x, w_in, preferred_element_type=WIDE)
    upstream = jnp.einsum("lrd,fld->lrf", slot_g, w_out, preferred_element_type=WIDE)
    squash = jax.nn.sigmoid(pre_act)
    active = pre_act * squash
    gate_part = jnp.sum(active * upstream, axis=-1)
    act_gated = (gate_slot * active).astype(NARROW)
    grad_pre = (gate_slot * squash * (1.0 + pre_act * (1.0 - squash)) * upstream).astype(NARROW)
    gate_part = jnp.swapaxes(gate_part.reshape(local_count, blocks, CAP), 0, 1)
    gate_tok = jnp.sum(jnp.where(choose, gate_part[..., None], 0.0), axis=2)
    gate_back = jnp.sum(jnp.where(named, gate_tok[..., None], 0.0), axis=1)
    part_x = jnp.einsum("lrf,dlf->lrd", grad_pre, w_in, preferred_element_type=WIDE)
    part_x = part_x.astype(NARROW).reshape(local_count, blocks, CAP, model_width)
    token_part = jnp.einsum("blst,lbsd->btd", pick, part_x, preferred_element_type=WIDE)
    scatter = functools.partial(lax.psum_scatter, axis_name="expert", scatter_dimension=0)
    grad_tokens = lax.psum(scatter(token_part), "fsdp").astype(NARROW)
    grad_gates = lax.psum(scatter(gate_back), "fsdp").astype(NARROW)
    grad_in = jnp.einsum("lrd,lrf->dlf", slot_x, grad_pre, preferred_element_type=WIDE).astype(NARROW)
    grad_out = jnp.einsum("lrf,lrd->fld", act_gated, slot_g, preferred_element_type=WIDE).astype(NARROW)
    return (grad_tokens, grad_gates, grad_in, grad_out)


def solution(mesh):
    return jax.shard_map(
        local,
        mesh=mesh,
        in_specs=(
            P("expert", None),
            P("expert", None),
            P("expert", None),
            P("expert", None),
            P(None, "expert", "fsdp"),
            P("fsdp", "expert", None),
        ),
        out_specs=(
            P("expert", None),
            P("expert", None),
            P(None, "expert", "fsdp"),
            P("fsdp", "expert", None),
        ),
        check_vma=False,
    )
```
